32 devices in a mesh: row: 8 (over y, x, core), col: 4 (over z).
Axes of the slice: x: 2, y: 2, z: 4, core: 2. Of those that a mesh axis runs over, the one named last changes fastest.
Arguments:
- green: bfloat16 [16384, 8192], P('row', 'col'), may hold values from -0.09375 to 0.09375
- mask: int32 [64, 32], P('row', 'col'), may hold values from 0 to 1, as said below
- probes: bfloat16 [8192, 256], P('col', 'row'), may hold values from -6 to 6
Outputs:
- sketch: float32 [16384, 256], P('row', 'col')
- adjoint: float32 [8192, 256], P('col', 'row')
The draws below stay inside these ranges and needn't reach their ends.
Inputs may be any that keep to these rules, and one draw needn't show every extreme that they name: `mask`: block row i belongs to gauge i % 6 and time block i // 6; block column j to window j // 8. A block is 1 when its time block is no earlier than the window's onset plus a travel delay of its gauge and subfault block.
All inputs are finite; a program needn't handle non-finite values.
Results may differ from the reference program's by a relative error of at most 0.0022.
Values may be sent and summed in bfloat16 or wider, within the bound.
No kernel may reach another device: no remote copies, remote signals or barrier semaphores. Data moves between devices by JAX's collectives and lax.ppermute only.
A program may use at most 128 MiB of HBM per device.

```python
import jax
import jax.numpy as jnp
from jax import lax

K = 256
SUBFAULTS = 2048
GAUGES = 6
BLK = 256
ROWS = 16384
WINDOWS = 4
COLS = 8192
RBLOCKS = 64
CBLOCKS = 32
TBLOCKS = 10


def draw_mask(key, part):
    per_window = SUBFAULTS // BLK
    travel = jax.random.randint(key, (GAUGES, per_window), 0, max(2, TBLOCKS // 4 + 1))
    travel = travel.at[0, 0].set(1)
    rows_idx = jnp.arange(RBLOCKS)
    gauge = rows_idx % GAUGES
    tblock = rows_idx // GAUGES
    cols_idx = jnp.arange(CBLOCKS)
    window = cols_idx // per_window
    subblock = cols_idx % per_window
    onset = window * TBLOCKS // (2 * WINDOWS)
    delay = travel[gauge][:, subblock]
    return (tblock[:, None] >= onset[None, :] + delay).astype(jnp.int32)


def shard_levels(own_key, shape, shards, least, top_value):
    factor_of, own = 1.0, jax.random.fold_in(own_key, 6)
    for position, blocks in shards:
        draws = jnp.exp(jax.random.uniform(jax.random.fold_in(own, position), (blocks,), jnp.float32, least / len(shards), top_value / len(shards)))
        factor_of = factor_of * jnp.repeat(draws, shape[position] // blocks).reshape([-1 if axis == position else 1 for axis in range(len(shape))])
    return factor_of


def normal_values(own_key, extent, width, most, pieces=(), kind=jnp.bfloat16):
    loudness = shard_levels(own_key, extent, pieces, -0.22, 0.18) if pieces else 1.0
    result = jax.random.normal(own_key, extent, jnp.float32) * width * loudness
    return jnp.minimum(jnp.maximum(result, -most), most).astype(kind)


def setup_inputs(seed: int = 0) -> dict:
    keys = jax.random.split(jax.random.key(seed), 4)
    return {
        "green": normal_values(keys[0], (ROWS, COLS), (COLS // 2) ** -0.5, 0.09375, ((0, 8), (1, 4))),
        "mask": draw_mask(jax.random.fold_in(keys[3], 71), 0),
        "probes": normal_values(keys[2], (COLS, K), 1.0, 6.0, ((0, 4), (1, 8))),
    }


def reference(green, mask, probes):
    shaped = green.reshape(RBLOCKS, BLK, CBLOCKS, BLK)
    tiles = (shaped * mask.astype(jnp.bfloat16)[:, None, :, None]).reshape(ROWS, COLS)
    sketch = jnp.dot(tiles, probes, preferred_element_type=jnp.float32)
    lowered = sketch.astype(jnp.bfloat16)
    adjoint = lax.dot_general(tiles, lowered, (((0,), (0,)), ((), ())), preferred_element_type=jnp.float32)
    return sketch, adjoint
```

```python
import functools

import jax
import jax.numpy as jnp
from jax import lax
from jax.experimental import pallas as pl
from jax.experimental.pallas import tpu as pltpu
from jax.sharding import PartitionSpec as P

F32, BF16 = jnp.float32, jnp.bfloat16
CHUNKS = 1


def exchange(value, axis, offset):
    size = lax.axis_size(axis)
    return lax.ppermute(value, axis, [(i, i ^ offset) for i in range(size)])


def level(mask_ref, i, j, block):
    return jnp.full((block, block), mask_ref[i, j].astype(F32)).astype(BF16)


def sketch_kernel(where, mask_ref, green_ref, *refs, offsets_row, offsets_col, base, block):
    blocks, outs = refs[: len(offsets_row)], refs[len(offsets_row) : -2]
    probes, total = refs[-2:]
    width = blocks[0].shape[0]
    share = outs[0].shape[0]

    @pl.when(pl.program_id(0) == 0)
    def _():
        for offset, ref in zip(offsets_row, blocks):
            start = pl.multiple_of((where[0] ^ offset) * width, width)
            probes[pl.ds(start, width), :] = ref[...]

    i = pl.program_id(0) + base
    tiles = jnp.concatenate(
        [
            green_ref[:, j * block : (j + 1) * block] * level(mask_ref, i, j, block)
            for j in range(green_ref.shape[1] // block)
        ],
        axis=1,
    )
    total[...] = lax.dot_general(probes[...], tiles, (((1,), (1,)), ((), ())), preferred_element_type=F32)
    for offset, out in zip(offsets_col, outs):
        start = pl.multiple_of((where[1] ^ offset) * share, share)
        out[...] = total[pl.ds(start, share), :].astype(out.dtype)


def partial_sketch(where, mask, green, blocks, offsets_row, offsets_col, chunk, chunks, width):
    rows, cols = green.shape
    block = rows // mask.shape[0]
    steps = rows // block // chunks
    share = width // len(offsets_col)
    base = chunk * steps
    kernel = functools.partial(
        sketch_kernel, offsets_row=offsets_row, offsets_col=offsets_col, base=base, block=block
    )
    smem = pl.BlockSpec(memory_space=pltpu.SMEM)
    return pl.pallas_call(
        kernel,
        grid=(steps,),
        in_specs=[smem, smem, pl.BlockSpec((block, cols), lambda i: (i + base, 0))]
        + [pl.BlockSpec(b.shape, lambda i: (0, 0)) for b in blocks],
        out_specs=[pl.BlockSpec((share, block), lambda i: (0, i))] * len(offsets_col),
        out_shape=[
            jax.ShapeDtypeStruct((share, rows // chunks), F32 if offset == 0 else BF16) for offset in offsets_col
        ],
        scratch_shapes=[pltpu.VMEM((width, cols), BF16), pltpu.VMEM((width, block), F32)],
        compiler_params=pltpu.CompilerParams(vmem_limit_bytes=32 * 2**20),
        cost_estimate=pl.CostEstimate(
            flops=2 * width * cols * rows // chunks, bytes_accessed=2 * rows * cols // chunks, transcendentals=0
        ),
        name="partial_sketch",
    )(where, mask, green, *blocks)


def adjoint_kernel(where, mask_ref, green_ref, *refs, offsets_col, offsets_core, chunks, block):
    count = len(offsets_col) * chunks
    shares, outs = refs[:count], refs[count:-2]
    lowered, total = refs[-2:]
    share, length = shares[0].shape
    width = outs[0].shape[0]

    @pl.when(pl.program_id(0) == 0)
    def _():
        for k, ref in enumerate(shares):
            start = pl.multiple_of((where[1] ^ offsets_col[k // chunks]) * share, share)
            at = (k % chunks) * length
            lowered[pl.ds(start, share), at : at + length] = ref[...]

    j = pl.program_id(0)
    tiles = jnp.concatenate(
        [
            green_ref[i * block : (i + 1) * block, :] * level(mask_ref, i, j, block)
            for i in range(green_ref.shape[0] // block)
        ],
        axis=0,
    )
    total[...] = jnp.dot(lowered[...], tiles, preferred_element_type=F32)
    sibling = outs[-1]
    for k, offset in enumerate(offsets_core):
        start = pl.multiple_of((where[0] ^ offset) * width, width)
        outs[k][...] = total[pl.ds(start, width), :]
        start = pl.multiple_of((where[0] ^ 1 ^ offset) * width, width)
        sibling[k * width : (k + 1) * width, :] = total[pl.ds(start, width), :].astype(sibling.dtype)


def partial_adjoint(where, mask, green, shares, offsets_col, offsets_core, chunks, width):
    rows, cols = green.shape
    block = cols // mask.shape[1]
    own = width // (2 * len(offsets_core))
    kernel = functools.partial(
        adjoint_kernel, offsets_col=offsets_col, offsets_core=offsets_core, chunks=chunks, block=block
    )
    smem = pl.BlockSpec(memory_space=pltpu.SMEM)
    heights = [own] * len(offsets_core) + [own * len(offsets_core)]
    return pl.pallas_call(
        kernel,
        grid=(cols // block,),
        in_specs=[smem, smem, pl.BlockSpec((rows, block), lambda j: (0, j))]
        + [pl.BlockSpec(s.shape, lambda j: (0, 0)) for s in shares],
        out_specs=[pl.BlockSpec((h, block), lambda j: (0, j)) for h in heights],
        out_shape=[jax.ShapeDtypeStruct((h, cols), F32) for h in heights],
        scratch_shapes=[pltpu.VMEM((width, rows), BF16), pltpu.VMEM((width, block), F32)],
        compiler_params=pltpu.CompilerParams(vmem_limit_bytes=32 * 2**20),
        cost_estimate=pl.CostEstimate(
            flops=2 * width * cols * rows, bytes_accessed=2 * rows * cols, transcendentals=0
        ),
        name="partial_adjoint",
    )(where, mask, green, *shares)


def local(green, mask, probes):
    n_row, n_col = lax.axis_size("row"), lax.axis_size("col")
    where = jnp.stack([lax.axis_index("row"), lax.axis_index("col")]).astype(jnp.int32)
    width = probes.shape[1] * n_row
    offsets_col = list(range(n_col))
    offsets_core = list(range(0, n_row, 2))

    own = probes.T
    held = [own] + [exchange(own, "row", offset) for offset in offsets_core[1:]]
    twins = [exchange(block, "row", 1) for block in held]
    blocks = held + twins
    offsets_row = offsets_core + [offset ^ 1 for offset in offsets_core]

    sums, shares = [], [[] for _ in offsets_col]
    for chunk in range(CHUNKS):
        parts = partial_sketch(where, mask, green, blocks, offsets_row, offsets_col, chunk, CHUNKS, width)
        total = parts[0]
        for offset in offsets_col[1:]:
            total = total + exchange(parts[offset], "col", offset).astype(F32)
        sums.append(total)
        lowered = total.astype(BF16)
        for offset in offsets_col:
            shares[offset].append(lowered if offset == 0 else exchange(lowered, "col", offset))
    sketch = jnp.concatenate(sums, axis=1) if CHUNKS > 1 else sums[0]

    flat = [share for per_offset in shares for share in per_offset]
    *mine, others = partial_adjoint(where, mask, green, flat, offsets_col, offsets_core, CHUNKS, width)
    others = exchange(others, "row", 1)
    own_width = mine[0].shape[0]
    pairs = [m + others[k * own_width : (k + 1) * own_width] for k, m in enumerate(mine)]
    adjoint = pairs[0]
    for offset, pair in zip(offsets_core[1:], pairs[1:]):
        adjoint = adjoint + exchange(pair.astype(BF16), "row", offset).astype(F32)
    return sketch.T, adjoint.T


def solution(mesh):
    in_specs = (P("row", "col"), P("row", "col"), P("col", "row"))
    out_specs = (P("row", "col"), P("col", "row"))
    return jax.shard_map(local, mesh=mesh, in_specs=in_specs, out_specs=out_specs, check_vma=False)
```

```python
import functools

import jax
import jax.numpy as jnp
from jax import lax
from jax.experimental import pallas as pl
from jax.experimental.pallas import tpu as pltpu
from jax.sharding import PartitionSpec as P

F32, BF16 = jnp.float32, jnp.bfloat16
VMEM_LIMIT = 28 * 2**20
STEP = 512


def exchange(value, axis, offset):
    size = lax.axis_size(axis)
    return lax.ppermute(value, axis, [(i, i ^ offset) for i in range(size)])


def relay(value, axis, hop):
    size = lax.axis_size(axis)
    return lax.ppermute(value, axis, [(i, i + hop) for i in range(size) if 0 <= i + hop < size])


def mask_kernel(mask_ref, green_ref, tiles, sems, *, block):
    rows, cols = tiles.shape
    copies = []
    for step in range(rows // STEP):
        at = pl.ds(step * STEP, STEP)
        copies.append(pltpu.make_async_copy(green_ref.at[at], tiles.at[at], sems.at[step]))
        copies[-1].start()
    for step, copy in enumerate(copies):
        copy.wait()
        for i in range(step * STEP // block, (step + 1) * STEP // block):
            for j in range(cols // block):

                @pl.when(mask_ref[i, j] == 0)
                def _():
                    tiles[i * block : (i + 1) * block, j * block : (j + 1) * block] = jnp.zeros((block, block), BF16)


def masked(green, mask):
    rows, cols = green.shape
    return pl.pallas_call(
        functools.partial(mask_kernel, block=rows // mask.shape[0]),
        in_specs=[pl.BlockSpec(memory_space=pltpu.SMEM), pl.BlockSpec(memory_space=pltpu.HBM)],
        out_specs=pl.BlockSpec(memory_space=pltpu.VMEM),
        out_shape=pltpu.VMEM((rows, cols), BF16),
        scratch_shapes=[pltpu.SemaphoreType.DMA((rows // STEP,))],
        compiler_params=pltpu.CompilerParams(vmem_limit_bytes=VMEM_LIMIT),
        cost_estimate=pl.CostEstimate(flops=0, bytes_accessed=2 * rows * cols, transcendentals=0),
        name="masked_tiles",
    )(mask, pltpu.with_memory_space_constraint(green, pltpu.HBM))


def sketch_kernel(where, tiles, *refs, offsets_row, offsets_col):
    blocks, outs = refs[: len(offsets_row)], refs[len(offsets_row) : -2]
    probes, total = refs[-2:]
    width = blocks[0].shape[0]
    share = outs[0].shape[0]
    for offset, ref in zip(offsets_row, blocks):
        start = pl.multiple_of((where[0] ^ offset) * width, width)
        probes[pl.ds(start, width), :] = ref[...]
    for step in range(tiles.shape[0] // STEP):
        at = slice(step * STEP, (step + 1) * STEP)
        total[:, at] = lax.dot_general(
            probes[...], tiles[at, :], (((1,), (1,)), ((), ())), preferred_element_type=F32
        )
    for offset, out in zip(offsets_col, outs):
        start = pl.multiple_of((where[1] ^ offset) * share, share)
        out[...] = total[pl.ds(start, share), :].astype(out.dtype)


def partial_sketch(where, tiles, blocks, offsets_row, offsets_col):
    rows, cols = tiles.shape
    width = blocks[0].shape[0] * len(blocks)
    share = width // len(offsets_col)
    vmem = pl.BlockSpec(memory_space=pltpu.VMEM)
    return pl.pallas_call(
        functools.partial(sketch_kernel, offsets_row=offsets_row, offsets_col=offsets_col),
        in_specs=[pl.BlockSpec(memory_space=pltpu.SMEM)] + [vmem] * (1 + len(blocks)),
        out_specs=[vmem] * len(offsets_col),
        out_shape=[jax.ShapeDtypeStruct((share, rows), F32 if offset == 0 else BF16) for offset in offsets_col],
        scratch_shapes=[pltpu.VMEM((width, cols), BF16), pltpu.VMEM((width, rows), F32)],
        compiler_params=pltpu.CompilerParams(vmem_limit_bytes=VMEM_LIMIT),
        cost_estimate=pl.CostEstimate(
            flops=2 * width * cols * rows, bytes_accessed=2 * rows * cols, transcendentals=0
        ),
        name="partial_sketch",
    )(where, tiles, *blocks)


def adjoint_kernel(where, tiles, *refs, hops, offsets_core):
    shares, outs = refs[: len(hops)], refs[len(hops) : -2]
    lowered, total = refs[-2:]
    share = shares[0].shape[0]
    width = outs[0].shape[0]
    for hop, ref in zip(hops, shares):
        origin = where[1] + hop

        @pl.when((origin >= 0) & (origin < lowered.shape[0] // share))
        def _():
            lowered[pl.ds(pl.multiple_of(origin * share, share), share), :] = ref[...]

    for step in range(tiles.shape[1] // STEP):
        at = slice(step * STEP, (step + 1) * STEP)
        total[:, at] = jnp.dot(lowered[...], tiles[:, at], preferred_element_type=F32)
    sibling = outs[-1]
    for k, offset in enumerate(offsets_core):
        start = pl.multiple_of((where[0] ^ offset) * width, width)
        outs[k][...] = total[pl.ds(start, width), :]
        start = pl.multiple_of((where[0] ^ 1 ^ offset) * width, width)
        sibling[k * width : (k + 1) * width, :] = total[pl.ds(start, width), :].astype(sibling.dtype)


def partial_adjoint(where, tiles, shares, hops, offsets_core, width):
    rows, cols = tiles.shape
    own = width // (2 * len(offsets_core))
    heights = [own] * len(offsets_core) + [own * len(offsets_core)]
    vmem = pl.BlockSpec(memory_space=pltpu.VMEM)
    return pl.pallas_call(
        functools.partial(adjoint_kernel, hops=hops, offsets_core=offsets_core),
        in_specs=[pl.BlockSpec(memory_space=pltpu.SMEM)] + [vmem] * (1 + len(shares)),
        out_specs=[vmem] * len(heights),
        out_shape=[jax.ShapeDtypeStruct((h, cols), F32) for h in heights],
        scratch_shapes=[pltpu.VMEM((width, rows), BF16), pltpu.VMEM((width, cols), F32)],
        compiler_params=pltpu.CompilerParams(vmem_limit_bytes=VMEM_LIMIT),
        cost_estimate=pl.CostEstimate(
            flops=2 * width * cols * rows, bytes_accessed=2 * rows * cols, transcendentals=0
        ),
        name="partial_adjoint",
    )(where, tiles, *shares)


def join(parts, group):
    length = parts[0].shape[1]
    return jnp.concatenate([p.reshape(-1, group, length) for p in parts], axis=1).reshape(-1, length)


def local(green, mask, probes):
    n_row, n_col = lax.axis_size("row"), lax.axis_size("col")
    where = jnp.stack([lax.axis_index("row"), lax.axis_index("col")]).astype(jnp.int32)
    own_width = probes.shape[1]
    chunks = 2 if own_width % 32 == 0 and n_row % n_col == 0 else 1
    piece = own_width // chunks
    width = piece * n_row
    offsets_col = list(range(n_col))
    offsets_core = list(range(0, n_row, 2))
    offsets_row = offsets_core + [offset ^ 1 for offset in offsets_core]

    tiles = masked(green, mask)

    blocks = []
    for chunk in range(chunks):
        own = probes.T[chunk * piece : (chunk + 1) * piece]
        held = [own] + [exchange(own, "row", offset) for offset in offsets_core[1:]]
        blocks.append(held + [exchange(block, "row", 1) for block in held])

    sketches, adjoints = [], []
    for chunk in range(chunks):
        parts = partial_sketch(where, tiles, blocks[chunk], offsets_row, offsets_col)
        total = parts[0]
        for offset in offsets_col[1:]:
            total = total + exchange(parts[offset], "col", offset).astype(F32)
        sketches.append(total)

        shares, hops = [total.astype(BF16)], [0]
        up = down = shares[0]
        for hop in range(1, n_col):
            up, down = relay(up, "col", 1), relay(down, "col", -1)
            shares += [up, down]
            hops += [-hop, hop]

        *mine, others = partial_adjoint(where, tiles, shares, hops, offsets_core, width)
        others = exchange(others, "row", 1)
        pairs = [m + others[k * piece : (k + 1) * piece] for k, m in enumerate(mine)]
        adjoint = pairs[0]
        for offset, pair in zip(offsets_core[1:], pairs[1:]):
            adjoint = adjoint + exchange(pair.astype(BF16), "row", offset).astype(F32)
        adjoints.append(adjoint)
    return join(sketches, piece).T, join(adjoints, piece).T


def solution(mesh):
    in_specs = (P("row", "col"), P("row", "col"), P("col", "row"))
    out_specs = (P("row", "col"), P("col", "row"))
    return jax.shard_map(local, mesh=mesh, in_specs=in_specs, out_specs=out_specs, check_vma=False)
```

```python
import functools

import jax
import jax.numpy as jnp
from jax import lax
from jax.experimental import pallas as pl
from jax.experimental.pallas import tpu as pltpu
from jax.sharding import PartitionSpec as P

F32, BF16 = jnp.float32, jnp.bfloat16
VMEM_LIMIT = 28 * 2**20
STEP = 512


def spread(value, axis):
    copies = jnp.broadcast_to(value, (lax.axis_size(axis), *value.shape)).reshape(-1, value.shape[1])
    return lax.all_to_all(copies, axis, 0, 0, tiled=True)


def gathered_sum(own, parts, axis):
    size = lax.axis_size(axis)
    terms = lax.all_to_all(parts, axis, 0, 0, tiled=True).reshape(size, *own.shape)
    me = lax.axis_index(axis)
    total = own
    for k in range(size):
        total = total + jnp.where(me == k, 0.0, terms[k].astype(F32))
    return total


def mask_kernel(mask_ref, green_ref, tiles, sems, *, block):
    rows, cols = tiles.shape
    copies = []
    for step in range(rows // STEP):
        at = pl.ds(step * STEP, STEP)
        copies.append(pltpu.make_async_copy(green_ref.at[at], tiles.at[at], sems.at[step]))
        copies[-1].start()
    for step, copy in enumerate(copies):
        copy.wait()
        for i in range(step * STEP // block, (step + 1) * STEP // block):
            for j in range(cols // block):

                @pl.when(mask_ref[i, j] == 0)
                def _():
                    tiles[i * block : (i + 1) * block, j * block : (j + 1) * block] = jnp.zeros((block, block), BF16)


def masked(green, mask):
    rows, cols = green.shape
    return pl.pallas_call(
        functools.partial(mask_kernel, block=rows // mask.shape[0]),
        in_specs=[pl.BlockSpec(memory_space=pltpu.SMEM), pl.BlockSpec(memory_space=pltpu.HBM)],
        out_specs=pl.BlockSpec(memory_space=pltpu.VMEM),
        out_shape=pltpu.VMEM((rows, cols), BF16),
        scratch_shapes=[pltpu.SemaphoreType.DMA((rows // STEP,))],
        compiler_params=pltpu.CompilerParams(vmem_limit_bytes=VMEM_LIMIT),
        cost_estimate=pl.CostEstimate(flops=0, bytes_accessed=2 * rows * cols, transcendentals=0),
        name="masked_tiles",
    )(mask, pltpu.with_memory_space_constraint(green, pltpu.HBM))


def product_kernel(me, tiles, left, parts, own, total, *, transposed):
    for step in range(tiles.shape[0] // STEP):
        at = slice(step * STEP, (step + 1) * STEP)
        if transposed:
            term = lax.dot_general(left[...], tiles[at, :], (((1,), (1,)), ((), ())), preferred_element_type=F32)
        else:
            term = jnp.dot(left[...], tiles[:, at], preferred_element_type=F32)
        total[:, at] = term
        parts[:, at] = term.astype(BF16)
    share = own.shape[0]
    own[...] = total[pl.ds(pl.multiple_of(me[0] * share, share), share), :]


def product(tiles, left, axis, transposed):
    length = tiles.shape[0 if transposed else 1]
    width = left.shape[0]
    share = width // lax.axis_size(axis)
    me = lax.axis_index(axis).astype(jnp.int32).reshape(1)
    vmem = pl.BlockSpec(memory_space=pltpu.VMEM)
    return pl.pallas_call(
        functools.partial(product_kernel, transposed=transposed),
        in_specs=[pl.BlockSpec(memory_space=pltpu.SMEM), vmem, vmem],
        out_specs=[vmem, vmem],
        out_shape=[jax.ShapeDtypeStruct((width, length), BF16), jax.ShapeDtypeStruct((share, length), F32)],
        scratch_shapes=[pltpu.VMEM((width, length), F32)],
        compiler_params=pltpu.CompilerParams(vmem_limit_bytes=VMEM_LIMIT),
        cost_estimate=pl.CostEstimate(
            flops=2 * width * tiles.shape[0] * tiles.shape[1],
            bytes_accessed=2 * tiles.shape[0] * tiles.shape[1],
            transcendentals=0,
        ),
        name="partial_sketch" if transposed else "partial_adjoint",
    )(me, tiles, left)


def local(green, mask, probes):
    tiles = masked(green, mask)
    parts, own = product(tiles, spread(probes.T, "row"), "col", True)
    sketch = gathered_sum(own, parts, "col")
    parts, own = product(tiles, spread(sketch.astype(BF16), "col"), "row", False)
    return sketch.T, gathered_sum(own, parts, "row").T


def solution(mesh):
    in_specs = (P("row", "col"), P("row", "col"), P("col", "row"))
    out_specs = (P("row", "col"), P("col", "row"))
    return jax.shard_map(local, mesh=mesh, in_specs=in_specs, out_specs=out_specs, check_vma=False)
```

```python
import functools

import jax
import jax.numpy as jnp
from jax import lax
from jax.experimental import pallas as pl
from jax.experimental.pallas import tpu as pltpu
from jax.sharding import PartitionSpec as P

F32, BF16 = jnp.float32, jnp.bfloat16
VMEM_LIMIT = 28 * 2**20
STEP = 512
CHUNKS = 1


def exchange(value, axis, offset):
    size = lax.axis_size(axis)
    return lax.ppermute(value, axis, [(i, i ^ offset) for i in range(size)])


def mask_kernel(mask_ref, green_ref, tiles, sems, *, block):
    rows, cols = tiles.shape
    copies = []
    for step in range(rows // STEP):
        at = pl.ds(step * STEP, STEP)
        copies.append(pltpu.make_async_copy(green_ref.at[at], tiles.at[at], sems.at[step]))
        copies[-1].start()
    for step, copy in enumerate(copies):
        copy.wait()
        for i in range(step * STEP // block, (step + 1) * STEP // block):
            for j in range(cols // block):

                @pl.when(mask_ref[i, j] == 0)
                def _():
                    tiles[i * block : (i + 1) * block, j * block : (j + 1) * block] = jnp.zeros((block, block), BF16)


def masked(green, mask):
    rows, cols = green.shape
    return pl.pallas_call(
        functools.partial(mask_kernel, block=rows // mask.shape[0]),
        in_specs=[pl.BlockSpec(memory_space=pltpu.SMEM), pl.BlockSpec(memory_space=pltpu.HBM)],
        out_specs=pl.BlockSpec(memory_space=pltpu.VMEM),
        out_shape=pltpu.VMEM((rows, cols), BF16),
        scratch_shapes=[pltpu.SemaphoreType.DMA((rows // STEP,))],
        compiler_params=pltpu.CompilerParams(vmem_limit_bytes=VMEM_LIMIT),
        cost_estimate=pl.CostEstimate(flops=0, bytes_accessed=2 * rows * cols, transcendentals=0),
        name="masked_tiles",
    )(mask, pltpu.with_memory_space_constraint(green, pltpu.HBM))


def sketch_kernel(where, tiles, *refs, offsets_row, offsets_col):
    blocks, outs = refs[: len(offsets_row)], refs[len(offsets_row) : -2]
    probes, total = refs[-2:]
    width = blocks[0].shape[0]
    share = outs[0].shape[0]
    for offset, ref in zip(offsets_row, blocks):
        start = pl.multiple_of((where[0] ^ offset) * width, width)
        probes[pl.ds(start, width), :] = ref[...]
    for step in range(tiles.shape[0] // STEP):
        at = slice(step * STEP, (step + 1) * STEP)
        total[:, at] = lax.dot_general(
            probes[...], tiles[at, :], (((1,), (1,)), ((), ())), preferred_element_type=F32
        )
    for offset, out in zip(offsets_col, outs):
        start = pl.multiple_of((where[1] ^ offset) * share, share)
        out[...] = total[pl.ds(start, share), :].astype(out.dtype)


def partial_sketch(where, tiles, blocks, offsets_row, offsets_col):
    rows, cols = tiles.shape
    width = blocks[0].shape[0] * len(blocks)
    share = width // len(offsets_col)
    vmem = pl.BlockSpec(memory_space=pltpu.VMEM)
    return pl.pallas_call(
        functools.partial(sketch_kernel, offsets_row=offsets_row, offsets_col=offsets_col),
        in_specs=[pl.BlockSpec(memory_space=pltpu.SMEM)] + [vmem] * (1 + len(blocks)),
        out_specs=[vmem] * len(offsets_col),
        out_shape=[jax.ShapeDtypeStruct((share, rows), F32 if offset == 0 else BF16) for offset in offsets_col],
        scratch_shapes=[pltpu.VMEM((width, cols), BF16), pltpu.VMEM((width, rows), F32)],
        compiler_params=pltpu.CompilerParams(vmem_limit_bytes=VMEM_LIMIT),
        cost_estimate=pl.CostEstimate(
            flops=2 * width * cols * rows, bytes_accessed=2 * rows * cols, transcendentals=0
        ),
        name="partial_sketch",
    )(where, tiles, *blocks)


def adjoint_kernel(where, tiles, *refs, offsets_col, offsets_core):
    shares, outs = refs[: len(offsets_col)], refs[len(offsets_col) : -2]
    lowered, total = refs[-2:]
    share = shares[0].shape[0]
    width = outs[0].shape[0]
    for offset, ref in zip(offsets_col, shares):
        start = pl.multiple_of((where[1] ^ offset) * share, share)
        lowered[pl.ds(start, share), :] = ref[...]
    for step in range(tiles.shape[1] // STEP):
        at = slice(step * STEP, (step + 1) * STEP)
        total[:, at] = jnp.dot(lowered[...], tiles[:, at], preferred_element_type=F32)
    sibling = outs[-1]
    for k, offset in enumerate(offsets_core):
        start = pl.multiple_of((where[0] ^ offset) * width, width)
        outs[k][...] = total[pl.ds(start, width), :]
        start = pl.multiple_of((where[0] ^ 1 ^ offset) * width, width)
        sibling[k * width : (k + 1) * width, :] = total[pl.ds(start, width), :].astype(sibling.dtype)


def partial_adjoint(where, tiles, shares, offsets_col, offsets_core, width):
    rows, cols = tiles.shape
    own = width // (2 * len(offsets_core))
    heights = [own] * len(offsets_core) + [own * len(offsets_core)]
    vmem = pl.BlockSpec(memory_space=pltpu.VMEM)
    return pl.pallas_call(
        functools.partial(adjoint_kernel, offsets_col=offsets_col, offsets_core=offsets_core),
        in_specs=[pl.BlockSpec(memory_space=pltpu.SMEM)] + [vmem] * (1 + len(shares)),
        out_specs=[vmem] * len(heights),
        out_shape=[jax.ShapeDtypeStruct((h, cols), F32) for h in heights],
        scratch_shapes=[pltpu.VMEM((width, rows), BF16), pltpu.VMEM((width, cols), F32)],
        compiler_params=pltpu.CompilerParams(vmem_limit_bytes=VMEM_LIMIT),
        cost_estimate=pl.CostEstimate(
            flops=2 * width * cols * rows, bytes_accessed=2 * rows * cols, transcendentals=0
        ),
        name="partial_adjoint",
    )(where, tiles, *shares)


def join(parts, group):
    length = parts[0].shape[1]
    return jnp.concatenate([p.reshape(-1, group, length) for p in parts], axis=1).reshape(-1, length)


def local(green, mask, probes):
    n_row, n_col = lax.axis_size("row"), lax.axis_size("col")
    where = jnp.stack([lax.axis_index("row"), lax.axis_index("col")]).astype(jnp.int32)
    own_width = probes.shape[1]
    chunks = CHUNKS if own_width % (16 * CHUNKS) == 0 and n_row % n_col == 0 else 1
    piece = own_width // chunks
    width = piece * n_row
    offsets_col = list(range(n_col))
    offsets_core = list(range(0, n_row, 2))
    gather_core = [0] + offsets_core[:0:-1]
    offsets_row = gather_core + [offset ^ 1 for offset in gather_core]
    far_first = [0] + offsets_col[:0:-1]

    tiles = masked(green, mask)

    blocks = []
    for chunk in range(chunks):
        own = probes.T[chunk * piece : (chunk + 1) * piece]
        held = [own] + [exchange(own, "row", offset) for offset in gather_core[1:]]
        blocks.append(held + [exchange(block, "row", 1) for block in held])

    sketches, adjoints = [], []
    for chunk in range(chunks):
        parts = partial_sketch(where, tiles, blocks[chunk], offsets_row, offsets_col)
        total = parts[0]
        for offset in offsets_col[1:]:
            total = total + exchange(parts[offset], "col", offset).astype(F32)
        sketches.append(total)

        lowered = total.astype(BF16)
        shares = [lowered] + [exchange(lowered, "col", offset) for offset in far_first[1:]]

        *mine, others = partial_adjoint(where, tiles, shares, far_first, offsets_core, width)
        others = exchange(others, "row", 1)
        pairs = [m + others[k * piece : (k + 1) * piece] for k, m in enumerate(mine)]
        adjoint = pairs[0]
        for offset, pair in zip(offsets_core[1:], pairs[1:]):
            adjoint = adjoint + exchange(pair.astype(BF16), "row", offset).astype(F32)
        adjoints.append(adjoint)
    return join(sketches, piece).T, join(adjoints, piece).T


def solution(mesh):
    in_specs = (P("row", "col"), P("row", "col"), P("col", "row"))
    out_specs = (P("row", "col"), P("col", "row"))
    return jax.shard_map(local, mesh=mesh, in_specs=in_specs, out_specs=out_specs, check_vma=False)
```

```python
import functools

import jax
import jax.numpy as jnp
from jax import lax
from jax.experimental import pallas as pl
from jax.experimental.pallas import tpu as pltpu
from jax.sharding import PartitionSpec as P

F32, BF16 = jnp.float32, jnp.bfloat16
VMEM_LIMIT = 28 * 2**20
STEP = 512
CHUNKS = 1


def exchange(value, axis, offset):
    size = lax.axis_size(axis)
    return lax.ppermute(value, axis, [(i, i ^ offset) for i in range(size)])


def after(value, *earlier):
    return lax.optimization_barrier((value, earlier))[0]


def mask_kernel(mask_ref, green_ref, tiles, sems, *, block):
    rows, cols = tiles.shape
    copies = []
    for step in range(rows // STEP):
        at = pl.ds(step * STEP, STEP)
        copies.append(pltpu.make_async_copy(green_ref.at[at], tiles.at[at], sems.at[step]))
        copies[-1].start()
    for step, copy in enumerate(copies):
        copy.wait()
        for i in range(step * STEP // block, (step + 1) * STEP // block):
            for j in range(cols // block):

                @pl.when(mask_ref[i, j] == 0)
                def _():
                    tiles[i * block : (i + 1) * block, j * block : (j + 1) * block] = jnp.zeros((block, block), BF16)


def masked(green, mask):
    rows, cols = green.shape
    return pl.pallas_call(
        functools.partial(mask_kernel, block=rows // mask.shape[0]),
        in_specs=[pl.BlockSpec(memory_space=pltpu.SMEM), pl.BlockSpec(memory_space=pltpu.HBM)],
        out_specs=pl.BlockSpec(memory_space=pltpu.VMEM),
        out_shape=pltpu.VMEM((rows, cols), BF16),
        scratch_shapes=[pltpu.SemaphoreType.DMA((rows // STEP,))],
        compiler_params=pltpu.CompilerParams(vmem_limit_bytes=VMEM_LIMIT),
        cost_estimate=pl.CostEstimate(flops=0, bytes_accessed=2 * rows * cols, transcendentals=0),
        name="masked_tiles",
    )(mask, pltpu.with_memory_space_constraint(green, pltpu.HBM))


def sketch_kernel(where, tiles, *refs, offsets_row, offsets_col):
    blocks, outs = refs[: len(offsets_row)], refs[len(offsets_row) : -2]
    probes, total = refs[-2:]
    width = blocks[0].shape[0]
    share = outs[0].shape[0]
    for offset, ref in zip(offsets_row, blocks):
        start = pl.multiple_of((where[0] ^ offset) * width, width)
        probes[pl.ds(start, width), :] = ref[...]
    for step in range(tiles.shape[0] // STEP):
        at = slice(step * STEP, (step + 1) * STEP)
        total[:, at] = lax.dot_general(
            probes[...], tiles[at, :], (((1,), (1,)), ((), ())), preferred_element_type=F32
        )
    for offset, out in zip(offsets_col, outs):
        start = pl.multiple_of((where[1] ^ offset) * share, share)
        out[...] = total[pl.ds(start, share), :].astype(out.dtype)


def partial_sketch(where, tiles, blocks, offsets_row, offsets_col):
    rows, cols = tiles.shape
    width = blocks[0].shape[0] * len(blocks)
    share = width // len(offsets_col)
    vmem = pl.BlockSpec(memory_space=pltpu.VMEM)
    return pl.pallas_call(
        functools.partial(sketch_kernel, offsets_row=offsets_row, offsets_col=offsets_col),
        in_specs=[pl.BlockSpec(memory_space=pltpu.SMEM)] + [vmem] * (1 + len(blocks)),
        out_specs=[vmem] * len(offsets_col),
        out_shape=[jax.ShapeDtypeStruct((share, rows), F32 if offset == 0 else BF16) for offset in offsets_col],
        scratch_shapes=[pltpu.VMEM((width, cols), BF16), pltpu.VMEM((width, rows), F32)],
        compiler_params=pltpu.CompilerParams(vmem_limit_bytes=VMEM_LIMIT),
        cost_estimate=pl.CostEstimate(
            flops=2 * width * cols * rows, bytes_accessed=4 * width * (rows + cols), transcendentals=0
        ),
        name="partial_sketch",
    )(where, tiles, *blocks)


def adjoint_kernel(where, tiles, *refs, offsets_col, offsets_core):
    shares, outs = refs[: len(offsets_col)], refs[len(offsets_col) : -2]
    lowered, total = refs[-2:]
    share = shares[0].shape[0]
    width = outs[0].shape[0]
    for offset, ref in zip(offsets_col, shares):
        start = pl.multiple_of((where[1] ^ offset) * share, share)
        lowered[pl.ds(start, share), :] = ref[...]
    for step in range(tiles.shape[1] // STEP):
        at = slice(step * STEP, (step + 1) * STEP)
        total[:, at] = jnp.dot(lowered[...], tiles[:, at], preferred_element_type=F32)
    sibling = outs[-1]
    for k, offset in enumerate(offsets_core):
        start = pl.multiple_of((where[0] ^ offset) * width, width)
        outs[k][...] = total[pl.ds(start, width), :]
        start = pl.multiple_of((where[0] ^ 1 ^ offset) * width, width)
        sibling[k * width : (k + 1) * width, :] = total[pl.ds(start, width), :].astype(sibling.dtype)


def partial_adjoint(where, tiles, shares, offsets_col, offsets_core, width):
    rows, cols = tiles.shape
    own = width // (2 * len(offsets_core))
    heights = [own] * len(offsets_core) + [own * len(offsets_core)]
    vmem = pl.BlockSpec(memory_space=pltpu.VMEM)
    return pl.pallas_call(
        functools.partial(adjoint_kernel, offsets_col=offsets_col, offsets_core=offsets_core),
        in_specs=[pl.BlockSpec(memory_space=pltpu.SMEM)] + [vmem] * (1 + len(shares)),
        out_specs=[vmem] * len(heights),
        out_shape=[jax.ShapeDtypeStruct((h, cols), F32) for h in heights],
        scratch_shapes=[pltpu.VMEM((width, rows), BF16), pltpu.VMEM((width, cols), F32)],
        compiler_params=pltpu.CompilerParams(vmem_limit_bytes=VMEM_LIMIT),
        cost_estimate=pl.CostEstimate(
            flops=2 * width * cols * rows, bytes_accessed=4 * width * (rows + cols), transcendentals=0
        ),
        name="partial_adjoint",
    )(where, tiles, *shares)


def join(parts, group):
    length = parts[0].shape[1]
    return jnp.concatenate([p.reshape(-1, group, length) for p in parts], axis=1).reshape(-1, length)


def local(green, mask, probes):
    n_row, n_col = lax.axis_size("row"), lax.axis_size("col")
    where = jnp.stack([lax.axis_index("row"), lax.axis_index("col")]).astype(jnp.int32)
    own_width = probes.shape[1]
    chunks = CHUNKS if own_width % (16 * CHUNKS) == 0 and n_row % n_col == 0 else 1
    piece = own_width // chunks
    width = piece * n_row
    offsets_col = list(range(n_col))
    offsets_core = list(range(0, n_row, 2))
    gather_core = [0] + offsets_core[:0:-1]
    offsets_row = gather_core + [offset ^ 1 for offset in gather_core]
    far_first = [0] + offsets_col[:0:-1]

    tiles = masked(green, mask)

    blocks = []
    for chunk in range(chunks):
        own = probes.T[chunk * piece : (chunk + 1) * piece]
        held = [own] + [exchange(own, "row", offset) for offset in gather_core[1:]]
        held = after(held, tiles)
        blocks.append(held + [exchange(block, "row", 1) for block in held])

    sketches, adjoints = [], []
    for chunk in range(chunks):
        parts = partial_sketch(where, tiles, blocks[chunk], offsets_row, offsets_col)
        total = parts[0]
        for offset in offsets_col[1:]:
            total = total + exchange(parts[offset], "col", offset).astype(F32)
        sketches.append(total)

        lowered = total.astype(BF16)
        shares = [lowered] + [exchange(lowered, "col", offset) for offset in far_first[1:]]

        *mine, others = partial_adjoint(where, tiles, shares, far_first, offsets_core, width)
        others = exchange(others, "row", 1)
        pairs = [m + others[k * piece : (k + 1) * piece] for k, m in enumerate(mine)]
        adjoint = pairs[0]
        for offset, pair in zip(offsets_core[1:], pairs[1:]):
            adjoint = adjoint + exchange(pair.astype(BF16), "row", offset).astype(F32)
        adjoints.append(adjoint)
    return join(sketches, piece).T, join(adjoints, piece).T


def solution(mesh):
    in_specs = (P("row", "col"), P("row", "col"), P("col", "row"))
    out_specs = (P("row", "col"), P("col", "row"))
    return jax.shard_map(local, mesh=mesh, in_specs=in_specs, out_specs=out_specs, check_vma=False)
```

```python
import functools

import jax
import jax.numpy as jnp
from jax import lax
from jax.experimental import pallas as pl
from jax.experimental.pallas import tpu as pltpu
from jax.sharding import PartitionSpec as P

F32, BF16 = jnp.float32, jnp.bfloat16
VMEM_LIMIT = 28 * 2**20
STEP = 512
CHUNKS = 2


def exchange(value, axis, offset):
    size = lax.axis_size(axis)
    return lax.ppermute(value, axis, [(i, i ^ offset) for i in range(size)])


def mask_kernel(mask_ref, green_ref, tiles, token, sems, *, block):
    rows, cols = tiles.shape
    token[...] = jnp.zeros(token.shape, token.dtype)
    copies = []
    for step in range(rows // STEP):
        at = pl.ds(step * STEP, STEP)
        copies.append(pltpu.make_async_copy(green_ref.at[at], tiles.at[at], sems.at[step]))
        copies[-1].start()
    for step, copy in enumerate(copies):
        copy.wait()
        for i in range(step * STEP // block, (step + 1) * STEP // block):
            for j in range(cols // block):

                @pl.when(mask_ref[i, j] == 0)
                def _():
                    tiles[i * block : (i + 1) * block, j * block : (j + 1) * block] = jnp.zeros((block, block), BF16)


def masked(green, mask):
    rows, cols = green.shape
    return pl.pallas_call(
        functools.partial(mask_kernel, block=rows // mask.shape[0]),
        in_specs=[pl.BlockSpec(memory_space=pltpu.SMEM), pl.BlockSpec(memory_space=pltpu.HBM)],
        out_specs=[pl.BlockSpec(memory_space=pltpu.VMEM)] * 2,
        out_shape=[pltpu.VMEM((rows, cols), BF16), jax.ShapeDtypeStruct((8, 128), F32)],
        scratch_shapes=[pltpu.SemaphoreType.DMA((rows // STEP,))],
        compiler_params=pltpu.CompilerParams(vmem_limit_bytes=VMEM_LIMIT),
        cost_estimate=pl.CostEstimate(flops=0, bytes_accessed=2 * rows * cols, transcendentals=0),
        name="masked_tiles",
    )(mask, pltpu.with_memory_space_constraint(green, pltpu.HBM))


def sketch_kernel(where, tiles, token, *refs, offsets_row, offsets_col, piece):
    blocks, outs = refs[: len(offsets_row)], refs[len(offsets_row) : -2]
    probes, total = refs[-2:]
    width = blocks[0].shape[0]
    for offset, ref in zip(offsets_row, blocks):
        start = pl.multiple_of((where[0] ^ offset) * width, width)
        probes[pl.ds(start, width), :] = ref[...]
    for step in range(tiles.shape[0] // STEP):
        at = slice(step * STEP, (step + 1) * STEP)
        total[:, at] = lax.dot_general(
            probes[...], tiles[at, :], (((1,), (1,)), ((), ())), preferred_element_type=F32
        )
    share = total.shape[0] // len(offsets_col)
    for k, out in enumerate(outs):
        chunk, offset = k // len(offsets_col), offsets_col[k % len(offsets_col)]
        for n in range(out.shape[0] // piece):
            start = pl.multiple_of((where[1] ^ offset) * share + n * width + chunk * piece, piece)
            out[n * piece : (n + 1) * piece, :] = total[pl.ds(start, piece), :].astype(out.dtype)


def partial_sketch(where, tiles, blocks, token, offsets_row, offsets_col, chunks):
    rows, cols = tiles.shape
    width = blocks[0].shape[0] * len(blocks)
    share = width // len(offsets_col) // chunks
    vmem = pl.BlockSpec(memory_space=pltpu.VMEM)
    outs = [jax.ShapeDtypeStruct((share, rows), F32 if offset == 0 else BF16) for offset in offsets_col] * chunks
    return pl.pallas_call(
        functools.partial(
            sketch_kernel, offsets_row=offsets_row, offsets_col=offsets_col, piece=blocks[0].shape[0] // chunks
        ),
        in_specs=[pl.BlockSpec(memory_space=pltpu.SMEM)] + [vmem] * (2 + len(blocks)),
        out_specs=[vmem] * len(outs),
        out_shape=outs,
        scratch_shapes=[pltpu.VMEM((width, cols), BF16), pltpu.VMEM((width, rows), F32)],
        compiler_params=pltpu.CompilerParams(vmem_limit_bytes=VMEM_LIMIT),
        cost_estimate=pl.CostEstimate(
            flops=2 * width * cols * rows, bytes_accessed=4 * width * (rows + cols), transcendentals=0
        ),
        name="partial_sketch",
    )(where, tiles, token, *blocks)


def adjoint_kernel(where, tiles, *refs, offsets_col, offsets_core, chunks):
    count = len(offsets_col) * chunks
    shares, outs = refs[:count], refs[count:-2]
    lowered, total = refs[-2:]
    share = shares[0].shape[0] * chunks
    width = outs[0].shape[0]
    piece = width // chunks
    for k, ref in enumerate(shares):
        chunk, offset = k // len(offsets_col), offsets_col[k % len(offsets_col)]
        for n in range(ref.shape[0] // piece):
            start = pl.multiple_of((where[1] ^ offset) * share + n * width + chunk * piece, piece)
            lowered[pl.ds(start, piece), :] = ref[n * piece : (n + 1) * piece, :]
    for step in range(tiles.shape[1] // STEP):
        at = slice(step * STEP, (step + 1) * STEP)
        total[:, at] = jnp.dot(lowered[...], tiles[:, at], preferred_element_type=F32)
    sibling = outs[-1]
    for k, offset in enumerate(offsets_core):
        start = pl.multiple_of((where[0] ^ offset) * width, width)
        outs[k][...] = total[pl.ds(start, width), :]
        start = pl.multiple_of((where[0] ^ 1 ^ offset) * width, width)
        sibling[k * width : (k + 1) * width, :] = total[pl.ds(start, width), :].astype(sibling.dtype)


def partial_adjoint(where, tiles, shares, offsets_col, offsets_core, width, chunks):
    rows, cols = tiles.shape
    own = width // (2 * len(offsets_core))
    heights = [own] * len(offsets_core) + [own * len(offsets_core)]
    vmem = pl.BlockSpec(memory_space=pltpu.VMEM)
    return pl.pallas_call(
        functools.partial(adjoint_kernel, offsets_col=offsets_col, offsets_core=offsets_core, chunks=chunks),
        in_specs=[pl.BlockSpec(memory_space=pltpu.SMEM)] + [vmem] * (1 + len(shares)),
        out_specs=[vmem] * len(heights),
        out_shape=[jax.ShapeDtypeStruct((h, cols), F32) for h in heights],
        scratch_shapes=[pltpu.VMEM((width, rows), BF16), pltpu.VMEM((width, cols), F32)],
        compiler_params=pltpu.CompilerParams(vmem_limit_bytes=VMEM_LIMIT),
        cost_estimate=pl.CostEstimate(
            flops=2 * width * cols * rows, bytes_accessed=4 * width * (rows + cols), transcendentals=0
        ),
        name="partial_adjoint",
    )(where, tiles, *shares)


def join(parts, group):
    length = parts[0].shape[1]
    return jnp.concatenate([p.reshape(-1, group, length) for p in parts], axis=1).reshape(-1, length)


def local(green, mask, probes):
    n_row, n_col = lax.axis_size("row"), lax.axis_size("col")
    where = jnp.stack([lax.axis_index("row"), lax.axis_index("col")]).astype(jnp.int32)
    own_width = probes.shape[1]
    chunks = CHUNKS if own_width % (16 * CHUNKS) == 0 and n_row % n_col == 0 else 1
    piece = own_width // chunks
    width = own_width * n_row
    offsets_col = list(range(n_col))
    offsets_core = list(range(0, n_row, 2))
    gather_core = [0] + offsets_core[:0:-1]
    offsets_row = gather_core + [offset ^ 1 for offset in gather_core]
    far_first = [0] + offsets_col[:0:-1]

    tiles, token = masked(green, mask)

    own = probes.T
    held = [own] + [exchange(own, "row", offset) for offset in gather_core[1:]]
    held, token = lax.optimization_barrier((held, token))
    blocks = held + [exchange(block, "row", 1) for block in held]

    parts = partial_sketch(where, tiles, blocks, token, offsets_row, offsets_col, chunks)
    totals, shares = [], []
    for chunk in range(chunks):
        terms = parts[chunk * n_col : (chunk + 1) * n_col]
        total = terms[0]
        for offset in offsets_col[1:]:
            total = total + exchange(terms[offset], "col", offset).astype(F32)
        totals.append(total)
        lowered = total.astype(BF16)
        shares.append([lowered] + [exchange(lowered, "col", offset) for offset in far_first[1:]])

    flat = [share for per_chunk in shares for share in per_chunk]
    *mine, others = partial_adjoint(where, tiles, flat, far_first, offsets_core, width, chunks)
    others = exchange(others, "row", 1)
    pairs = [m + others[k * own_width : (k + 1) * own_width] for k, m in enumerate(mine)]
    adjoint = pairs[0]
    for offset, pair in zip(offsets_core[1:], pairs[1:]):
        adjoint = adjoint + exchange(pair.astype(BF16), "row", offset).astype(F32)
    return join(totals, piece).T, adjoint.T


def solution(mesh):
    in_specs = (P("row", "col"), P("row", "col"), P("col", "row"))
    out_specs = (P("row", "col"), P("col", "row"))
    return jax.shard_map(local, mesh=mesh, in_specs=in_specs, out_specs=out_specs, check_vma=False)
```

```python
import functools

import jax
import jax.numpy as jnp
from jax import lax
from jax.experimental import pallas as pl
from jax.experimental.pallas import tpu as pltpu
from jax.sharding import PartitionSpec as P

F32, BF16 = jnp.float32, jnp.bfloat16
VMEM_LIMIT = 28 * 2**20
STEP = 512
CHUNKS = 2


def exchange(value, axis, offset):
    size = lax.axis_size(axis)
    return lax.ppermute(value, axis, [(i, i ^ offset) for i in range(size)])


def mask_kernel(mask_ref, green_ref, tiles, token, sems, *, block):
    rows, cols = tiles.shape
    token[...] = jnp.zeros(token.shape, token.dtype)
    copies = []
    for step in range(rows // STEP):
        at = pl.ds(step * STEP, STEP)
        copies.append(pltpu.make_async_copy(green_ref.at[at], tiles.at[at], sems.at[step]))
        copies[-1].start()
    for step, copy in enumerate(copies):
        copy.wait()
        for i in range(step * STEP // block, (step + 1) * STEP // block):
            for j in range(cols // block):

                @pl.when(mask_ref[i, j] == 0)
                def _():
                    tiles[i * block : (i + 1) * block, j * block : (j + 1) * block] = jnp.zeros((block, block), BF16)


def masked(green, mask):
    rows, cols = green.shape
    return pl.pallas_call(
        functools.partial(mask_kernel, block=rows // mask.shape[0]),
        in_specs=[pl.BlockSpec(memory_space=pltpu.SMEM), pl.BlockSpec(memory_space=pltpu.HBM)],
        out_specs=[pl.BlockSpec(memory_space=pltpu.VMEM)] * 2,
        out_shape=[pltpu.VMEM((rows, cols), BF16), jax.ShapeDtypeStruct((8, 128), F32)],
        scratch_shapes=[pltpu.SemaphoreType.DMA((rows // STEP,))],
        compiler_params=pltpu.CompilerParams(vmem_limit_bytes=VMEM_LIMIT),
        cost_estimate=pl.CostEstimate(flops=0, bytes_accessed=2 * rows * cols, transcendentals=0),
        name="masked_tiles",
    )(mask, pltpu.with_memory_space_constraint(green, pltpu.HBM))


def sketch_kernel(where, tiles, token, *refs, offsets_row, offsets_col, piece):
    blocks, outs = refs[: len(offsets_row)], refs[len(offsets_row) : -2]
    probes, total = refs[-2:]
    width = blocks[0].shape[0]
    for offset, ref in zip(offsets_row, blocks):
        start = pl.multiple_of((where[0] ^ offset) * width, width)
        probes[pl.ds(start, width), :] = ref[...]
    for step in range(tiles.shape[0] // STEP):
        at = slice(step * STEP, (step + 1) * STEP)
        total[:, at] = lax.dot_general(
            probes[...], tiles[at, :], (((1,), (1,)), ((), ())), preferred_element_type=F32
        )
    share = total.shape[0] // len(offsets_col)
    for k, out in enumerate(outs):
        chunk, offset = k // len(offsets_col), offsets_col[k % len(offsets_col)]
        for n in range(out.shape[0] // piece):
            start = pl.multiple_of((where[1] ^ offset) * share + n * width + chunk * piece, piece)
            out[n * piece : (n + 1) * piece, :] = total[pl.ds(start, piece), :].astype(out.dtype)


def partial_sketch(where, tiles, blocks, token, offsets_row, offsets_col, chunks):
    rows, cols = tiles.shape
    width = blocks[0].shape[0] * len(blocks)
    share = width // len(offsets_col) // chunks
    vmem = pl.BlockSpec(memory_space=pltpu.VMEM)
    outs = [jax.ShapeDtypeStruct((share, rows), F32 if offset == 0 else BF16) for offset in offsets_col] * chunks
    return pl.pallas_call(
        functools.partial(
            sketch_kernel, offsets_row=offsets_row, offsets_col=offsets_col, piece=blocks[0].shape[0] // chunks
        ),
        in_specs=[pl.BlockSpec(memory_space=pltpu.SMEM)] + [vmem] * (2 + len(blocks)),
        out_specs=[vmem] * len(outs),
        out_shape=outs,
        scratch_shapes=[pltpu.VMEM((width, cols), BF16), pltpu.VMEM((width, rows), F32)],
        compiler_params=pltpu.CompilerParams(vmem_limit_bytes=VMEM_LIMIT),
        cost_estimate=pl.CostEstimate(
            flops=2 * width * cols * rows, bytes_accessed=2 * rows * cols, transcendentals=0
        ),
        name="partial_sketch",
    )(where, tiles, token, *blocks)


def adjoint_kernel(where, tiles, *refs, offsets_col, offsets_core, chunks):
    count = len(offsets_col) * chunks
    shares, outs = refs[:count], refs[count:-2]
    lowered, total = refs[-2:]
    share = shares[0].shape[0] * chunks
    width = outs[0].shape[0]
    piece = width // chunks
    for k, ref in enumerate(shares):
        chunk, offset = k // len(offsets_col), offsets_col[k % len(offsets_col)]
        for n in range(ref.shape[0] // piece):
            start = pl.multiple_of((where[1] ^ offset) * share + n * width + chunk * piece, piece)
            lowered[pl.ds(start, piece), :] = ref[n * piece : (n + 1) * piece, :]
    for step in range(tiles.shape[1] // STEP):
        at = slice(step * STEP, (step + 1) * STEP)
        total[:, at] = jnp.dot(lowered[...], tiles[:, at], preferred_element_type=F32)
    sibling = outs[-1]
    for k, offset in enumerate(offsets_core):
        start = pl.multiple_of((where[0] ^ offset) * width, width)
        outs[k][...] = total[pl.ds(start, width), :]
        start = pl.multiple_of((where[0] ^ 1 ^ offset) * width, width)
        sibling[k * width : (k + 1) * width, :] = total[pl.ds(start, width), :].astype(sibling.dtype)


def partial_adjoint(where, tiles, shares, offsets_col, offsets_core, width, chunks):
    rows, cols = tiles.shape
    own = width // (2 * len(offsets_core))
    heights = [own] * len(offsets_core) + [own * len(offsets_core)]
    vmem = pl.BlockSpec(memory_space=pltpu.VMEM)
    return pl.pallas_call(
        functools.partial(adjoint_kernel, offsets_col=offsets_col, offsets_core=offsets_core, chunks=chunks),
        in_specs=[pl.BlockSpec(memory_space=pltpu.SMEM)] + [vmem] * (1 + len(shares)),
        out_specs=[vmem] * len(heights),
        out_shape=[jax.ShapeDtypeStruct((h, cols), F32) for h in heights],
        scratch_shapes=[pltpu.VMEM((width, rows), BF16), pltpu.VMEM((width, cols), F32)],
        compiler_params=pltpu.CompilerParams(vmem_limit_bytes=VMEM_LIMIT),
        cost_estimate=pl.CostEstimate(
            flops=2 * width * cols * rows, bytes_accessed=2 * rows * cols, transcendentals=0
        ),
        name="partial_adjoint",
    )(where, tiles, *shares)


def join(parts, group):
    length = parts[0].shape[1]
    return jnp.concatenate([p.reshape(-1, group, length) for p in parts], axis=1).reshape(-1, length)


def local(green, mask, probes):
    n_row, n_col = lax.axis_size("row"), lax.axis_size("col")
    where = jnp.stack([lax.axis_index("row"), lax.axis_index("col")]).astype(jnp.int32)
    own_width = probes.shape[1]
    chunks = CHUNKS if own_width % (16 * CHUNKS) == 0 and n_row % n_col == 0 else 1
    piece = own_width // chunks
    width = own_width * n_row
    offsets_col = list(range(n_col))
    offsets_core = list(range(0, n_row, 2))
    gather_core = [0] + offsets_core[:0:-1]
    offsets_row = gather_core + [offset ^ 1 for offset in gather_core]
    far_first = [0] + offsets_col[:0:-1]

    tiles, token = masked(green, mask)

    own = probes.T
    held = [own] + [exchange(own, "row", offset) for offset in gather_core[1:]]
    held, token = lax.optimization_barrier((held, token))
    blocks = held + [exchange(block, "row", 1) for block in held]

    parts = partial_sketch(where, tiles, blocks, token, offsets_row, offsets_col, chunks)
    totals, shares = [], []
    for chunk in range(chunks):
        terms = parts[chunk * n_col : (chunk + 1) * n_col]
        total = terms[0]
        for offset in offsets_col[1:]:
            total = total + exchange(terms[offset], "col", offset).astype(F32)
        totals.append(total)
        lowered = total.astype(BF16)
        shares.append([lowered] + [exchange(lowered, "col", offset) for offset in far_first[1:]])

    flat = [share for per_chunk in shares for share in per_chunk]
    *mine, others = partial_adjoint(where, tiles, flat, far_first, offsets_core, width, chunks)
    others = exchange(others, "row", 1)
    pairs = [m + others[k * own_width : (k + 1) * own_width] for k, m in enumerate(mine)]
    adjoint = pairs[0]
    for offset, pair in zip(offsets_core[1:], pairs[1:]):
        adjoint = adjoint + exchange(pair.astype(BF16), "row", offset).astype(F32)
    return join(totals, piece).T, adjoint.T


def solution(mesh):
    in_specs = (P("row", "col"), P("row", "col"), P("col", "row"))
    out_specs = (P("row", "col"), P("col", "row"))
    return jax.shard_map(local, mesh=mesh, in_specs=in_specs, out_specs=out_specs, check_vma=False)
```

```python
import functools

import jax
import jax.numpy as jnp
from jax import lax
from jax.experimental import pallas as pl
from jax.experimental.pallas import tpu as pltpu
from jax.sharding import PartitionSpec as P

F32, BF16 = jnp.float32, jnp.bfloat16
VMEM_LIMIT = 28 * 2**20
STEP = 512
CHUNKS = 2


def exchange(value, axis, offset):
    size = lax.axis_size(axis)
    return lax.ppermute(value, axis, [(i, i ^ offset) for i in range(size)])


def mask_kernel(where, mask_ref, green_ref, tiles, token, sems, *, block):
    rows, cols = tiles.shape
    token[...] = jnp.zeros(token.shape, token.dtype)
    copies = []
    for step in range(rows // STEP):
        at = pl.ds(step * STEP, STEP)
        copies.append(pltpu.make_async_copy(green_ref.at[at], tiles.at[at], sems.at[step]))
        copies[-1].start()
    for step, copy in enumerate(copies):
        copy.wait()
        for i in range(step * STEP // block, (step + 1) * STEP // block):
            for j in range(cols // block):

                @pl.when(mask_ref[i, j] == 0)
                def _():
                    tiles[i * block : (i + 1) * block, j * block : (j + 1) * block] = jnp.zeros((block, block), BF16)


def masked(where, green, mask):
    rows, cols = green.shape
    return pl.pallas_call(
        functools.partial(mask_kernel, block=rows // mask.shape[0]),
        in_specs=[pl.BlockSpec(memory_space=pltpu.SMEM)] * 2 + [pl.BlockSpec(memory_space=pltpu.HBM)],
        out_specs=[pl.BlockSpec(memory_space=pltpu.VMEM)] * 2,
        out_shape=[pltpu.VMEM((rows, cols), BF16), jax.ShapeDtypeStruct((8, 128), F32)],
        scratch_shapes=[pltpu.SemaphoreType.DMA((rows // STEP,))],
        compiler_params=pltpu.CompilerParams(vmem_limit_bytes=VMEM_LIMIT),
        cost_estimate=pl.CostEstimate(flops=0, bytes_accessed=2 * rows * cols, transcendentals=0),
        name="masked_tiles",
    )(where, mask, pltpu.with_memory_space_constraint(green, pltpu.HBM))


def sketch_kernel(where, tiles, token, *refs, offsets_row, offsets_col, piece):
    blocks, outs = refs[: len(offsets_row)], refs[len(offsets_row) : -2]
    probes, total = refs[-2:]
    width = blocks[0].shape[0]
    for offset, ref in zip(offsets_row, blocks):
        start = pl.multiple_of((where[0] ^ offset) * width, width)
        probes[pl.ds(start, width), :] = ref[...]
    for step in range(tiles.shape[0] // STEP):
        at = slice(step * STEP, (step + 1) * STEP)
        total[:, at] = lax.dot_general(
            probes[...], tiles[at, :], (((1,), (1,)), ((), ())), preferred_element_type=F32
        )
    share = total.shape[0] // len(offsets_col)
    for k, out in enumerate(outs):
        chunk, offset = k // len(offsets_col), offsets_col[k % len(offsets_col)]
        for n in range(out.shape[0] // piece):
            start = pl.multiple_of((where[1] ^ offset) * share + n * width + chunk * piece, piece)
            out[n * piece : (n + 1) * piece, :] = total[pl.ds(start, piece), :].astype(out.dtype)


def partial_sketch(where, tiles, blocks, token, offsets_row, offsets_col, chunks):
    rows, cols = tiles.shape
    width = blocks[0].shape[0] * len(blocks)
    share = width // len(offsets_col) // chunks
    vmem = pl.BlockSpec(memory_space=pltpu.VMEM)
    outs = [jax.ShapeDtypeStruct((share, rows), F32 if offset == 0 else BF16) for offset in offsets_col] * chunks
    return pl.pallas_call(
        functools.partial(
            sketch_kernel, offsets_row=offsets_row, offsets_col=offsets_col, piece=blocks[0].shape[0] // chunks
        ),
        in_specs=[pl.BlockSpec(memory_space=pltpu.SMEM)] + [vmem] * (2 + len(blocks)),
        out_specs=[vmem] * len(outs),
        out_shape=outs,
        scratch_shapes=[pltpu.VMEM((width, cols), BF16), pltpu.VMEM((width, rows), F32)],
        compiler_params=pltpu.CompilerParams(vmem_limit_bytes=VMEM_LIMIT),
        cost_estimate=pl.CostEstimate(
            flops=2 * width * cols * rows, bytes_accessed=2 * rows * cols, transcendentals=0
        ),
        name="partial_sketch",
    )(where, tiles, token, *blocks)


def adjoint_kernel(where, tiles, *refs, offsets_col, offsets_core, chunks):
    count = len(offsets_col) * chunks
    shares, outs = refs[:count], refs[count:-2]
    lowered, total = refs[-2:]
    share = shares[0].shape[0] * chunks
    width = outs[0].shape[0]
    piece = width // chunks
    for k, ref in enumerate(shares):
        chunk, offset = k // len(offsets_col), offsets_col[k % len(offsets_col)]
        for n in range(ref.shape[0] // piece):
            start = pl.multiple_of((where[1] ^ offset) * share + n * width + chunk * piece, piece)
            lowered[pl.ds(start, piece), :] = ref[n * piece : (n + 1) * piece, :]
    for step in range(tiles.shape[1] // STEP):
        at = slice(step * STEP, (step + 1) * STEP)
        total[:, at] = jnp.dot(lowered[...], tiles[:, at], preferred_element_type=F32)
    sibling = outs[-1]
    for k, offset in enumerate(offsets_core):
        start = pl.multiple_of((where[0] ^ offset) * width, width)
        outs[k][...] = total[pl.ds(start, width), :]
        start = pl.multiple_of((where[0] ^ 1 ^ offset) * width, width)
        sibling[k * width : (k + 1) * width, :] = total[pl.ds(start, width), :].astype(sibling.dtype)


def partial_adjoint(where, tiles, shares, offsets_col, offsets_core, width, chunks):
    rows, cols = tiles.shape
    own = width // (2 * len(offsets_core))
    heights = [own] * len(offsets_core) + [own * len(offsets_core)]
    vmem = pl.BlockSpec(memory_space=pltpu.VMEM)
    return pl.pallas_call(
        functools.partial(adjoint_kernel, offsets_col=offsets_col, offsets_core=offsets_core, chunks=chunks),
        in_specs=[pl.BlockSpec(memory_space=pltpu.SMEM)] + [vmem] * (1 + len(shares)),
        out_specs=[vmem] * len(heights),
        out_shape=[jax.ShapeDtypeStruct((h, cols), F32) for h in heights],
        scratch_shapes=[pltpu.VMEM((width, rows), BF16), pltpu.VMEM((width, cols), F32)],
        compiler_params=pltpu.CompilerParams(vmem_limit_bytes=VMEM_LIMIT),
        cost_estimate=pl.CostEstimate(
            flops=2 * width * cols * rows, bytes_accessed=2 * rows * cols, transcendentals=0
        ),
        name="partial_adjoint",
    )(where, tiles, *shares)


def join(parts, group):
    length = parts[0].shape[1]
    return jnp.concatenate([p.reshape(-1, group, length) for p in parts], axis=1).reshape(-1, length)


def local(green, mask, probes):
    n_row, n_col = lax.axis_size("row"), lax.axis_size("col")
    where = jnp.stack([lax.axis_index("row"), lax.axis_index("col")]).astype(jnp.int32)
    own_width = probes.shape[1]
    chunks = CHUNKS if own_width % (16 * CHUNKS) == 0 and n_row % n_col == 0 else 1
    piece = own_width // chunks
    width = own_width * n_row
    offsets_col = list(range(n_col))
    offsets_core = list(range(0, n_row, 2))
    gather_core = [0] + offsets_core[:0:-1]
    offsets_row = gather_core + [offset ^ 1 for offset in gather_core]
    far_first = [0] + offsets_col[:0:-1]

    tiles, token = masked(where, green, mask)

    own = probes.T
    held = [own] + [exchange(own, "row", offset) for offset in gather_core[1:]]
    held, token = lax.optimization_barrier((held, token))
    blocks = held + [exchange(block, "row", 1) for block in held]

    parts = partial_sketch(where, tiles, blocks, token, offsets_row, offsets_col, chunks)
    totals, shares = [], []
    for chunk in range(chunks):
        terms = parts[chunk * n_col : (chunk + 1) * n_col]
        total = terms[0]
        for offset in offsets_col[1:]:
            total = total + exchange(terms[offset], "col", offset).astype(F32)
        totals.append(total)
        lowered = total.astype(BF16)
        shares.append([lowered] + [exchange(lowered, "col", offset) for offset in far_first[1:]])

    flat = [share for per_chunk in shares for share in per_chunk]
    *mine, others = partial_adjoint(where, tiles, flat, far_first, offsets_core, width, chunks)
    others = exchange(others, "row", 1)
    pairs = [m + others[k * own_width : (k + 1) * own_width] for k, m in enumerate(mine)]
    adjoint = pairs[0]
    for offset, pair in zip(offsets_core[1:], pairs[1:]):
        adjoint = adjoint + exchange(pair.astype(BF16), "row", offset).astype(F32)
    return join(totals, piece).T, adjoint.T


def solution(mesh):
    in_specs = (P("row", "col"), P("row", "col"), P("col", "row"))
    out_specs = (P("row", "col"), P("col", "row"))
    return jax.shard_map(local, mesh=mesh, in_specs=in_specs, out_specs=out_specs, check_vma=False)
```

```python
import functools

import jax
import jax.numpy as jnp
from jax import lax
from jax.experimental import pallas as pl
from jax.experimental.pallas import tpu as pltpu
from jax.sharding import PartitionSpec as P

F32, BF16 = jnp.float32, jnp.bfloat16
VMEM_LIMIT = 28 * 2**20
STEP = 512
CHUNKS = 2


def exchange(value, axis, offset):
    size = lax.axis_size(axis)
    return lax.ppermute(value, axis, [(i, i ^ offset) for i in range(size)])


def at_end(where, size):
    return (where[1] == 0) | (where[1] == size - 1)


def pass_kernel(where, mine, came, out):
    @pl.when(at_end(where, 4))
    def _():
        out[...] = mine[...].astype(BF16)

    @pl.when(jnp.logical_not(at_end(where, 4)))
    def _():
        out[...] = (mine[...] + came[...].astype(F32)).astype(BF16)


def choose_kernel(where, mine, came, out):
    @pl.when(at_end(where, 4))
    def _():
        out[...] = mine[...]

    @pl.when(jnp.logical_not(at_end(where, 4)))
    def _():
        out[...] = came[...]


def total_kernel(where, mine, near, far, came, total, lowered):
    total[...] = mine[...] + near[...].astype(F32) + far[...].astype(F32)

    @pl.when(at_end(where, 4))
    def _():
        total[...] += came[...].astype(F32)

    lowered[...] = total[...].astype(BF16)


def small(kernel, where, *values, types):
    vmem = pl.BlockSpec(memory_space=pltpu.VMEM)
    return pl.pallas_call(
        kernel,
        in_specs=[pl.BlockSpec(memory_space=pltpu.SMEM)] + [vmem] * len(values),
        out_specs=[vmem] * len(types),
        out_shape=[jax.ShapeDtypeStruct(values[0].shape, kind) for kind in types],
        compiler_params=pltpu.CompilerParams(vmem_limit_bytes=VMEM_LIMIT),
        cost_estimate=pl.CostEstimate(flops=values[0].size, bytes_accessed=8 * values[0].size, transcendentals=0),
        name=kernel.__name__.replace("_kernel", "_rows"),
    )(where, *values)


def window_sums(where, terms):
    size = len(terms)
    if size == 4:
        came = lax.ppermute(terms[2], "col", [(0, 1), (3, 2), (2, 0), (1, 3)])
        near = exchange(terms[1], "col", 1)
        (onward,) = small(pass_kernel, where, terms[3], came, types=[BF16])
        far = exchange(onward, "col", 3)
        return small(total_kernel, where, terms[0], near, far, came, types=[F32, BF16])
    total = terms[0]
    for offset in range(1, size):
        total = total + exchange(terms[offset].astype(BF16), "col", offset).astype(F32)
    return total, total.astype(BF16)


def window_spread(where, lowered, size):
    if size == 4:
        far = exchange(lowered, "col", 3)
        near = exchange(lowered, "col", 1)
        (onward,) = small(choose_kernel, where, lowered, far, types=[BF16])
        return [lowered, near, lax.ppermute(onward, "col", [(0, 2), (3, 1), (1, 0), (2, 3)]), far]
    return [lowered] + [exchange(lowered, "col", offset) for offset in range(1, size)]


def mask_kernel(where, mask_ref, green_ref, tiles, token, sems, *, block):
    rows, cols = tiles.shape
    token[...] = jnp.zeros(token.shape, token.dtype)
    copies = []
    for step in range(rows // STEP):
        at = pl.ds(step * STEP, STEP)
        copies.append(pltpu.make_async_copy(green_ref.at[at], tiles.at[at], sems.at[step]))
        copies[-1].start()
    for step, copy in enumerate(copies):
        copy.wait()
        for i in range(step * STEP // block, (step + 1) * STEP // block):
            for j in range(cols // block):

                @pl.when(mask_ref[i, j] == 0)
                def _():
                    tiles[i * block : (i + 1) * block, j * block : (j + 1) * block] = jnp.zeros((block, block), BF16)


def masked(where, green, mask):
    rows, cols = green.shape
    return pl.pallas_call(
        functools.partial(mask_kernel, block=rows // mask.shape[0]),
        in_specs=[pl.BlockSpec(memory_space=pltpu.SMEM)] * 2 + [pl.BlockSpec(memory_space=pltpu.HBM)],
        out_specs=[pl.BlockSpec(memory_space=pltpu.VMEM)] * 2,
        out_shape=[pltpu.VMEM((rows, cols), BF16), jax.ShapeDtypeStruct((8, 128), F32)],
        scratch_shapes=[pltpu.SemaphoreType.DMA((rows // STEP,))],
        compiler_params=pltpu.CompilerParams(vmem_limit_bytes=VMEM_LIMIT),
        cost_estimate=pl.CostEstimate(flops=0, bytes_accessed=2 * rows * cols, transcendentals=0),
        name="masked_tiles",
    )(where, mask, pltpu.with_memory_space_constraint(green, pltpu.HBM))


def sketch_kernel(where, tiles, token, *refs, offsets_row, offsets_col, piece):
    blocks, outs = refs[: len(offsets_row)], refs[len(offsets_row) : -2]
    probes, total = refs[-2:]
    width = blocks[0].shape[0]
    for offset, ref in zip(offsets_row, blocks):
        start = pl.multiple_of((where[0] ^ offset) * width, width)
        probes[pl.ds(start, width), :] = ref[...]
    for step in range(tiles.shape[0] // STEP):
        at = slice(step * STEP, (step + 1) * STEP)
        total[:, at] = lax.dot_general(
            probes[...], tiles[at, :], (((1,), (1,)), ((), ())), preferred_element_type=F32
        )
    share = total.shape[0] // len(offsets_col)
    for k, out in enumerate(outs):
        chunk, offset = k // len(offsets_col), offsets_col[k % len(offsets_col)]
        for n in range(out.shape[0] // piece):
            start = pl.multiple_of((where[1] ^ offset) * share + n * width + chunk * piece, piece)
            out[n * piece : (n + 1) * piece, :] = total[pl.ds(start, piece), :].astype(out.dtype)


def partial_sketch(where, tiles, blocks, token, offsets_row, offsets_col, chunks):
    rows, cols = tiles.shape
    width = blocks[0].shape[0] * len(blocks)
    share = width // len(offsets_col) // chunks
    vmem = pl.BlockSpec(memory_space=pltpu.VMEM)
    exact = (0, offsets_col[-1])
    outs = [jax.ShapeDtypeStruct((share, rows), F32 if offset in exact else BF16) for offset in offsets_col] * chunks
    return pl.pallas_call(
        functools.partial(
            sketch_kernel, offsets_row=offsets_row, offsets_col=offsets_col, piece=blocks[0].shape[0] // chunks
        ),
        in_specs=[pl.BlockSpec(memory_space=pltpu.SMEM)] + [vmem] * (2 + len(blocks)),
        out_specs=[vmem] * len(outs),
        out_shape=outs,
        scratch_shapes=[pltpu.VMEM((width, cols), BF16), pltpu.VMEM((width, rows), F32)],
        compiler_params=pltpu.CompilerParams(vmem_limit_bytes=VMEM_LIMIT),
        cost_estimate=pl.CostEstimate(
            flops=2 * width * cols * rows, bytes_accessed=2 * rows * cols, transcendentals=0
        ),
        name="partial_sketch",
    )(where, tiles, token, *blocks)


def adjoint_kernel(where, tiles, *refs, offsets_col, offsets_core, chunks):
    count = len(offsets_col) * chunks
    shares, outs = refs[:count], refs[count:-2]
    lowered, total = refs[-2:]
    share = shares[0].shape[0] * chunks
    width = outs[0].shape[0]
    piece = width // chunks
    for k, ref in enumerate(shares):
        chunk, offset = k // len(offsets_col), offsets_col[k % len(offsets_col)]
        for n in range(ref.shape[0] // piece):
            start = pl.multiple_of((where[1] ^ offset) * share + n * width + chunk * piece, piece)
            lowered[pl.ds(start, piece), :] = ref[n * piece : (n + 1) * piece, :]
    for step in range(tiles.shape[1] // STEP):
        at = slice(step * STEP, (step + 1) * STEP)
        total[:, at] = jnp.dot(lowered[...], tiles[:, at], preferred_element_type=F32)
    sibling = outs[-1]
    for k, offset in enumerate(offsets_core):
        start = pl.multiple_of((where[0] ^ offset) * width, width)
        outs[k][...] = total[pl.ds(start, width), :]
        start = pl.multiple_of((where[0] ^ 1 ^ offset) * width, width)
        sibling[k * width : (k + 1) * width, :] = total[pl.ds(start, width), :].astype(sibling.dtype)


def partial_adjoint(where, tiles, shares, offsets_col, offsets_core, width, chunks):
    rows, cols = tiles.shape
    own = width // (2 * len(offsets_core))
    heights = [own] * len(offsets_core) + [own * len(offsets_core)]
    vmem = pl.BlockSpec(memory_space=pltpu.VMEM)
    return pl.pallas_call(
        functools.partial(adjoint_kernel, offsets_col=offsets_col, offsets_core=offsets_core, chunks=chunks),
        in_specs=[pl.BlockSpec(memory_space=pltpu.SMEM)] + [vmem] * (1 + len(shares)),
        out_specs=[vmem] * len(heights),
        out_shape=[jax.ShapeDtypeStruct((h, cols), F32) for h in heights],
        scratch_shapes=[pltpu.VMEM((width, rows), BF16), pltpu.VMEM((width, cols), F32)],
        compiler_params=pltpu.CompilerParams(vmem_limit_bytes=VMEM_LIMIT),
        cost_estimate=pl.CostEstimate(
            flops=2 * width * cols * rows, bytes_accessed=2 * rows * cols, transcendentals=0
        ),
        name="partial_adjoint",
    )(where, tiles, *shares)


def join(parts, group):
    length = parts[0].shape[1]
    return jnp.concatenate([p.reshape(-1, group, length) for p in parts], axis=1).reshape(-1, length)


def local(green, mask, probes):
    n_row, n_col = lax.axis_size("row"), lax.axis_size("col")
    where = jnp.stack([lax.axis_index("row"), lax.axis_index("col")]).astype(jnp.int32)
    own_width = probes.shape[1]
    chunks = CHUNKS if own_width % (16 * CHUNKS) == 0 and n_row % n_col == 0 else 1
    piece = own_width // chunks
    width = own_width * n_row
    offsets_col = list(range(n_col))
    offsets_core = list(range(0, n_row, 2))
    gather_core = [0] + offsets_core[:0:-1]
    offsets_row = gather_core + [offset ^ 1 for offset in gather_core]

    tiles, token = masked(where, green, mask)

    own = probes.T
    held = [own] + [exchange(own, "row", offset) for offset in gather_core[1:]]
    held, token = lax.optimization_barrier((held, token))
    blocks = held + [exchange(block, "row", 1) for block in held]

    parts = partial_sketch(where, tiles, blocks, token, offsets_row, offsets_col, chunks)
    totals, shares = [], []
    for chunk in range(chunks):
        total, lowered = window_sums(where, parts[chunk * n_col : (chunk + 1) * n_col])
        totals.append(total)
        shares.append(window_spread(where, lowered, n_col))

    flat = [share for per_chunk in shares for share in per_chunk]
    *mine, others = partial_adjoint(where, tiles, flat, offsets_col, offsets_core, width, chunks)
    others = exchange(others, "row", 1)
    pairs = [m + others[k * own_width : (k + 1) * own_width] for k, m in enumerate(mine)]
    adjoint = pairs[0]
    for offset, pair in zip(offsets_core[1:], pairs[1:]):
        adjoint = adjoint + exchange(pair.astype(BF16), "row", offset).astype(F32)
    return join(totals, piece).T, adjoint.T


def solution(mesh):
    in_specs = (P("row", "col"), P("row", "col"), P("col", "row"))
    out_specs = (P("row", "col"), P("col", "row"))
    return jax.shard_map(local, mesh=mesh, in_specs=in_specs, out_specs=out_specs, check_vma=False)
```

```python
import functools

import jax
import jax.numpy as jnp
from jax import lax
from jax.experimental import pallas as pl
from jax.experimental.pallas import tpu as pltpu
from jax.sharding import PartitionSpec as P

F32, BF16 = jnp.float32, jnp.bfloat16
VMEM_LIMIT = 28 * 2**20
STEP = 512
CHUNKS = 2


def exchange(value, axis, offset):
    size = lax.axis_size(axis)
    return lax.ppermute(value, axis, [(i, i ^ offset) for i in range(size)])


def at_end(where, size):
    return (where[1] == 0) | (where[1] == size - 1)


def window_sums(terms, ends):
    size = len(terms)
    if size == 4:
        came = lax.ppermute(terms[2], "col", [(0, 1), (3, 2), (2, 0), (1, 3)]).astype(F32)
        near = exchange(terms[1], "col", 1).astype(F32)
        onward = terms[3] + jnp.where(ends > 0, 0.0, came)
        far = exchange(onward.astype(BF16), "col", 3).astype(F32)
        return terms[0] + near + far + jnp.where(ends > 0, came, 0.0)
    total = terms[0]
    for offset in range(1, size):
        total = total + exchange(terms[offset].astype(BF16), "col", offset).astype(F32)
    return total


def window_spread(lowered, ends, size):
    if size == 4:
        far = exchange(lowered, "col", 3)
        near = exchange(lowered, "col", 1)
        onward = jnp.where(ends > 0, lowered, far)
        return [lowered, near, lax.ppermute(onward, "col", [(0, 2), (3, 1), (1, 0), (2, 3)]), far]
    return [lowered] + [exchange(lowered, "col", offset) for offset in range(1, size)]


def mask_kernel(where, mask_hbm, green_ref, tiles, token, mask_ref, mask_sem, sems, *, block):
    rows, cols = tiles.shape
    token[...] = jnp.zeros(token.shape, token.dtype)
    levels = pltpu.make_async_copy(mask_hbm, mask_ref, mask_sem)
    levels.start()
    copies = []
    for step in range(rows // STEP):
        at = pl.ds(step * STEP, STEP)
        copies.append(pltpu.make_async_copy(green_ref.at[at], tiles.at[at], sems.at[step]))
        copies[-1].start()
    levels.wait()
    for step, copy in enumerate(copies):
        copy.wait()
        for i in range(step * STEP // block, (step + 1) * STEP // block):
            for j in range(cols // block):

                @pl.when(mask_ref[i, j] == 0)
                def _():
                    tiles[i * block : (i + 1) * block, j * block : (j + 1) * block] = jnp.zeros((block, block), BF16)


def masked(where, green, mask):
    rows, cols = green.shape
    return pl.pallas_call(
        functools.partial(mask_kernel, block=rows // mask.shape[0]),
        in_specs=[pl.BlockSpec(memory_space=pltpu.SMEM)] + [pl.BlockSpec(memory_space=pltpu.HBM)] * 2,
        out_specs=[pl.BlockSpec(memory_space=pltpu.VMEM)] * 2,
        out_shape=[pltpu.VMEM((rows, cols), BF16), jax.ShapeDtypeStruct((8, 128), F32)],
        scratch_shapes=[
            pltpu.SMEM(mask.shape, mask.dtype),
            pltpu.SemaphoreType.DMA,
            pltpu.SemaphoreType.DMA((rows // STEP,)),
        ],
        compiler_params=pltpu.CompilerParams(vmem_limit_bytes=VMEM_LIMIT),
        cost_estimate=pl.CostEstimate(flops=0, bytes_accessed=2 * rows * cols, transcendentals=0),
        name="masked_tiles",
    )(where, *(pltpu.with_memory_space_constraint(array, pltpu.HBM) for array in (mask, green)))


def sketch_kernel(where, tiles, token, *refs, offsets_row, offsets_col, piece):
    chunks = refs[0].shape[0] // piece
    blocks, outs = refs[: len(offsets_row)], refs[len(offsets_row) : -2 - chunks]
    probes, total = refs[-2:]
    for ends in refs[-2 - chunks : -2]:
        ends[...] = jnp.full(ends.shape, at_end(where, len(offsets_col)).astype(F32))
    width = blocks[0].shape[0]
    for offset, ref in zip(offsets_row, blocks):
        start = pl.multiple_of((where[0] ^ offset) * width, width)
        probes[pl.ds(start, width), :] = ref[...]
    for step in range(tiles.shape[0] // STEP):
        at = slice(step * STEP, (step + 1) * STEP)
        total[:, at] = lax.dot_general(
            probes[...], tiles[at, :], (((1,), (1,)), ((), ())), preferred_element_type=F32
        )
    share = total.shape[0] // len(offsets_col)
    for k, out in enumerate(outs):
        chunk, offset = k // len(offsets_col), offsets_col[k % len(offsets_col)]
        for n in range(out.shape[0] // piece):
            start = pl.multiple_of((where[1] ^ offset) * share + n * width + chunk * piece, piece)
            out[n * piece : (n + 1) * piece, :] = total[pl.ds(start, piece), :].astype(out.dtype)


def partial_sketch(where, tiles, blocks, token, offsets_row, offsets_col, chunks):
    rows, cols = tiles.shape
    width = blocks[0].shape[0] * len(blocks)
    share = width // len(offsets_col) // chunks
    vmem = pl.BlockSpec(memory_space=pltpu.VMEM)
    exact = (0, offsets_col[-1])
    outs = [jax.ShapeDtypeStruct((share, rows), F32 if offset in exact else BF16) for offset in offsets_col] * chunks
    outs += [jax.ShapeDtypeStruct((share, rows), F32)] * chunks
    return pl.pallas_call(
        functools.partial(
            sketch_kernel, offsets_row=offsets_row, offsets_col=offsets_col, piece=blocks[0].shape[0] // chunks
        ),
        in_specs=[pl.BlockSpec(memory_space=pltpu.SMEM)] + [vmem] * (2 + len(blocks)),
        out_specs=[vmem] * len(outs),
        out_shape=outs,
        scratch_shapes=[pltpu.VMEM((width, cols), BF16), pltpu.VMEM((width, rows), F32)],
        compiler_params=pltpu.CompilerParams(vmem_limit_bytes=VMEM_LIMIT),
        cost_estimate=pl.CostEstimate(
            flops=2 * width * cols * rows, bytes_accessed=2 * rows * cols, transcendentals=0
        ),
        name="partial_sketch",
    )(where, tiles, token, *blocks)


def adjoint_kernel(where, tiles, *refs, offsets_col, offsets_core, chunks):
    count = len(offsets_col) * chunks
    shares, outs = refs[:count], refs[count:-2]
    lowered, total = refs[-2:]
    share = shares[0].shape[0] * chunks
    width = outs[0].shape[0]
    piece = width // chunks
    for k, ref in enumerate(shares):
        chunk, offset = k // len(offsets_col), offsets_col[k % len(offsets_col)]
        for n in range(ref.shape[0] // piece):
            start = pl.multiple_of((where[1] ^ offset) * share + n * width + chunk * piece, piece)
            lowered[pl.ds(start, piece), :] = ref[n * piece : (n + 1) * piece, :]
    for step in range(tiles.shape[1] // STEP):
        at = slice(step * STEP, (step + 1) * STEP)
        total[:, at] = jnp.dot(lowered[...], tiles[:, at], preferred_element_type=F32)
    sibling = outs[-1]
    for k, offset in enumerate(offsets_core):
        start = pl.multiple_of((where[0] ^ offset) * width, width)
        outs[k][...] = total[pl.ds(start, width), :]
        start = pl.multiple_of((where[0] ^ 1 ^ offset) * width, width)
        sibling[k * width : (k + 1) * width, :] = total[pl.ds(start, width), :].astype(sibling.dtype)


def partial_adjoint(where, tiles, shares, offsets_col, offsets_core, width, chunks):
    rows, cols = tiles.shape
    own = width // (2 * len(offsets_core))
    heights = [own] * len(offsets_core) + [own * len(offsets_core)]
    vmem = pl.BlockSpec(memory_space=pltpu.VMEM)
    return pl.pallas_call(
        functools.partial(adjoint_kernel, offsets_col=offsets_col, offsets_core=offsets_core, chunks=chunks),
        in_specs=[pl.BlockSpec(memory_space=pltpu.SMEM)] + [vmem] * (1 + len(shares)),
        out_specs=[vmem] * len(heights),
        out_shape=[jax.ShapeDtypeStruct((h, cols), F32) for h in heights],
        scratch_shapes=[pltpu.VMEM((width, rows), BF16), pltpu.VMEM((width, cols), F32)],
        compiler_params=pltpu.CompilerParams(vmem_limit_bytes=VMEM_LIMIT),
        cost_estimate=pl.CostEstimate(
            flops=2 * width * cols * rows, bytes_accessed=2 * rows * cols, transcendentals=0
        ),
        name="partial_adjoint",
    )(where, tiles, *shares)


def join(parts, group):
    length = parts[0].shape[1]
    return jnp.concatenate([p.reshape(-1, group, length) for p in parts], axis=1).reshape(-1, length)


def local(green, mask, probes):
    n_row, n_col = lax.axis_size("row"), lax.axis_size("col")
    where = jnp.stack([lax.axis_index("row"), lax.axis_index("col")]).astype(jnp.int32)
    own_width = probes.shape[1]
    chunks = CHUNKS if own_width % (16 * CHUNKS) == 0 and n_row % n_col == 0 else 1
    piece = own_width // chunks
    width = own_width * n_row
    offsets_col = list(range(n_col))
    offsets_core = list(range(0, n_row, 2))
    gather_core = [0] + offsets_core[:0:-1]
    offsets_row = gather_core + [offset ^ 1 for offset in gather_core]

    tiles, token = masked(where, green, mask)

    own = probes.T
    held = [own] + [exchange(own, "row", offset) for offset in gather_core[1:]]
    twin = exchange(own, "row", 1)
    held, token = lax.optimization_barrier((held, token))
    blocks = held + [twin] + [exchange(block, "row", 1) for block in held[1:]]

    parts = partial_sketch(where, tiles, blocks, token, offsets_row, offsets_col, chunks)
    totals, shares = [], []
    parts, ends = parts[:-chunks], parts[-chunks:]
    for chunk in range(chunks):
        totals.append(window_sums(parts[chunk * n_col : (chunk + 1) * n_col], ends[chunk]))
        shares.append(window_spread(totals[-1].astype(BF16), ends[chunk], n_col))

    flat = [share for per_chunk in shares for share in per_chunk]
    *mine, others = partial_adjoint(where, tiles, flat, offsets_col, offsets_core, width, chunks)
    others = exchange(others, "row", 1)
    pairs = [m + others[k * own_width : (k + 1) * own_width] for k, m in enumerate(mine)]
    adjoint = pairs[0]
    for offset, pair in zip(offsets_core[1:], pairs[1:]):
        adjoint = adjoint + exchange(pair.astype(BF16), "row", offset).astype(F32)
    return join(totals, piece).T, adjoint.T


def solution(mesh):
    in_specs = (P("row", "col"), P("row", "col"), P("col", "row"))
    out_specs = (P("row", "col"), P("col", "row"))
    return jax.shard_map(local, mesh=mesh, in_specs=in_specs, out_specs=out_specs, check_vma=False)
```

```python
import functools

import jax
import jax.numpy as jnp
from jax import lax
from jax.experimental import pallas as pl
from jax.experimental.pallas import tpu as pltpu
from jax.sharding import PartitionSpec as P

F32, BF16 = jnp.float32, jnp.bfloat16
VMEM_LIMIT = 28 * 2**20
STEP = 512
CHUNKS = 2


def exchange(value, axis, offset):
    size = lax.axis_size(axis)
    return lax.ppermute(value, axis, [(i, i ^ offset) for i in range(size)])


def at_end(where, size):
    return (where[1] == 0) | (where[1] == size - 1)


def after(value, earlier):
    return lax.optimization_barrier((value, earlier))[0]


def window_sums(terms, ends):
    size = len(terms)
    if size == 4:
        came = lax.ppermute(terms[2], "col", [(0, 1), (3, 2), (2, 0), (1, 3)])
        came = came.astype(F32)
        onward = terms[3] + jnp.where(ends > 0, 0.0, came)
        onward = onward.astype(BF16)
        far = exchange(onward, "col", 3).astype(F32)
        near = exchange(after(terms[1], onward), "col", 1).astype(F32)
        return terms[0] + near + far + jnp.where(ends > 0, came, 0.0)
    total = terms[0]
    for offset in range(1, size):
        total = total + exchange(terms[offset].astype(BF16), "col", offset).astype(F32)
    return total


def window_spread(lowered, ends, size):
    if size == 4:
        far = exchange(lowered, "col", 3)
        near = exchange(lowered, "col", 1)
        onward = jnp.where(ends > 0, lowered, far)
        return [lowered, near, lax.ppermute(onward, "col", [(0, 2), (3, 1), (1, 0), (2, 3)]), far]
    return [lowered] + [exchange(lowered, "col", offset) for offset in range(1, size)]


def mask_kernel(where, mask_hbm, green_ref, tiles, token, mask_ref, mask_sem, sems, *, block):
    rows, cols = tiles.shape
    token[...] = jnp.zeros(token.shape, token.dtype)
    levels = pltpu.make_async_copy(mask_hbm, mask_ref, mask_sem)
    levels.start()
    copies = []
    for step in range(rows // STEP):
        at = pl.ds(step * STEP, STEP)
        copies.append(pltpu.make_async_copy(green_ref.at[at], tiles.at[at], sems.at[step]))
        copies[-1].start()
    levels.wait()
    for step, copy in enumerate(copies):
        copy.wait()
        for i in range(step * STEP // block, (step + 1) * STEP // block):
            for j in range(cols // block):

                @pl.when(mask_ref[i, j] == 0)
                def _():
                    tiles[i * block : (i + 1) * block, j * block : (j + 1) * block] = jnp.zeros((block, block), BF16)


def masked(where, green, mask):
    rows, cols = green.shape
    return pl.pallas_call(
        functools.partial(mask_kernel, block=rows // mask.shape[0]),
        in_specs=[pl.BlockSpec(memory_space=pltpu.SMEM)] + [pl.BlockSpec(memory_space=pltpu.HBM)] * 2,
        out_specs=[pl.BlockSpec(memory_space=pltpu.VMEM)] * 2,
        out_shape=[pltpu.VMEM((rows, cols), BF16), jax.ShapeDtypeStruct((8, 128), F32)],
        scratch_shapes=[
            pltpu.SMEM(mask.shape, mask.dtype),
            pltpu.SemaphoreType.DMA,
            pltpu.SemaphoreType.DMA((rows // STEP,)),
        ],
        compiler_params=pltpu.CompilerParams(vmem_limit_bytes=VMEM_LIMIT),
        cost_estimate=pl.CostEstimate(flops=0, bytes_accessed=2 * rows * cols, transcendentals=0),
        name="masked_tiles",
    )(where, *(pltpu.with_memory_space_constraint(array, pltpu.HBM) for array in (mask, green)))


def sketch_kernel(where, tiles, token, *refs, offsets_row, offsets_col, piece):
    chunks = refs[0].shape[0] // piece
    blocks, outs = refs[: len(offsets_row)], refs[len(offsets_row) : -2 - chunks]
    probes, total = refs[-2:]
    for ends in refs[-2 - chunks : -2]:
        ends[...] = jnp.full(ends.shape, at_end(where, len(offsets_col)).astype(F32))
    width = blocks[0].shape[0]
    for offset, ref in zip(offsets_row, blocks):
        start = pl.multiple_of((where[0] ^ offset) * width, width)
        probes[pl.ds(start, width), :] = ref[...]
    for step in range(tiles.shape[0] // STEP):
        at = slice(step * STEP, (step + 1) * STEP)
        total[:, at] = lax.dot_general(
            probes[...], tiles[at, :], (((1,), (1,)), ((), ())), preferred_element_type=F32
        )
    share = total.shape[0] // len(offsets_col)
    for k, out in enumerate(outs):
        chunk, offset = k // len(offsets_col), offsets_col[k % len(offsets_col)]
        for n in range(out.shape[0] // piece):
            start = pl.multiple_of((where[1] ^ offset) * share + n * width + chunk * piece, piece)
            out[n * piece : (n + 1) * piece, :] = total[pl.ds(start, piece), :].astype(out.dtype)


def partial_sketch(where, tiles, blocks, token, offsets_row, offsets_col, chunks):
    rows, cols = tiles.shape
    width = blocks[0].shape[0] * len(blocks)
    share = width // len(offsets_col) // chunks
    vmem = pl.BlockSpec(memory_space=pltpu.VMEM)
    exact = (0, offsets_col[-1])
    outs = [jax.ShapeDtypeStruct((share, rows), F32 if offset in exact else BF16) for offset in offsets_col] * chunks
    outs += [jax.ShapeDtypeStruct((share, rows), F32)] * chunks
    return pl.pallas_call(
        functools.partial(
            sketch_kernel, offsets_row=offsets_row, offsets_col=offsets_col, piece=blocks[0].shape[0] // chunks
        ),
        in_specs=[pl.BlockSpec(memory_space=pltpu.SMEM)] + [vmem] * (2 + len(blocks)),
        out_specs=[vmem] * len(outs),
        out_shape=outs,
        scratch_shapes=[pltpu.VMEM((width, cols), BF16), pltpu.VMEM((width, rows), F32)],
        compiler_params=pltpu.CompilerParams(vmem_limit_bytes=VMEM_LIMIT),
        cost_estimate=pl.CostEstimate(
            flops=2 * width * cols * rows, bytes_accessed=2 * rows * cols, transcendentals=0
        ),
        name="partial_sketch",
    )(where, tiles, token, *blocks)


def adjoint_kernel(where, tiles, *refs, offsets_col, offsets_core, chunks):
    count = len(offsets_col) * chunks
    shares, outs = refs[:count], refs[count:-2]
    lowered, total = refs[-2:]
    share = shares[0].shape[0] * chunks
    width = outs[0].shape[0]
    piece = width // chunks
    for k, ref in enumerate(shares):
        chunk, offset = k // len(offsets_col), offsets_col[k % len(offsets_col)]
        for n in range(ref.shape[0] // piece):
            start = pl.multiple_of((where[1] ^ offset) * share + n * width + chunk * piece, piece)
            lowered[pl.ds(start, piece), :] = ref[n * piece : (n + 1) * piece, :]
    for step in range(tiles.shape[1] // STEP):
        at = slice(step * STEP, (step + 1) * STEP)
        total[:, at] = jnp.dot(lowered[...], tiles[:, at], preferred_element_type=F32)
    sibling = outs[-1]
    for k, offset in enumerate(offsets_core):
        start = pl.multiple_of((where[0] ^ offset) * width, width)
        outs[k][...] = total[pl.ds(start, width), :]
        start = pl.multiple_of((where[0] ^ 1 ^ offset) * width, width)
        sibling[k * width : (k + 1) * width, :] = total[pl.ds(start, width), :].astype(sibling.dtype)


def partial_adjoint(where, tiles, shares, offsets_col, offsets_core, width, chunks):
    rows, cols = tiles.shape
    own = width // (2 * len(offsets_core))
    heights = [own] * len(offsets_core) + [own * len(offsets_core)]
    vmem = pl.BlockSpec(memory_space=pltpu.VMEM)
    return pl.pallas_call(
        functools.partial(adjoint_kernel, offsets_col=offsets_col, offsets_core=offsets_core, chunks=chunks),
        in_specs=[pl.BlockSpec(memory_space=pltpu.SMEM)] + [vmem] * (1 + len(shares)),
        out_specs=[vmem] * len(heights),
        out_shape=[jax.ShapeDtypeStruct((h, cols), F32) for h in heights],
        scratch_shapes=[pltpu.VMEM((width, rows), BF16), pltpu.VMEM((width, cols), F32)],
        compiler_params=pltpu.CompilerParams(vmem_limit_bytes=VMEM_LIMIT),
        cost_estimate=pl.CostEstimate(
            flops=2 * width * cols * rows, bytes_accessed=2 * rows * cols, transcendentals=0
        ),
        name="partial_adjoint",
    )(where, tiles, *shares)


def join(parts, group):
    length = parts[0].shape[1]
    return jnp.concatenate([p.reshape(-1, group, length) for p in parts], axis=1).reshape(-1, length)


def local(green, mask, probes):
    n_row, n_col = lax.axis_size("row"), lax.axis_size("col")
    where = jnp.stack([lax.axis_index("row"), lax.axis_index("col")]).astype(jnp.int32)
    own_width = probes.shape[1]
    chunks = CHUNKS if own_width % (16 * CHUNKS) == 0 and n_row % n_col == 0 else 1
    piece = own_width // chunks
    width = own_width * n_row
    offsets_col = list(range(n_col))
    offsets_core = list(range(0, n_row, 2))
    gather_core = [0] + offsets_core[:0:-1]
    offsets_row = gather_core + [offset ^ 1 for offset in gather_core]

    tiles, token = masked(where, green, mask)

    own = probes.T
    held = [own] + [exchange(own, "row", offset) for offset in gather_core[1:]]
    twin = exchange(own, "row", 1)
    held, token = lax.optimization_barrier((held, token))
    blocks = held + [twin] + [exchange(block, "row", 1) for block in held[1:]]

    parts = partial_sketch(where, tiles, blocks, token, offsets_row, offsets_col, chunks)
    totals, shares = [], []
    parts, ends = parts[:-chunks], parts[-chunks:]
    for chunk in range(chunks):
        totals.append(window_sums(parts[chunk * n_col : (chunk + 1) * n_col], ends[chunk]))
        shares.append(window_spread(totals[-1].astype(BF16), ends[chunk], n_col))

    flat = [share for per_chunk in shares for share in per_chunk]
    *mine, others = partial_adjoint(where, tiles, flat, offsets_col, offsets_core, width, chunks)
    others = exchange(others, "row", 1)
    pairs = [m + others[k * own_width : (k + 1) * own_width] for k, m in enumerate(mine)]
    adjoint = pairs[0]
    for offset in offsets_core[1:2] + offsets_core[:1:-1]:
        adjoint = adjoint + exchange(pairs[offset // 2].astype(BF16), "row", offset).astype(F32)
    return join(totals, piece).T, adjoint.T


def solution(mesh):
    in_specs = (P("row", "col"), P("row", "col"), P("col", "row"))
    out_specs = (P("row", "col"), P("col", "row"))
    return jax.shard_map(local, mesh=mesh, in_specs=in_specs, out_specs=out_specs, check_vma=False)
```

```python
import functools

import jax
import jax.numpy as jnp
from jax import lax
from jax.experimental import pallas as pl
from jax.experimental.pallas import tpu as pltpu
from jax.sharding import PartitionSpec as P

F32, BF16 = jnp.float32, jnp.bfloat16
VMEM_LIMIT = 28 * 2**20
STEP = 512
CHUNKS = 2


def exchange(value, axis, offset):
    size = lax.axis_size(axis)
    return lax.ppermute(value, axis, [(i, i ^ offset) for i in range(size)])


def at_end(where, size):
    return (where[1] == 0) | (where[1] == size - 1)


def after(value, earlier):
    return lax.optimization_barrier((value, earlier))[0]


def window_sums(terms, ends):
    size = len(terms)
    if size == 4:
        came = lax.ppermute(terms[2], "col", [(0, 1), (3, 2), (2, 0), (1, 3)])
        came = came.astype(F32)
        onward = terms[3] + jnp.where(ends > 0, 0.0, came)
        onward = onward.astype(BF16)
        far = exchange(onward, "col", 3).astype(F32)
        near = exchange(after(terms[1], onward), "col", 1).astype(F32)
        return terms[0] + near + far + jnp.where(ends > 0, came, 0.0)
    total = terms[0]
    for offset in range(1, size):
        total = total + exchange(terms[offset].astype(BF16), "col", offset).astype(F32)
    return total


def window_spread(lowered, ends, size):
    if size == 4:
        far = exchange(lowered, "col", 3)
        near = exchange(lowered, "col", 1)
        onward = jnp.where(ends > 0, lowered, far)
        return [lowered, near, lax.ppermute(onward, "col", [(0, 2), (3, 1), (1, 0), (2, 3)]), far]
    return [lowered] + [exchange(lowered, "col", offset) for offset in range(1, size)]


def mask_kernel(where, mask_hbm, green_ref, tiles, token, mask_ref, mask_sem, sems, *, block):
    rows, cols = tiles.shape
    token[...] = jnp.zeros(token.shape, token.dtype)
    levels = pltpu.make_async_copy(mask_hbm, mask_ref, mask_sem)
    levels.start()
    copies = []
    for step in range(rows // STEP):
        at = pl.ds(step * STEP, STEP)
        copies.append(pltpu.make_async_copy(green_ref.at[at], tiles.at[at], sems.at[step]))
        copies[-1].start()
    levels.wait()
    for step, copy in enumerate(copies):
        copy.wait()
        for i in range(step * STEP // block, (step + 1) * STEP // block):
            for j in range(cols // block):

                @pl.when(mask_ref[i, j] == 0)
                def _():
                    tiles[i * block : (i + 1) * block, j * block : (j + 1) * block] = jnp.zeros((block, block), BF16)


def masked(where, green, mask):
    rows, cols = green.shape
    return pl.pallas_call(
        functools.partial(mask_kernel, block=rows // mask.shape[0]),
        in_specs=[pl.BlockSpec(memory_space=pltpu.SMEM)] + [pl.BlockSpec(memory_space=pltpu.HBM)] * 2,
        out_specs=[pl.BlockSpec(memory_space=pltpu.VMEM)] * 2,
        out_shape=[pltpu.VMEM((rows, cols), BF16), jax.ShapeDtypeStruct((8, 128), F32)],
        scratch_shapes=[
            pltpu.SMEM(mask.shape, mask.dtype),
            pltpu.SemaphoreType.DMA,
            pltpu.SemaphoreType.DMA((rows // STEP,)),
        ],
        compiler_params=pltpu.CompilerParams(vmem_limit_bytes=VMEM_LIMIT),
        cost_estimate=pl.CostEstimate(flops=0, bytes_accessed=2 * rows * cols, transcendentals=0),
        name="masked_tiles",
    )(where, *(pltpu.with_memory_space_constraint(array, pltpu.HBM) for array in (mask, green)))


def sketch_kernel(where, tiles, token, *refs, base, offsets_row, offsets_col):
    blocks, outs, ends, probes = refs[: len(offsets_row)], refs[len(offsets_row) : -2], refs[-2], refs[-1]
    own = blocks[0].shape[0]
    ratio = len(offsets_row) // len(offsets_col)
    share = own * ratio
    ends[...] = jnp.full(ends.shape, at_end(where, len(offsets_col)).astype(F32))
    for offset, ref in zip(offsets_row, blocks):
        column = where[0] ^ offset
        start = (lax.div(column, ratio) ^ where[1]) * share + lax.rem(column, ratio) * own
        probes[pl.ds(pl.multiple_of(start, own), own), :] = ref[...]
    for step in range(ends.shape[1] // STEP):
        rows, at = slice(base + step * STEP, base + (step + 1) * STEP), slice(step * STEP, (step + 1) * STEP)
        term = lax.dot_general(probes[...], tiles[rows, :], (((1,), (1,)), ((), ())), preferred_element_type=F32)
        for k, out in enumerate(outs):
            out[:, at] = term[k * share : (k + 1) * share].astype(out.dtype)


def partial_sketch(where, tiles, blocks, token, offsets_row, offsets_col, chunk, chunks):
    rows, cols = tiles.shape
    rows //= chunks
    width = blocks[0].shape[0] * len(blocks)
    share = width // len(offsets_col)
    vmem = pl.BlockSpec(memory_space=pltpu.VMEM)
    exact = (0, offsets_col[-1])
    outs = [jax.ShapeDtypeStruct((share, rows), F32 if offset in exact else BF16) for offset in offsets_col]
    outs.append(jax.ShapeDtypeStruct((share, rows), F32))
    return pl.pallas_call(
        functools.partial(sketch_kernel, base=chunk * rows, offsets_row=offsets_row, offsets_col=offsets_col),
        in_specs=[pl.BlockSpec(memory_space=pltpu.SMEM)] + [vmem] * (2 + len(blocks)),
        out_specs=[vmem] * len(outs),
        out_shape=outs,
        scratch_shapes=[pltpu.VMEM((width, cols), BF16)],
        compiler_params=pltpu.CompilerParams(vmem_limit_bytes=VMEM_LIMIT),
        cost_estimate=pl.CostEstimate(
            flops=2 * width * cols * rows, bytes_accessed=2 * rows * cols, transcendentals=0
        ),
        name="partial_sketch",
    )(where, tiles, token, *blocks)


def adjoint_kernel(where, tiles, *refs, base, parts, offsets_col, devices):
    shares, earlier, outs, lowered = refs[: len(offsets_col)], refs[len(offsets_col) : -1 - parts], refs[-1 - parts : -1], refs[-1]
    share, rows = shares[0].shape
    ratio = devices // len(offsets_col)
    own = share // ratio
    for offset, ref in zip(offsets_col, shares):
        for n in range(ratio):
            apart = where[0] ^ ((where[1] ^ offset) * ratio + n)
            start = ((apart >> 1) + (apart & 1) * (devices // 2)) * own
            lowered[pl.ds(pl.multiple_of(start, own), own), :] = ref[n * own : (n + 1) * own, :]
    for step in range(tiles.shape[1] // STEP):
        at = slice(step * STEP, (step + 1) * STEP)
        term = jnp.dot(lowered[...], tiles[base : base + rows, at], preferred_element_type=F32)
        if earlier:
            term += earlier[0][:, at]
        height = outs[0].shape[0]
        for k, out in enumerate(outs):
            out[:, at] = term[k * height : (k + 1) * height]


def partial_adjoint(where, tiles, shares, earlier, offsets_col, devices, chunk, chunks):
    rows, cols = tiles.shape
    rows //= chunks
    width = shares[0].shape[0] * len(offsets_col)
    parts = 2 if chunk == chunks - 1 else 1
    vmem = pl.BlockSpec(memory_space=pltpu.VMEM)
    return pl.pallas_call(
        functools.partial(
            adjoint_kernel, base=chunk * rows, parts=parts, offsets_col=offsets_col, devices=devices
        ),
        in_specs=[pl.BlockSpec(memory_space=pltpu.SMEM)] + [vmem] * (1 + len(shares) + len(earlier)),
        out_specs=[vmem] * parts,
        out_shape=[jax.ShapeDtypeStruct((width // parts, cols), F32)] * parts,
        scratch_shapes=[pltpu.VMEM((width, rows), BF16)],
        compiler_params=pltpu.CompilerParams(vmem_limit_bytes=VMEM_LIMIT),
        cost_estimate=pl.CostEstimate(
            flops=2 * width * cols * rows, bytes_accessed=2 * rows * cols, transcendentals=0
        ),
        name="partial_adjoint",
    )(where, tiles, *shares, *earlier)


def local(green, mask, probes):
    n_row, n_col = lax.axis_size("row"), lax.axis_size("col")
    where = jnp.stack([lax.axis_index("row"), lax.axis_index("col")]).astype(jnp.int32)
    own_width = probes.shape[1]
    chunks = CHUNKS if green.shape[0] % (CHUNKS * STEP) == 0 else 1
    offsets_col = list(range(n_col))
    offsets_core = list(range(0, n_row, 2))
    gather_core = [0] + offsets_core[:0:-1]
    offsets_row = gather_core + [offset ^ 1 for offset in gather_core]
    tiles, token = masked(where, green, mask)

    own = probes.T
    held = [own] + [exchange(own, "row", offset) for offset in gather_core[1:]]
    twin = exchange(own, "row", 1)
    held, token = lax.optimization_barrier((held, token))
    blocks = held + [twin] + [exchange(block, "row", 1) for block in held[1:]]

    totals, shares = [], []
    for chunk in range(chunks):
        *parts, ends = partial_sketch(where, tiles, blocks, token, offsets_row, offsets_col, chunk, chunks)
        totals.append(window_sums(parts, ends))
        shares.append(window_spread(totals[-1].astype(BF16), ends, n_col))

    earlier = []
    for chunk in range(chunks):
        earlier = partial_adjoint(where, tiles, shares[chunk], earlier, offsets_col, n_row, chunk, chunks)
    mine, others = earlier
    others = exchange(others, "row", 1)
    cuts = [slice(k * own_width, (k + 1) * own_width) for k in range(len(offsets_core))]
    pairs = [mine[cut] + others[cut] for cut in cuts]
    adjoint = pairs[0]
    for offset in offsets_core[1:2] + offsets_core[:1:-1]:
        adjoint = adjoint + exchange(pairs[offset // 2].astype(BF16), "row", offset).astype(F32)
    return jnp.concatenate(totals, axis=1).T, adjoint.T


def solution(mesh):
    in_specs = (P("row", "col"), P("row", "col"), P("col", "row"))
    out_specs = (P("row", "col"), P("col", "row"))
    return jax.shard_map(local, mesh=mesh, in_specs=in_specs, out_specs=out_specs, check_vma=False)
```

```python
import functools

import jax
import jax.numpy as jnp
from jax import lax
from jax.experimental import pallas as pl
from jax.experimental.pallas import tpu as pltpu
from jax.sharding import PartitionSpec as P

F32, BF16 = jnp.float32, jnp.bfloat16
VMEM_LIMIT = 28 * 2**20
STEP = 512
CHUNKS = 2


def exchange(value, axis, offset):
    size = lax.axis_size(axis)
    return lax.ppermute(value, axis, [(i, i ^ offset) for i in range(size)])


def at_end(where, size):
    return (where[1] == 0) | (where[1] == size - 1)


def after(value, earlier):
    return lax.optimization_barrier((value, earlier))[0]


def window_sums(terms, ends):
    size = len(terms)
    if size == 4:
        came = lax.ppermute(terms[2], "col", [(0, 1), (3, 2), (2, 0), (1, 3)])
        came = came.astype(F32)
        onward = terms[3] + jnp.where(ends > 0, 0.0, came)
        onward = onward.astype(BF16)
        far = exchange(onward, "col", 3).astype(F32)
        near = exchange(after(terms[1], onward), "col", 1).astype(F32)
        return terms[0] + near + far + jnp.where(ends > 0, came, 0.0)
    total = terms[0]
    for offset in range(1, size):
        total = total + exchange(terms[offset].astype(BF16), "col", offset).astype(F32)
    return total


def window_spread(lowered, ends, size):
    if size == 4:
        far = exchange(lowered, "col", 3)
        near = exchange(lowered, "col", 1)
        onward = jnp.where(ends > 0, lowered, far)
        return [lowered, near, lax.ppermute(onward, "col", [(0, 2), (3, 1), (1, 0), (2, 3)]), far]
    return [lowered] + [exchange(lowered, "col", offset) for offset in range(1, size)]


def mask_kernel(where, mask_hbm, green_ref, tiles, token, mask_ref, mask_sem, sems, *, block):
    rows, cols = tiles.shape
    token[...] = jnp.zeros(token.shape, token.dtype)
    levels = pltpu.make_async_copy(mask_hbm, mask_ref, mask_sem)
    levels.start()
    copies = []
    for step in range(rows // STEP):
        at = pl.ds(step * STEP, STEP)
        copies.append(pltpu.make_async_copy(green_ref.at[at], tiles.at[at], sems.at[step]))
        copies[-1].start()
    levels.wait()
    for step, copy in enumerate(copies):
        copy.wait()
        for i in range(step * STEP // block, (step + 1) * STEP // block):
            for j in range(cols // block):

                @pl.when(mask_ref[i, j] == 0)
                def _():
                    tiles[i * block : (i + 1) * block, j * block : (j + 1) * block] = jnp.zeros((block, block), BF16)


def masked(where, green, mask):
    rows, cols = green.shape
    return pl.pallas_call(
        functools.partial(mask_kernel, block=rows // mask.shape[0]),
        in_specs=[pl.BlockSpec(memory_space=pltpu.SMEM)] + [pl.BlockSpec(memory_space=pltpu.HBM)] * 2,
        out_specs=[pl.BlockSpec(memory_space=pltpu.VMEM)] * 2,
        out_shape=[pltpu.VMEM((rows, cols), BF16), jax.ShapeDtypeStruct((8, 128), F32)],
        scratch_shapes=[
            pltpu.SMEM(mask.shape, mask.dtype),
            pltpu.SemaphoreType.DMA,
            pltpu.SemaphoreType.DMA((rows // STEP,)),
        ],
        compiler_params=pltpu.CompilerParams(vmem_limit_bytes=VMEM_LIMIT),
        cost_estimate=pl.CostEstimate(flops=0, bytes_accessed=2 * rows * cols, transcendentals=0),
        name="masked_tiles",
    )(where, *(pltpu.with_memory_space_constraint(array, pltpu.HBM) for array in (mask, green)))


def sketch_kernel(where, tiles, token, *refs, base, offsets_row, offsets_col):
    count = len(refs) - 2 - len(offsets_col)
    blocks, outs, ends, probes = refs[:count], refs[count:-2], refs[-2], refs[-1]
    own = probes.shape[0] // len(offsets_row)
    ratio = len(offsets_row) // len(offsets_col)
    share = own * ratio
    ends[...] = jnp.full(ends.shape, at_end(where, len(offsets_col)).astype(F32))
    pieces = [(ref, at) for ref in blocks for at in range(0, ref.shape[0], own)]
    for offset, (ref, at) in zip(offsets_row, pieces):
        column = where[0] ^ offset
        start = (lax.div(column, ratio) ^ where[1]) * share + lax.rem(column, ratio) * own
        probes[pl.ds(pl.multiple_of(start, own), own), :] = ref[at : at + own, :]
    for step in range(ends.shape[1] // STEP):
        rows, at = slice(base + step * STEP, base + (step + 1) * STEP), slice(step * STEP, (step + 1) * STEP)
        term = lax.dot_general(probes[...], tiles[rows, :], (((1,), (1,)), ((), ())), preferred_element_type=F32)
        for k, out in enumerate(outs):
            out[:, at] = term[k * share : (k + 1) * share].astype(out.dtype)


def partial_sketch(where, tiles, blocks, token, offsets_row, offsets_col, chunk, chunks):
    rows, cols = tiles.shape
    rows //= chunks
    width = blocks[0].shape[0] * len(blocks)
    share = width // len(offsets_col)
    vmem = pl.BlockSpec(memory_space=pltpu.VMEM)
    exact = (0, offsets_col[-1])
    outs = [jax.ShapeDtypeStruct((share, rows), F32 if offset in exact else BF16) for offset in offsets_col]
    outs.append(jax.ShapeDtypeStruct((share, rows), F32))
    return pl.pallas_call(
        functools.partial(sketch_kernel, base=chunk * rows, offsets_row=offsets_row, offsets_col=offsets_col),
        in_specs=[pl.BlockSpec(memory_space=pltpu.SMEM)] + [vmem] * (2 + len(blocks)),
        out_specs=[vmem] * len(outs),
        out_shape=outs,
        scratch_shapes=[pltpu.VMEM((width, cols), BF16)],
        compiler_params=pltpu.CompilerParams(vmem_limit_bytes=VMEM_LIMIT),
        cost_estimate=pl.CostEstimate(
            flops=2 * width * cols * rows, bytes_accessed=2 * rows * cols, transcendentals=0
        ),
        name="partial_sketch",
    )(where, tiles, token, *blocks)


def adjoint_kernel(where, tiles, *refs, base, parts, offsets_col, devices):
    shares, earlier, outs, lowered = refs[: len(offsets_col)], refs[len(offsets_col) : -1 - parts], refs[-1 - parts : -1], refs[-1]
    share, rows = shares[0].shape
    ratio = devices // len(offsets_col)
    own = share // ratio
    for offset, ref in zip(offsets_col, shares):
        for n in range(ratio):
            apart = where[0] ^ ((where[1] ^ offset) * ratio + n)
            start = ((apart >> 1) + (apart & 1) * (devices // 2)) * own
            lowered[pl.ds(pl.multiple_of(start, own), own), :] = ref[n * own : (n + 1) * own, :]
    for step in range(tiles.shape[1] // STEP):
        at = slice(step * STEP, (step + 1) * STEP)
        term = jnp.dot(lowered[...], tiles[base : base + rows, at], preferred_element_type=F32)
        if earlier:
            term += earlier[0][:, at]
        height = outs[0].shape[0]
        for k, out in enumerate(outs):
            out[:, at] = term[k * height : (k + 1) * height]


def partial_adjoint(where, tiles, shares, earlier, offsets_col, devices, chunk, chunks):
    rows, cols = tiles.shape
    rows //= chunks
    width = shares[0].shape[0] * len(offsets_col)
    parts = 2 if chunk == chunks - 1 else 1
    vmem = pl.BlockSpec(memory_space=pltpu.VMEM)
    return pl.pallas_call(
        functools.partial(
            adjoint_kernel, base=chunk * rows, parts=parts, offsets_col=offsets_col, devices=devices
        ),
        in_specs=[pl.BlockSpec(memory_space=pltpu.SMEM)] + [vmem] * (1 + len(shares) + len(earlier)),
        out_specs=[vmem] * parts,
        out_shape=[jax.ShapeDtypeStruct((width // parts, cols), F32)] * parts,
        scratch_shapes=[pltpu.VMEM((width, rows), BF16)],
        compiler_params=pltpu.CompilerParams(vmem_limit_bytes=VMEM_LIMIT),
        cost_estimate=pl.CostEstimate(
            flops=2 * width * cols * rows, bytes_accessed=2 * rows * cols, transcendentals=0
        ),
        name="partial_adjoint",
    )(where, tiles, *shares, *earlier)


def local(green, mask, probes):
    n_row, n_col = lax.axis_size("row"), lax.axis_size("col")
    where = jnp.stack([lax.axis_index("row"), lax.axis_index("col")]).astype(jnp.int32)
    own_width = probes.shape[1]
    chunks = CHUNKS if green.shape[0] % (CHUNKS * STEP) == 0 else 1
    offsets_col = list(range(n_col))
    offsets_core = list(range(0, n_row, 2))
    gather_core = [0] + offsets_core[:0:-1]
    offsets_row = gather_core + [offset ^ 1 for offset in gather_core]
    tiles, token = masked(where, green, mask)

    own = probes.T
    held = [own] + [exchange(own, "row", offset) for offset in gather_core[1:]]
    held, token = lax.optimization_barrier((held, token))
    held = jnp.concatenate(held)
    blocks = [held, exchange(held, "row", 1)]

    totals, shares = [], []
    for chunk in range(chunks):
        *parts, ends = partial_sketch(where, tiles, blocks, token, offsets_row, offsets_col, chunk, chunks)
        totals.append(window_sums(parts, ends))
        shares.append(window_spread(totals[-1].astype(BF16), ends, n_col))

    earlier = []
    for chunk in range(chunks):
        earlier = partial_adjoint(where, tiles, shares[chunk], earlier, offsets_col, n_row, chunk, chunks)
    mine, others = earlier
    others = exchange(others, "row", 1)
    cuts = [slice(k * own_width, (k + 1) * own_width) for k in range(len(offsets_core))]
    pairs = [mine[cut] + others[cut] for cut in cuts]
    adjoint = pairs[0]
    for offset in offsets_core[1:2] + offsets_core[:1:-1]:
        adjoint = adjoint + exchange(pairs[offset // 2].astype(BF16), "row", offset).astype(F32)
    return jnp.concatenate(totals, axis=1).T, adjoint.T


def solution(mesh):
    in_specs = (P("row", "col"), P("row", "col"), P("col", "row"))
    out_specs = (P("row", "col"), P("col", "row"))
    return jax.shard_map(local, mesh=mesh, in_specs=in_specs, out_specs=out_specs, check_vma=False)
```

```python
import functools

import jax
import jax.numpy as jnp
from jax import lax
from jax.experimental import pallas as pl
from jax.experimental.pallas import tpu as pltpu
from jax.sharding import PartitionSpec as P

F32, BF16 = jnp.float32, jnp.bfloat16
VMEM_LIMIT = 28 * 2**20
STEP = 512
CHUNKS = 2


def exchange(value, axis, offset):
    size = lax.axis_size(axis)
    return lax.ppermute(value, axis, [(i, i ^ offset) for i in range(size)])


def at_end(where, size):
    return (where[1] == 0) | (where[1] == size - 1)


def after(value, earlier):
    return lax.optimization_barrier((value, earlier))[0]


def window_sums(terms, ends):
    size = len(terms)
    if size == 4:
        came = lax.ppermute(terms[2], "col", [(0, 1), (3, 2), (2, 0), (1, 3)])
        came = came.astype(F32)
        onward = terms[3] + jnp.where(ends > 0, 0.0, came)
        onward = onward.astype(BF16)
        far = exchange(onward, "col", 3).astype(F32)
        near = exchange(after(terms[1], onward), "col", 1).astype(F32)
        return terms[0] + near + far + jnp.where(ends > 0, came, 0.0)
    total = terms[0]
    for offset in range(1, size):
        total = total + exchange(terms[offset].astype(BF16), "col", offset).astype(F32)
    return total


def window_spread(lowered, ends, size):
    if size == 4:
        far = exchange(lowered, "col", 3)
        near = exchange(lowered, "col", 1)
        onward = jnp.where(ends > 0, lowered, far)
        return [lowered, near, lax.ppermute(onward, "col", [(0, 2), (3, 1), (1, 0), (2, 3)]), far]
    return [lowered] + [exchange(lowered, "col", offset) for offset in range(1, size)]


def mask_kernel(where, mask_hbm, green_ref, tiles, token, mask_ref, mask_sem, sems, *, block):
    rows, cols = tiles.shape
    token[...] = jnp.zeros(token.shape, token.dtype)
    levels = pltpu.make_async_copy(mask_hbm, mask_ref, mask_sem)
    levels.start()
    copies = []
    for step in range(rows // STEP):
        at = pl.ds(step * STEP, STEP)
        copies.append(pltpu.make_async_copy(green_ref.at[at], tiles.at[at], sems.at[step]))
        copies[-1].start()
    levels.wait()
    for step, copy in enumerate(copies):
        copy.wait()
        for i in range(step * STEP // block, (step + 1) * STEP // block):
            for j in range(cols // block):

                @pl.when(mask_ref[i, j] == 0)
                def _():
                    tiles[i * block : (i + 1) * block, j * block : (j + 1) * block] = jnp.zeros((block, block), BF16)


def masked(where, green, mask):
    rows, cols = green.shape
    return pl.pallas_call(
        functools.partial(mask_kernel, block=rows // mask.shape[0]),
        in_specs=[pl.BlockSpec(memory_space=pltpu.SMEM)] + [pl.BlockSpec(memory_space=pltpu.HBM)] * 2,
        out_specs=[pl.BlockSpec(memory_space=pltpu.VMEM)] * 2,
        out_shape=[pltpu.VMEM((rows, cols), BF16), jax.ShapeDtypeStruct((8, 128), F32)],
        scratch_shapes=[
            pltpu.SMEM(mask.shape, mask.dtype),
            pltpu.SemaphoreType.DMA,
            pltpu.SemaphoreType.DMA((rows // STEP,)),
        ],
        compiler_params=pltpu.CompilerParams(vmem_limit_bytes=VMEM_LIMIT),
        cost_estimate=pl.CostEstimate(flops=0, bytes_accessed=2 * rows * cols, transcendentals=0),
        name="masked_tiles",
    )(where, *(pltpu.with_memory_space_constraint(array, pltpu.HBM) for array in (mask, green)))


def sketch_kernel(where, tiles, token, *refs, base, offsets_row, offsets_col):
    blocks, outs, ends, probes = refs[: len(offsets_row)], refs[len(offsets_row) : -2], refs[-2], refs[-1]
    own = blocks[0].shape[0]
    ratio = len(offsets_row) // len(offsets_col)
    share = own * ratio
    ends[...] = jnp.full(ends.shape, at_end(where, len(offsets_col)).astype(F32))
    for offset, ref in zip(offsets_row, blocks):
        column = where[0] ^ offset
        start = (lax.div(column, ratio) ^ where[1]) * share + lax.rem(column, ratio) * own
        probes[pl.ds(pl.multiple_of(start, own), own), :] = ref[...]
    for step in range(ends.shape[1] // STEP):
        rows, at = slice(base + step * STEP, base + (step + 1) * STEP), slice(step * STEP, (step + 1) * STEP)
        term = lax.dot_general(probes[...], tiles[rows, :], (((1,), (1,)), ((), ())), preferred_element_type=F32)
        for k, out in enumerate(outs):
            out[:, at] = term[k * share : (k + 1) * share].astype(out.dtype)


def partial_sketch(where, tiles, blocks, token, offsets_row, offsets_col, chunk, chunks):
    rows, cols = tiles.shape
    rows //= chunks
    width = blocks[0].shape[0] * len(blocks)
    share = width // len(offsets_col)
    vmem = pl.BlockSpec(memory_space=pltpu.VMEM)
    exact = (0, offsets_col[-1])
    outs = [jax.ShapeDtypeStruct((share, rows), F32 if offset in exact else BF16) for offset in offsets_col]
    outs.append(jax.ShapeDtypeStruct((share, rows), F32))
    return pl.pallas_call(
        functools.partial(sketch_kernel, base=chunk * rows, offsets_row=offsets_row, offsets_col=offsets_col),
        in_specs=[pl.BlockSpec(memory_space=pltpu.SMEM)] + [vmem] * (2 + len(blocks)),
        out_specs=[vmem] * len(outs),
        out_shape=outs,
        scratch_shapes=[pltpu.VMEM((width, cols), BF16)],
        compiler_params=pltpu.CompilerParams(vmem_limit_bytes=VMEM_LIMIT),
        cost_estimate=pl.CostEstimate(
            flops=2 * width * cols * rows, bytes_accessed=2 * rows * cols, transcendentals=0
        ),
        name="partial_sketch",
    )(where, tiles, token, *blocks)


def adjoint_kernel(where, tiles, *refs, base, parts, offsets_col, devices):
    shares, earlier, outs, lowered = refs[: len(offsets_col)], refs[len(offsets_col) : -1 - parts], refs[-1 - parts : -1], refs[-1]
    share, rows = shares[0].shape
    ratio = devices // len(offsets_col)
    own = share // ratio
    for offset, ref in zip(offsets_col, shares):
        for n in range(ratio):
            apart = where[0] ^ ((where[1] ^ offset) * ratio + n)
            start = ((apart >> 1) + (apart & 1) * (devices // 2)) * own
            lowered[pl.ds(pl.multiple_of(start, own), own), :] = ref[n * own : (n + 1) * own, :]
    for step in range(tiles.shape[1] // STEP):
        at = slice(step * STEP, (step + 1) * STEP)
        term = jnp.dot(lowered[...], tiles[base : base + rows, at], preferred_element_type=F32)
        if earlier:
            term += earlier[0][:, at]
        height = outs[0].shape[0]
        for k, out in enumerate(outs):
            out[:, at] = term[k * height : (k + 1) * height]


def partial_adjoint(where, tiles, shares, earlier, offsets_col, devices, chunk, chunks):
    rows, cols = tiles.shape
    rows //= chunks
    width = shares[0].shape[0] * len(offsets_col)
    parts = 2 if chunk == chunks - 1 else 1
    vmem = pl.BlockSpec(memory_space=pltpu.VMEM)
    return pl.pallas_call(
        functools.partial(
            adjoint_kernel, base=chunk * rows, parts=parts, offsets_col=offsets_col, devices=devices
        ),
        in_specs=[pl.BlockSpec(memory_space=pltpu.SMEM)] + [vmem] * (1 + len(shares) + len(earlier)),
        out_specs=[vmem] * parts,
        out_shape=[jax.ShapeDtypeStruct((width // parts, cols), F32)] * parts,
        scratch_shapes=[pltpu.VMEM((width, rows), BF16)],
        compiler_params=pltpu.CompilerParams(vmem_limit_bytes=VMEM_LIMIT),
        cost_estimate=pl.CostEstimate(
            flops=0, bytes_accessed=0, transcendentals=0
        ),
        name="partial_adjoint",
    )(where, tiles, *shares, *earlier)


def local(green, mask, probes):
    n_row, n_col = lax.axis_size("row"), lax.axis_size("col")
    where = jnp.stack([lax.axis_index("row"), lax.axis_index("col")]).astype(jnp.int32)
    own_width = probes.shape[1]
    chunks = CHUNKS if green.shape[0] % (CHUNKS * STEP) == 0 else 1
    offsets_col = list(range(n_col))
    offsets_core = list(range(0, n_row, 2))
    gather_core = [0] + offsets_core[:0:-1]
    offsets_row = gather_core + [offset ^ 1 for offset in gather_core]
    tiles, token = masked(where, green, mask)

    own = probes.T
    held = [own] + [exchange(own, "row", offset) for offset in gather_core[1:]]
    twin = exchange(own, "row", 1)
    held, token = lax.optimization_barrier((held, token))
    blocks = held + [twin] + [exchange(block, "row", 1) for block in held[1:]]

    totals, shares = [], []
    for chunk in range(chunks):
        *parts, ends = partial_sketch(where, tiles, blocks, token, offsets_row, offsets_col, chunk, chunks)
        totals.append(window_sums(parts, ends))
        shares.append(window_spread(totals[-1].astype(BF16), ends, n_col))

    earlier = []
    for chunk in range(chunks):
        earlier = partial_adjoint(where, tiles, shares[chunk], earlier, offsets_col, n_row, chunk, chunks)
    mine, others = earlier
    others = exchange(others, "row", 1)
    cuts = [slice(k * own_width, (k + 1) * own_width) for k in range(len(offsets_core))]
    pairs = [mine[cut] + others[cut] for cut in cuts]
    adjoint = pairs[0]
    for offset in offsets_core[1:2] + offsets_core[:1:-1]:
        adjoint = adjoint + exchange(pairs[offset // 2].astype(BF16), "row", offset).astype(F32)
    return jnp.concatenate(totals, axis=1).T, adjoint.T


def solution(mesh):
    in_specs = (P("row", "col"), P("row", "col"), P("col", "row"))
    out_specs = (P("row", "col"), P("col", "row"))
    return jax.shard_map(local, mesh=mesh, in_specs=in_specs, out_specs=out_specs, check_vma=False)
```

```python
import functools

import jax
import jax.numpy as jnp
from jax import lax
from jax.experimental import pallas as pl
from jax.experimental.pallas import tpu as pltpu
from jax.sharding import PartitionSpec as P

F32, BF16 = jnp.float32, jnp.bfloat16
VMEM_LIMIT = 28 * 2**20
STEP = 512
CHUNKS = 2


def exchange(value, axis, offset):
    size = lax.axis_size(axis)
    return lax.ppermute(value, axis, [(i, i ^ offset) for i in range(size)])


def at_end(where, size):
    return (where[1] == 0) | (where[1] == size - 1)


def after(value, earlier):
    return lax.optimization_barrier((value, earlier))[0]


def window_sums(terms, ends):
    size = len(terms)
    if size == 4:
        came = lax.ppermute(terms[2], "col", [(0, 1), (3, 2), (2, 0), (1, 3)])
        came = came.astype(F32)
        onward = terms[3] + jnp.where(ends > 0, 0.0, came)
        onward = onward.astype(BF16)
        far = exchange(onward, "col", 3).astype(F32)
        near = exchange(after(terms[1], onward), "col", 1).astype(F32)
        return terms[0] + near + far + jnp.where(ends > 0, came, 0.0)
    total = terms[0]
    for offset in range(1, size):
        total = total + exchange(terms[offset].astype(BF16), "col", offset).astype(F32)
    return total


def window_spread(lowered, ends, size):
    if size == 4:
        far = exchange(lowered, "col", 3)
        near = exchange(lowered, "col", 1)
        onward = jnp.where(ends > 0, lowered, far)
        return [lowered, near, lax.ppermute(onward, "col", [(0, 2), (3, 1), (1, 0), (2, 3)]), far]
    return [lowered] + [exchange(lowered, "col", offset) for offset in range(1, size)]


def mask_kernel(where, mask_hbm, green_ref, tiles, token, mask_ref, mask_sem, sems, *, block):
    rows, cols = tiles.shape
    token[...] = jnp.zeros(token.shape, token.dtype)
    levels = pltpu.make_async_copy(mask_hbm, mask_ref, mask_sem)
    levels.start()
    copies = []
    for step in range(rows // STEP):
        at = pl.ds(step * STEP, STEP)
        copies.append(pltpu.make_async_copy(green_ref.at[at], tiles.at[at], sems.at[step]))
        copies[-1].start()
    levels.wait()
    for step, copy in enumerate(copies):
        copy.wait()
        for i in range(step * STEP // block, (step + 1) * STEP // block):
            for j in range(cols // block):

                @pl.when(mask_ref[i, j] == 0)
                def _():
                    tiles[i * block : (i + 1) * block, j * block : (j + 1) * block] = jnp.zeros((block, block), BF16)


def masked(where, green, mask):
    rows, cols = green.shape
    return pl.pallas_call(
        functools.partial(mask_kernel, block=rows // mask.shape[0]),
        in_specs=[pl.BlockSpec(memory_space=pltpu.SMEM)] + [pl.BlockSpec(memory_space=pltpu.HBM)] * 2,
        out_specs=[pl.BlockSpec(memory_space=pltpu.VMEM)] * 2,
        out_shape=[pltpu.VMEM((rows, cols), BF16), jax.ShapeDtypeStruct((8, 128), F32)],
        scratch_shapes=[
            pltpu.SMEM(mask.shape, mask.dtype),
            pltpu.SemaphoreType.DMA,
            pltpu.SemaphoreType.DMA((rows // STEP,)),
        ],
        compiler_params=pltpu.CompilerParams(vmem_limit_bytes=VMEM_LIMIT),
        cost_estimate=pl.CostEstimate(flops=0, bytes_accessed=2 * rows * cols, transcendentals=0),
        name="masked_tiles",
    )(where, *(pltpu.with_memory_space_constraint(array, pltpu.HBM) for array in (mask, green)))


def sketch_kernel(where, tiles, token, *refs, base, offsets_row, offsets_col):
    blocks, outs, ends, probes = refs[: len(offsets_row)], refs[len(offsets_row) : -2], refs[-2], refs[-1]
    own = blocks[0].shape[0]
    ratio = len(offsets_row) // len(offsets_col)
    share = own * ratio
    ends[...] = jnp.full(ends.shape, at_end(where, len(offsets_col)).astype(F32))
    for offset, ref in zip(offsets_row, blocks):
        column = where[0] ^ offset
        start = (lax.div(column, ratio) ^ where[1]) * share + lax.rem(column, ratio) * own
        probes[pl.ds(pl.multiple_of(start, own), own), :] = ref[...]
    for step in range(ends.shape[1] // STEP):
        rows, at = slice(base + step * STEP, base + (step + 1) * STEP), slice(step * STEP, (step + 1) * STEP)
        term = lax.dot_general(probes[...], tiles[rows, :], (((1,), (1,)), ((), ())), preferred_element_type=F32)
        for k, out in enumerate(outs):
            out[:, at] = term[k * share : (k + 1) * share].astype(out.dtype)


def partial_sketch(where, tiles, blocks, token, offsets_row, offsets_col, chunk, chunks):
    rows, cols = tiles.shape
    rows //= chunks
    width = blocks[0].shape[0] * len(blocks)
    share = width // len(offsets_col)
    vmem = pl.BlockSpec(memory_space=pltpu.VMEM)
    exact = (0, offsets_col[-1])
    outs = [jax.ShapeDtypeStruct((share, rows), F32 if offset in exact else BF16) for offset in offsets_col]
    outs.append(jax.ShapeDtypeStruct((share, rows), F32))
    return pl.pallas_call(
        functools.partial(sketch_kernel, base=chunk * rows, offsets_row=offsets_row, offsets_col=offsets_col),
        in_specs=[pl.BlockSpec(memory_space=pltpu.SMEM)] + [vmem] * (2 + len(blocks)),
        out_specs=[vmem] * len(outs),
        out_shape=outs,
        scratch_shapes=[pltpu.VMEM((width, cols), BF16)],
        compiler_params=pltpu.CompilerParams(vmem_limit_bytes=VMEM_LIMIT),
        cost_estimate=pl.CostEstimate(
            flops=2 * width * cols * rows, bytes_accessed=2 * rows * cols, transcendentals=0
        ),
        name="partial_sketch",
    )(where, tiles, token, *blocks)


def adjoint_kernel(where, tiles, *refs, base, parts, offsets_col, devices):
    shares, earlier, outs, lowered = refs[: len(offsets_col)], refs[len(offsets_col) : -1 - parts], refs[-1 - parts : -1], refs[-1]
    share, rows = shares[0].shape
    ratio = devices // len(offsets_col)
    own = share // ratio
    for offset, ref in zip(offsets_col, shares):
        for n in range(ratio):
            apart = where[0] ^ ((where[1] ^ offset) * ratio + n)
            start = ((apart >> 1) + (apart & 1) * (devices // 2)) * own
            lowered[pl.ds(pl.multiple_of(start, own), own), :] = ref[n * own : (n + 1) * own, :]
    for step in range(tiles.shape[1] // STEP):
        at = slice(step * STEP, (step + 1) * STEP)
        term = jnp.dot(lowered[...], tiles[base : base + rows, at], preferred_element_type=F32)
        if earlier:
            term += earlier[0][:, at]
        height = outs[0].shape[0]
        for k, out in enumerate(outs):
            out[:, at] = term[k * height : (k + 1) * height]


def partial_adjoint(where, tiles, shares, earlier, offsets_col, devices, chunk, chunks):
    rows, cols = tiles.shape
    rows //= chunks
    width = shares[0].shape[0] * len(offsets_col)
    parts = 4 if chunk == chunks - 1 else 1
    vmem = pl.BlockSpec(memory_space=pltpu.VMEM)
    return pl.pallas_call(
        functools.partial(
            adjoint_kernel, base=chunk * rows, parts=parts, offsets_col=offsets_col, devices=devices
        ),
        in_specs=[pl.BlockSpec(memory_space=pltpu.SMEM)] + [vmem] * (1 + len(shares) + len(earlier)),
        out_specs=[vmem] * parts,
        out_shape=[jax.ShapeDtypeStruct((width // parts, cols), F32)] * parts,
        scratch_shapes=[pltpu.VMEM((width, rows), BF16)],
        compiler_params=pltpu.CompilerParams(vmem_limit_bytes=VMEM_LIMIT),
        cost_estimate=pl.CostEstimate(
            flops=0, bytes_accessed=0, transcendentals=0
        ),
        name="partial_adjoint",
    )(where, tiles, *shares, *earlier)


def local(green, mask, probes):
    n_row, n_col = lax.axis_size("row"), lax.axis_size("col")
    where = jnp.stack([lax.axis_index("row"), lax.axis_index("col")]).astype(jnp.int32)
    own_width = probes.shape[1]
    chunks = CHUNKS if green.shape[0] % (CHUNKS * STEP) == 0 else 1
    offsets_col = list(range(n_col))
    offsets_core = list(range(0, n_row, 2))
    gather_core = [0] + offsets_core[:0:-1]
    offsets_row = gather_core + [offset ^ 1 for offset in gather_core]
    tiles, token = masked(where, green, mask)

    own = probes.T
    held = [own] + [exchange(own, "row", offset) for offset in gather_core[1:]]
    twin = exchange(own, "row", 1)
    held, token = lax.optimization_barrier((held, token))
    blocks = held + [twin] + [exchange(block, "row", 1) for block in held[1:]]

    totals, shares = [], []
    for chunk in range(chunks):
        *parts, ends = partial_sketch(where, tiles, blocks, token, offsets_row, offsets_col, chunk, chunks)
        totals.append(window_sums(parts, ends))
        shares.append(window_spread(totals[-1].astype(BF16), ends, n_col))

    earlier = []
    for chunk in range(chunks):
        earlier = partial_adjoint(where, tiles, shares[chunk], earlier, offsets_col, n_row, chunk, chunks)
    pairs = []
    for mine, others in (earlier[1::2], earlier[::2]):
        others = exchange(others, "row", 1)
        bands = [slice(at, at + own_width) for at in range(0, mine.shape[0], own_width)]
        pairs = [mine[band] + others[band] for band in bands] + pairs
    adjoint = pairs[0]
    for offset in offsets_core[1:]:
        adjoint = adjoint + exchange(pairs[offset // 2].astype(BF16), "row", offset).astype(F32)
    return jnp.concatenate(totals, axis=1).T, adjoint.T


def solution(mesh):
    in_specs = (P("row", "col"), P("row", "col"), P("col", "row"))
    out_specs = (P("row", "col"), P("col", "row"))
    return jax.shard_map(local, mesh=mesh, in_specs=in_specs, out_specs=out_specs, check_vma=False)
```

```python
import functools

import jax
import jax.numpy as jnp
from jax import lax
from jax.experimental import pallas as pl
from jax.experimental.pallas import tpu as pltpu
from jax.sharding import PartitionSpec as P

F32, BF16 = jnp.float32, jnp.bfloat16
VMEM_LIMIT = 28 * 2**20
STEP = 512
CHUNKS = 2


def exchange(value, axis, offset):
    size = lax.axis_size(axis)
    return lax.ppermute(value, axis, [(i, i ^ offset) for i in range(size)])


def at_end(where, size):
    return (where[1] == 0) | (where[1] == size - 1)


def after(value, earlier):
    return lax.optimization_barrier((value, earlier))[0]


def window_sums(terms, ends):
    size = len(terms)
    if size == 4:
        came = lax.ppermute(terms[2], "col", [(0, 1), (3, 2), (2, 0), (1, 3)])
        came = came.astype(F32)
        onward = terms[3] + jnp.where(ends > 0, 0.0, came)
        onward = onward.astype(BF16)
        far = exchange(onward, "col", 3).astype(F32)
        near = exchange(after(terms[1], onward), "col", 1).astype(F32)
        return terms[0] + near + far + jnp.where(ends > 0, came, 0.0)
    total = terms[0]
    for offset in range(1, size):
        total = total + exchange(terms[offset].astype(BF16), "col", offset).astype(F32)
    return total


def window_spread(lowered, ends, size):
    if size == 4:
        far = exchange(lowered, "col", 3)
        near = exchange(lowered, "col", 1)
        onward = jnp.where(ends > 0, lowered, far)
        return [lowered, near, lax.ppermute(onward, "col", [(0, 2), (3, 1), (1, 0), (2, 3)]), far]
    return [lowered] + [exchange(lowered, "col", offset) for offset in range(1, size)]


def mask_kernel(where, mask_hbm, green_ref, tiles, token, mask_ref, mask_sem, sems, *, block):
    rows, cols = tiles.shape
    token[...] = jnp.zeros(token.shape, token.dtype)
    levels = pltpu.make_async_copy(mask_hbm, mask_ref, mask_sem)
    levels.start()
    copies = []
    for step in range(rows // STEP):
        at = pl.ds(step * STEP, STEP)
        copies.append(pltpu.make_async_copy(green_ref.at[at], tiles.at[at], sems.at[step]))
        copies[-1].start()
    levels.wait()
    for step, copy in enumerate(copies):
        copy.wait()
        for i in range(step * STEP // block, (step + 1) * STEP // block):
            for j in range(cols // block):

                @pl.when(mask_ref[i, j] == 0)
                def _():
                    tiles[i * block : (i + 1) * block, j * block : (j + 1) * block] = jnp.zeros((block, block), BF16)


def masked(where, green, mask):
    rows, cols = green.shape
    return pl.pallas_call(
        functools.partial(mask_kernel, block=rows // mask.shape[0]),
        in_specs=[pl.BlockSpec(memory_space=pltpu.SMEM)] + [pl.BlockSpec(memory_space=pltpu.HBM)] * 2,
        out_specs=[pl.BlockSpec(memory_space=pltpu.VMEM)] * 2,
        out_shape=[pltpu.VMEM((rows, cols), BF16), jax.ShapeDtypeStruct((8, 128), F32)],
        scratch_shapes=[
            pltpu.SMEM(mask.shape, mask.dtype),
            pltpu.SemaphoreType.DMA,
            pltpu.SemaphoreType.DMA((rows // STEP,)),
        ],
        compiler_params=pltpu.CompilerParams(vmem_limit_bytes=VMEM_LIMIT),
        cost_estimate=pl.CostEstimate(flops=0, bytes_accessed=2 * rows * cols, transcendentals=0),
        name="masked_tiles",
    )(where, *(pltpu.with_memory_space_constraint(array, pltpu.HBM) for array in (mask, green)))


def sketch_kernel(where, tiles, token, *refs, base, offsets_row, offsets_col):
    blocks, outs, ends, probes = refs[: len(offsets_row)], refs[len(offsets_row) : -2], refs[-2], refs[-1]
    own = blocks[0].shape[0]
    ratio = len(offsets_row) // len(offsets_col)
    share = own * ratio
    ends[...] = jnp.full(ends.shape, at_end(where, len(offsets_col)).astype(F32))
    for offset, ref in zip(offsets_row, blocks):
        column = where[0] ^ offset
        start = (lax.div(column, ratio) ^ where[1]) * share + lax.rem(column, ratio) * own
        probes[pl.ds(pl.multiple_of(start, own), own), :] = ref[...]
    for step in range(ends.shape[1] // STEP):
        rows, at = slice(base + step * STEP, base + (step + 1) * STEP), slice(step * STEP, (step + 1) * STEP)
        term = lax.dot_general(probes[...], tiles[rows, :], (((1,), (1,)), ((), ())), preferred_element_type=F32)
        for k, out in enumerate(outs):
            out[:, at] = term[k * share : (k + 1) * share].astype(out.dtype)


def partial_sketch(where, tiles, blocks, token, offsets_row, offsets_col, chunk, chunks):
    rows, cols = tiles.shape
    rows //= chunks
    width = blocks[0].shape[0] * len(blocks)
    share = width // len(offsets_col)
    vmem = pl.BlockSpec(memory_space=pltpu.VMEM)
    exact = (0, offsets_col[-1])
    outs = [jax.ShapeDtypeStruct((share, rows), F32 if offset in exact else BF16) for offset in offsets_col]
    outs.append(jax.ShapeDtypeStruct((share, rows), F32))
    return pl.pallas_call(
        functools.partial(sketch_kernel, base=chunk * rows, offsets_row=offsets_row, offsets_col=offsets_col),
        in_specs=[pl.BlockSpec(memory_space=pltpu.SMEM)] + [vmem] * (2 + len(blocks)),
        out_specs=[vmem] * len(outs),
        out_shape=outs,
        scratch_shapes=[pltpu.VMEM((width, cols), BF16)],
        compiler_params=pltpu.CompilerParams(vmem_limit_bytes=VMEM_LIMIT),
        cost_estimate=pl.CostEstimate(
            flops=2 * width * cols * rows, bytes_accessed=2 * rows * cols, transcendentals=0
        ),
        name="partial_sketch",
    )(where, tiles, token, *blocks)


def adjoint_kernel(where, tiles, *refs, base, span, parts, offsets_col, devices):
    shares, earlier, outs, lowered = refs[: len(offsets_col)], refs[len(offsets_col) : -1 - parts], refs[-1 - parts : -1], refs[-1]
    share, rows = shares[0].shape
    ratio = devices // len(offsets_col)
    own = share // ratio
    for offset, ref in zip(offsets_col, shares):
        for n in range(ratio):
            apart = where[0] ^ ((where[1] ^ offset) * ratio + n)
            start = ((apart >> 1) + (apart & 1) * (devices // 2)) * own
            lowered[pl.ds(pl.multiple_of(start, own), own), :] = ref[n * own : (n + 1) * own, :]
    for step in range(tiles.shape[1] // STEP):
        at = slice(step * STEP, (step + 1) * STEP)
        term = jnp.dot(lowered[span, :], tiles[base : base + rows, at], preferred_element_type=F32)
        if earlier:
            term += earlier[0][span, at]
        height = outs[0].shape[0]
        for k, out in enumerate(outs):
            out[:, at] = term[k * height : (k + 1) * height]


def partial_adjoint(where, tiles, shares, earlier, span, parts, offsets_col, devices, base):
    cols = tiles.shape[1]
    share, rows = shares[0].shape
    width = share * len(offsets_col)
    height = (span.stop - span.start) // parts
    vmem = pl.BlockSpec(memory_space=pltpu.VMEM)
    return pl.pallas_call(
        functools.partial(
            adjoint_kernel, base=base, span=span, parts=parts, offsets_col=offsets_col, devices=devices
        ),
        in_specs=[pl.BlockSpec(memory_space=pltpu.SMEM)] + [vmem] * (1 + len(shares) + len(earlier)),
        out_specs=[vmem] * parts,
        out_shape=[jax.ShapeDtypeStruct((height, cols), F32)] * parts,
        scratch_shapes=[pltpu.VMEM((width, rows), BF16)],
        compiler_params=pltpu.CompilerParams(vmem_limit_bytes=VMEM_LIMIT),
        cost_estimate=pl.CostEstimate(
            flops=0, bytes_accessed=0, transcendentals=0
        ),
        name="partial_adjoint",
    )(where, tiles, *shares, *earlier)


def local(green, mask, probes):
    n_row, n_col = lax.axis_size("row"), lax.axis_size("col")
    where = jnp.stack([lax.axis_index("row"), lax.axis_index("col")]).astype(jnp.int32)
    own_width = probes.shape[1]
    chunks = CHUNKS if green.shape[0] % (CHUNKS * STEP) == 0 else 1
    offsets_col = list(range(n_col))
    offsets_core = list(range(0, n_row, 2))
    gather_core = offsets_core
    offsets_row = gather_core + [offset ^ 1 for offset in gather_core]
    tiles, token = masked(where, green, mask)

    own = probes.T
    held = [own] + [exchange(own, "row", offset) for offset in gather_core[1:]]
    twin = exchange(own, "row", 1)
    held, token = lax.optimization_barrier((held, token))
    blocks = held + [twin] + [exchange(block, "row", 1) for block in held[1:]]

    totals, shares = [], []
    for chunk in range(chunks):
        *parts, ends = partial_sketch(where, tiles, blocks, token, offsets_row, offsets_col, chunk, chunks)
        totals.append(window_sums(parts, ends))
        shares.append(window_spread(totals[-1].astype(BF16), ends, n_col))

    earlier = []
    length = green.shape[0] // chunks
    width = own_width * n_row
    for chunk in range(chunks - 1):
        earlier = partial_adjoint(
            where, tiles, shares[chunk], earlier, slice(0, width), 1, offsets_col, n_row, chunk * length
        )
    theirs, ours = (
        partial_adjoint(where, tiles, shares[-1], earlier, span, 2, offsets_col, n_row, (chunks - 1) * length)
        for span in (slice(width // 2, width), slice(0, width // 2))
    )
    pairs = []
    for mine, others in zip(ours[::-1], theirs[::-1]):
        others = exchange(others, "row", 1)
        bands = [slice(at, at + own_width) for at in range(0, mine.shape[0], own_width)]
        pairs = [mine[band] + others[band] for band in bands] + pairs
    adjoint = pairs[0]
    for offset in offsets_core[1:2] + offsets_core[:1:-1]:
        adjoint = adjoint + exchange(pairs[offset // 2].astype(BF16), "row", offset).astype(F32)
    return jnp.concatenate(totals, axis=1).T, adjoint.T


def solution(mesh):
    in_specs = (P("row", "col"), P("row", "col"), P("col", "row"))
    out_specs = (P("row", "col"), P("col", "row"))
    return jax.shard_map(local, mesh=mesh, in_specs=in_specs, out_specs=out_specs, check_vma=False)
```

```python
import functools

import jax
import jax.numpy as jnp
from jax import lax
from jax.experimental import pallas as pl
from jax.experimental.pallas import tpu as pltpu
from jax.sharding import PartitionSpec as P

F32, BF16 = jnp.float32, jnp.bfloat16
VMEM_LIMIT = 28 * 2**20
STEP = 512


def exchange(value, axis, offset):
    size = lax.axis_size(axis)
    return lax.ppermute(value, axis, [(i, i ^ offset) for i in range(size)])


def at_end(where, size):
    return (where[1] == 0) | (where[1] == size - 1)


def after(value, earlier):
    return lax.optimization_barrier((value, earlier))[0]


def window_sums(terms, ends, earlier):
    size = len(terms)
    came = ends
    if size == 4:
        came = lax.ppermute(terms[2], "col", [(0, 1), (3, 2), (2, 0), (1, 3)])
        extra = came.astype(F32)
        onward = terms[3] + jnp.where(ends > 0, 0.0, extra)
        onward = onward.astype(BF16)
        far = exchange(onward, "col", 3).astype(F32)
        near = exchange(after(terms[1], onward), "col", 1).astype(F32)
        return after(terms[0], earlier) + near + far + jnp.where(ends > 0, extra, 0.0), came
    total = terms[0]
    for offset in range(1, size):
        total = total + exchange(terms[offset].astype(BF16), "col", offset).astype(F32)
    return total, came


def window_spread(lowered, ends, size):
    if size == 4:
        far = exchange(lowered, "col", 3)
        near = exchange(lowered, "col", 1)
        onward = jnp.where(ends > 0, lowered, far)
        return [lowered, near, lax.ppermute(onward, "col", [(0, 2), (3, 1), (1, 0), (2, 3)]), far]
    return [lowered] + [exchange(lowered, "col", offset) for offset in range(1, size)]


def mask_kernel(where, mask_hbm, green_ref, tiles, token, mask_ref, mask_sem, sems, *, block):
    rows, cols = tiles.shape
    token[...] = jnp.zeros(token.shape, token.dtype)
    levels = pltpu.make_async_copy(mask_hbm, mask_ref, mask_sem)
    levels.start()
    copies = []
    for step in range(rows // STEP):
        at = pl.ds(step * STEP, STEP)
        copies.append(pltpu.make_async_copy(green_ref.at[at], tiles.at[at], sems.at[step]))
        copies[-1].start()
    levels.wait()
    for step, copy in enumerate(copies):
        copy.wait()
        for i in range(step * STEP // block, (step + 1) * STEP // block):
            for j in range(cols // block):

                @pl.when(mask_ref[i, j] == 0)
                def _():
                    tiles[i * block : (i + 1) * block, j * block : (j + 1) * block] = jnp.zeros((block, block), BF16)


def masked(where, green, mask):
    rows, cols = green.shape
    return pl.pallas_call(
        functools.partial(mask_kernel, block=rows // mask.shape[0]),
        in_specs=[pl.BlockSpec(memory_space=pltpu.SMEM)] + [pl.BlockSpec(memory_space=pltpu.HBM)] * 2,
        out_specs=[pl.BlockSpec(memory_space=pltpu.VMEM)] * 2,
        out_shape=[pltpu.VMEM((rows, cols), BF16), jax.ShapeDtypeStruct((8, 128), F32)],
        scratch_shapes=[
            pltpu.SMEM(mask.shape, mask.dtype),
            pltpu.SemaphoreType.DMA,
            pltpu.SemaphoreType.DMA((rows // STEP,)),
        ],
        compiler_params=pltpu.CompilerParams(vmem_limit_bytes=VMEM_LIMIT),
        cost_estimate=pl.CostEstimate(flops=0, bytes_accessed=2 * rows * cols, transcendentals=0),
        name="masked_tiles",
    )(where, *(pltpu.with_memory_space_constraint(array, pltpu.HBM) for array in (mask, green)))


def sketch_kernel(where, tiles, token, *refs, base, offsets_row, offsets_col):
    blocks, outs, ends, probes = refs[: len(offsets_row)], refs[len(offsets_row) : -2], refs[-2], refs[-1]
    own = blocks[0].shape[0]
    ratio = len(offsets_row) // len(offsets_col)
    share = own * ratio
    ends[...] = jnp.full(ends.shape, at_end(where, len(offsets_col)).astype(F32))
    for offset, ref in zip(offsets_row, blocks):
        column = where[0] ^ offset
        start = (lax.div(column, ratio) ^ where[1]) * share + lax.rem(column, ratio) * own
        probes[pl.ds(pl.multiple_of(start, own), own), :] = ref[...]
    for step in range(ends.shape[1] // STEP):
        rows, at = slice(base + step * STEP, base + (step + 1) * STEP), slice(step * STEP, (step + 1) * STEP)
        term = lax.dot_general(probes[...], tiles[rows, :], (((1,), (1,)), ((), ())), preferred_element_type=F32)
        for k, out in enumerate(outs):
            out[:, at] = term[k * share : (k + 1) * share].astype(out.dtype)


def partial_sketch(where, tiles, blocks, token, offsets_row, offsets_col, base, rows):
    cols = tiles.shape[1]
    width = blocks[0].shape[0] * len(blocks)
    share = width // len(offsets_col)
    vmem = pl.BlockSpec(memory_space=pltpu.VMEM)
    exact = (0, offsets_col[-1])
    outs = [jax.ShapeDtypeStruct((share, rows), F32 if offset in exact else BF16) for offset in offsets_col]
    outs.append(jax.ShapeDtypeStruct((share, rows), F32))
    return pl.pallas_call(
        functools.partial(sketch_kernel, base=base, offsets_row=offsets_row, offsets_col=offsets_col),
        in_specs=[pl.BlockSpec(memory_space=pltpu.SMEM)] + [vmem] * (2 + len(blocks)),
        out_specs=[vmem] * len(outs),
        out_shape=outs,
        scratch_shapes=[pltpu.VMEM((width, cols), BF16)],
        compiler_params=pltpu.CompilerParams(vmem_limit_bytes=VMEM_LIMIT),
        cost_estimate=pl.CostEstimate(
            flops=2 * width * cols * rows, bytes_accessed=2 * rows * cols, transcendentals=0
        ),
        name="partial_sketch",
    )(where, tiles, token, *blocks)


def adjoint_kernel(where, tiles, *refs, base, parts, offsets_col, devices):
    shares, earlier, outs, lowered = refs[: len(offsets_col)], refs[len(offsets_col) : -1 - parts], refs[-1 - parts : -1], refs[-1]
    share, rows = shares[0].shape
    ratio = devices // len(offsets_col)
    own = share // ratio
    for offset, ref in zip(offsets_col, shares):
        for n in range(ratio):
            apart = where[0] ^ ((where[1] ^ offset) * ratio + n)
            start = ((apart >> 1) + (apart & 1) * (devices // 2)) * own
            lowered[pl.ds(pl.multiple_of(start, own), own), :] = ref[n * own : (n + 1) * own, :]
    for step in range(tiles.shape[1] // STEP):
        at = slice(step * STEP, (step + 1) * STEP)
        term = jnp.dot(lowered[...], tiles[base : base + rows, at], preferred_element_type=F32)
        if earlier:
            term += earlier[0][:, at]
        height = outs[0].shape[0]
        for k, out in enumerate(outs):
            out[:, at] = term[k * height : (k + 1) * height]


def partial_adjoint(where, tiles, shares, earlier, parts, offsets_col, devices, base):
    cols = tiles.shape[1]
    share, rows = shares[0].shape
    width = share * len(offsets_col)
    vmem = pl.BlockSpec(memory_space=pltpu.VMEM)
    return pl.pallas_call(
        functools.partial(
            adjoint_kernel, base=base, parts=parts, offsets_col=offsets_col, devices=devices
        ),
        in_specs=[pl.BlockSpec(memory_space=pltpu.SMEM)] + [vmem] * (1 + len(shares) + len(earlier)),
        out_specs=[vmem] * parts,
        out_shape=[jax.ShapeDtypeStruct((width // parts, cols), F32)] * parts,
        scratch_shapes=[pltpu.VMEM((width, rows), BF16)],
        compiler_params=pltpu.CompilerParams(vmem_limit_bytes=VMEM_LIMIT),
        cost_estimate=pl.CostEstimate(
            flops=0, bytes_accessed=0, transcendentals=0
        ),
        name="partial_adjoint",
    )(where, tiles, *shares, *earlier)


def chunk_cuts(rows):
    quarter = rows // 4
    return [(0, quarter), (quarter, 2 * quarter), (3 * quarter, quarter)]


def local(green, mask, probes):
    n_row, n_col = lax.axis_size("row"), lax.axis_size("col")
    where = jnp.stack([lax.axis_index("row"), lax.axis_index("col")]).astype(jnp.int32)
    own_width = probes.shape[1]
    cuts = chunk_cuts(green.shape[0])
    offsets_col = list(range(n_col))
    offsets_core = list(range(0, n_row, 2))
    gather_core = [0] + offsets_core[:0:-1]
    offsets_row = gather_core + [offset ^ 1 for offset in gather_core]
    tiles, token = masked(where, green, mask)

    own = probes.T
    held = [own] + [exchange(own, "row", offset) for offset in gather_core[1:]]
    twin = exchange(own, "row", 1)
    held, token = lax.optimization_barrier((held, token))
    blocks = held + [twin] + [exchange(block, "row", 1) for block in held[1:]]

    totals, shares, firsts = [], [], []
    earlier = token
    for base, rows in cuts:
        *parts, ends = partial_sketch(where, tiles, blocks, token, offsets_row, offsets_col, base, rows)
        total, came = window_sums(parts, ends, earlier)
        token = after(ends, firsts[0]) if firsts else ends
        firsts.append(came)
        totals.append(total)
        shares.append(window_spread(totals[-1].astype(BF16), ends, n_col))
        earlier = shares[-1][-1 if len(shares) == 1 else 0]

    earlier = []
    for chunk, (base, rows) in enumerate(cuts):
        parts = 4 if chunk == len(cuts) - 1 else 1
        earlier = partial_adjoint(where, tiles, shares[chunk], earlier, parts, offsets_col, n_row, base)
    pairs = []
    for mine, others in (earlier[1::2], earlier[::2]):
        others = exchange(others, "row", 1)
        bands = [slice(at, at + own_width) for at in range(0, mine.shape[0], own_width)]
        pairs = [mine[band] + others[band] for band in bands] + pairs
    adjoint = pairs[0]
    for offset in offsets_core[1:]:
        adjoint = adjoint + exchange(pairs[offset // 2].astype(BF16), "row", offset).astype(F32)
    return jnp.concatenate(totals, axis=1).T, adjoint.T


def solution(mesh):
    in_specs = (P("row", "col"), P("row", "col"), P("col", "row"))
    out_specs = (P("row", "col"), P("col", "row"))
    return jax.shard_map(local, mesh=mesh, in_specs=in_specs, out_specs=out_specs, check_vma=False)
```

```python
import functools

import jax
import jax.numpy as jnp
from jax import lax
from jax.experimental import pallas as pl
from jax.experimental.pallas import tpu as pltpu
from jax.sharding import PartitionSpec as P

F32, BF16 = jnp.float32, jnp.bfloat16
VMEM_LIMIT = 28 * 2**20
STEP = 512
CHUNKS = 2


def exchange(value, axis, offset):
    size = lax.axis_size(axis)
    return lax.ppermute(value, axis, [(i, i ^ offset) for i in range(size)])


def at_end(size):
    place = lax.axis_index("col")
    return (place == 0) | (place == size - 1)


def after(value, earlier):
    return lax.optimization_barrier((value, earlier))[0]


def window_sums(terms, ends):
    size = len(terms)
    if size == 4:
        came = lax.ppermute(terms[2], "col", [(0, 1), (3, 2), (2, 0), (1, 3)])
        came = came.astype(F32)
        onward = terms[3] + jnp.where(ends > 0, 0.0, came)
        onward = onward.astype(BF16)
        far = exchange(onward, "col", 3).astype(F32)
        near = exchange(after(terms[1], onward), "col", 1).astype(F32)
        return terms[0] + near + far + jnp.where(ends > 0, came, 0.0)
    total = terms[0]
    for offset in range(1, size):
        total = total + exchange(terms[offset].astype(BF16), "col", offset).astype(F32)
    return total


def window_spread(lowered, ends, size):
    if size == 4:
        far = exchange(lowered, "col", 3)
        near = exchange(lowered, "col", 1)
        onward = jnp.where(ends > 0, lowered, far)
        return [lowered, near, lax.ppermute(onward, "col", [(0, 2), (3, 1), (1, 0), (2, 3)]), far]
    return [lowered] + [exchange(lowered, "col", offset) for offset in range(1, size)]


def mask_kernel(mask_hbm, green_ref, tiles, token, mask_ref, mask_sem, sems, *, block):
    rows, cols = tiles.shape
    token[...] = jnp.zeros(token.shape, token.dtype)
    levels = pltpu.make_async_copy(mask_hbm, mask_ref, mask_sem)
    levels.start()
    copies = []
    for step in range(rows // STEP):
        at = pl.ds(step * STEP, STEP)
        copies.append(pltpu.make_async_copy(green_ref.at[at], tiles.at[at], sems.at[step]))
        copies[-1].start()
    levels.wait()
    for step, copy in enumerate(copies):
        copy.wait()
        for i in range(step * STEP // block, (step + 1) * STEP // block):
            for j in range(cols // block):

                @pl.when(mask_ref[i, j] == 0)
                def _():
                    tiles[i * block : (i + 1) * block, j * block : (j + 1) * block] = jnp.zeros((block, block), BF16)


def masked(green, mask):
    rows, cols = green.shape
    return pl.pallas_call(
        functools.partial(mask_kernel, block=rows // mask.shape[0]),
        in_specs=[pl.BlockSpec(memory_space=pltpu.HBM)] * 2,
        out_specs=[pl.BlockSpec(memory_space=pltpu.VMEM)] * 2,
        out_shape=[pltpu.VMEM((rows, cols), BF16), jax.ShapeDtypeStruct((8, 128), F32)],
        scratch_shapes=[
            pltpu.SMEM(mask.shape, mask.dtype),
            pltpu.SemaphoreType.DMA,
            pltpu.SemaphoreType.DMA((rows // STEP,)),
        ],
        compiler_params=pltpu.CompilerParams(vmem_limit_bytes=VMEM_LIMIT),
        cost_estimate=pl.CostEstimate(flops=0, bytes_accessed=2 * rows * cols, transcendentals=0),
        name="masked_tiles",
    )(*(pltpu.with_memory_space_constraint(array, pltpu.HBM) for array in (mask, green)))


def sketch_kernel(tiles, token, *refs, base, offsets_row, offsets_col):
    blocks, outs, ends, probes = refs[: len(offsets_row)], refs[len(offsets_row) : -2], refs[-2], refs[-1]
    own = blocks[0].shape[0]
    ratio = len(offsets_row) // len(offsets_col)
    share = own * ratio
    ends[...] = jnp.full(ends.shape, at_end(len(offsets_col)).astype(F32))
    row, col = lax.axis_index("row"), lax.axis_index("col")
    for offset, ref in zip(offsets_row, blocks):
        column = row ^ offset
        start = (lax.div(column, ratio) ^ col) * share + lax.rem(column, ratio) * own
        probes[pl.ds(pl.multiple_of(start, own), own), :] = ref[...]
    for step in range(ends.shape[1] // STEP):
        rows, at = slice(base + step * STEP, base + (step + 1) * STEP), slice(step * STEP, (step + 1) * STEP)
        term = lax.dot_general(probes[...], tiles[rows, :], (((1,), (1,)), ((), ())), preferred_element_type=F32)
        for k, out in enumerate(outs):
            out[:, at] = term[k * share : (k + 1) * share].astype(out.dtype)


def partial_sketch(tiles, blocks, token, offsets_row, offsets_col, chunk, chunks):
    rows, cols = tiles.shape
    rows //= chunks
    width = blocks[0].shape[0] * len(blocks)
    share = width // len(offsets_col)
    vmem = pl.BlockSpec(memory_space=pltpu.VMEM)
    exact = (0, offsets_col[-1])
    outs = [jax.ShapeDtypeStruct((share, rows), F32 if offset in exact else BF16) for offset in offsets_col]
    outs.append(jax.ShapeDtypeStruct((share, rows), F32))
    return pl.pallas_call(
        functools.partial(sketch_kernel, base=chunk * rows, offsets_row=offsets_row, offsets_col=offsets_col),
        in_specs=[vmem] * (2 + len(blocks)),
        out_specs=[vmem] * len(outs),
        out_shape=outs,
        scratch_shapes=[pltpu.VMEM((width, cols), BF16)],
        compiler_params=pltpu.CompilerParams(vmem_limit_bytes=VMEM_LIMIT),
        cost_estimate=pl.CostEstimate(
            flops=2 * width * cols * rows, bytes_accessed=2 * rows * cols, transcendentals=0
        ),
        name="partial_sketch",
    )(tiles, token, *blocks)


def adjoint_kernel(tiles, *refs, base, parts, offsets_col, devices):
    shares, earlier, outs, lowered = refs[: len(offsets_col)], refs[len(offsets_col) : -1 - parts], refs[-1 - parts : -1], refs[-1]
    share, rows = shares[0].shape
    ratio = devices // len(offsets_col)
    own = share // ratio
    row, col = lax.axis_index("row"), lax.axis_index("col")
    for offset, ref in zip(offsets_col, shares):
        for n in range(ratio):
            apart = row ^ ((col ^ offset) * ratio + n)
            start = ((apart >> 1) + (apart & 1) * (devices // 2)) * own
            lowered[pl.ds(pl.multiple_of(start, own), own), :] = ref[n * own : (n + 1) * own, :]
    for step in range(tiles.shape[1] // STEP):
        at = slice(step * STEP, (step + 1) * STEP)
        term = jnp.dot(lowered[...], tiles[base : base + rows, at], preferred_element_type=F32)
        if earlier:
            term += earlier[0][:, at]
        height = outs[0].shape[0]
        for k, out in enumerate(outs):
            out[:, at] = term[k * height : (k + 1) * height]


def partial_adjoint(tiles, shares, earlier, offsets_col, devices, chunk, chunks):
    rows, cols = tiles.shape
    rows //= chunks
    width = shares[0].shape[0] * len(offsets_col)
    parts = 4 if chunk == chunks - 1 else 1
    vmem = pl.BlockSpec(memory_space=pltpu.VMEM)
    return pl.pallas_call(
        functools.partial(
            adjoint_kernel, base=chunk * rows, parts=parts, offsets_col=offsets_col, devices=devices
        ),
        in_specs=[vmem] * (1 + len(shares) + len(earlier)),
        out_specs=[vmem] * parts,
        out_shape=[jax.ShapeDtypeStruct((width // parts, cols), F32)] * parts,
        scratch_shapes=[pltpu.VMEM((width, rows), BF16)],
        compiler_params=pltpu.CompilerParams(vmem_limit_bytes=VMEM_LIMIT),
        cost_estimate=pl.CostEstimate(
            flops=0, bytes_accessed=0, transcendentals=0
        ),
        name="partial_adjoint",
    )(tiles, *shares, *earlier)


def local(green, mask, probes):
    n_row, n_col = lax.axis_size("row"), lax.axis_size("col")
    own_width = probes.shape[1]
    chunks = CHUNKS if green.shape[0] % (CHUNKS * STEP) == 0 else 1
    offsets_col = list(range(n_col))
    offsets_core = list(range(0, n_row, 2))
    gather_core = [0] + offsets_core[:0:-1]
    offsets_row = gather_core + [offset ^ 1 for offset in gather_core]
    tiles, token = masked(green, mask)

    own = probes.T
    held = [own] + [exchange(own, "row", offset) for offset in gather_core[1:]]
    twin = exchange(own, "row", 1)
    held, token = lax.optimization_barrier((held, token))
    blocks = held + [twin] + [exchange(block, "row", 1) for block in held[1:]]

    totals, shares = [], []
    for chunk in range(chunks):
        *parts, ends = partial_sketch(tiles, blocks, token, offsets_row, offsets_col, chunk, chunks)
        totals.append(window_sums(parts, ends))
        shares.append(window_spread(totals[-1].astype(BF16), ends, n_col))

    earlier = []
    for chunk in range(chunks):
        earlier = partial_adjoint(tiles, shares[chunk], earlier, offsets_col, n_row, chunk, chunks)
    pairs = []
    for mine, others in (earlier[1::2], earlier[::2]):
        others = exchange(others, "row", 1)
        bands = [slice(at, at + own_width) for at in range(0, mine.shape[0], own_width)]
        pairs = [mine[band] + others[band] for band in bands] + pairs
    adjoint = pairs[0]
    for offset in offsets_core[1:]:
        adjoint = adjoint + exchange(pairs[offset // 2].astype(BF16), "row", offset).astype(F32)
    return jnp.concatenate(totals, axis=1).T, adjoint.T


def solution(mesh):
    in_specs = (P("row", "col"), P("row", "col"), P("col", "row"))
    out_specs = (P("row", "col"), P("col", "row"))
    return jax.shard_map(local, mesh=mesh, in_specs=in_specs, out_specs=out_specs, check_vma=False)
```

```python
import functools

import jax
import jax.numpy as jnp
from jax import lax
from jax.experimental import pallas as pl
from jax.experimental.pallas import tpu as pltpu
from jax.sharding import PartitionSpec as P

F32, BF16 = jnp.float32, jnp.bfloat16
VMEM_LIMIT = 28 * 2**20
STEP = 512
CHUNKS = 2


def exchange(value, axis, offset):
    size = lax.axis_size(axis)
    return lax.ppermute(value, axis, [(i, i ^ offset) for i in range(size)])


def at_end(size):
    place = lax.axis_index("col")
    return (place == 0) | (place == size - 1)


def after(value, earlier):
    return lax.optimization_barrier((value, earlier))[0]


def window_sums(terms, ends):
    size = len(terms)
    if size == 4:
        came = lax.ppermute(terms[2], "col", [(0, 1), (3, 2), (2, 0), (1, 3)])
        came = came.astype(F32)
        onward = terms[3] + jnp.where(ends > 0, 0.0, came)
        onward = onward.astype(BF16)
        far = exchange(onward, "col", 3).astype(F32)
        near = exchange(after(terms[1], onward), "col", 1).astype(F32)
        return terms[0] + near + far + jnp.where(ends > 0, came, 0.0)
    total = terms[0]
    for offset in range(1, size):
        total = total + exchange(terms[offset].astype(BF16), "col", offset).astype(F32)
    return total


def window_spread(lowered, ends, size):
    if size == 4:
        far = exchange(lowered, "col", 3)
        near = exchange(lowered, "col", 1)
        onward = jnp.where(ends > 0, lowered, far)
        return [lowered, near, lax.ppermute(onward, "col", [(0, 2), (3, 1), (1, 0), (2, 3)]), far]
    return [lowered] + [exchange(lowered, "col", offset) for offset in range(1, size)]


def mask_kernel(mask_hbm, green_ref, tiles, token, mask_ref, mask_sem, sems, *, block):
    rows, cols = tiles.shape
    token[...] = jnp.zeros(token.shape, token.dtype)
    levels = pltpu.make_async_copy(mask_hbm, mask_ref, mask_sem)
    levels.start()
    copies = []
    for step in range(rows // STEP):
        at = pl.ds(step * STEP, STEP)
        copies.append(pltpu.make_async_copy(green_ref.at[at], tiles.at[at], sems.at[step]))
        copies[-1].start()
    levels.wait()
    for step, copy in enumerate(copies):
        copy.wait()
        for i in range(step * STEP // block, (step + 1) * STEP // block):
            for j in range(cols // block):

                @pl.when(mask_ref[i, j] == 0)
                def _():
                    tiles[i * block : (i + 1) * block, j * block : (j + 1) * block] = jnp.zeros((block, block), BF16)


def masked(green, mask):
    rows, cols = green.shape
    return pl.pallas_call(
        functools.partial(mask_kernel, block=rows // mask.shape[0]),
        in_specs=[pl.BlockSpec(memory_space=pltpu.HBM)] * 2,
        out_specs=[pl.BlockSpec(memory_space=pltpu.VMEM)] * 2,
        out_shape=[pltpu.VMEM((rows, cols), BF16), jax.ShapeDtypeStruct((8, 128), F32)],
        scratch_shapes=[
            pltpu.SMEM(mask.shape, mask.dtype),
            pltpu.SemaphoreType.DMA,
            pltpu.SemaphoreType.DMA((rows // STEP,)),
        ],
        compiler_params=pltpu.CompilerParams(vmem_limit_bytes=VMEM_LIMIT),
        cost_estimate=pl.CostEstimate(flops=0, bytes_accessed=2 * rows * cols, transcendentals=0),
        name="masked_tiles",
    )(*(pltpu.with_memory_space_constraint(array, pltpu.HBM) for array in (mask, green)))


def sketch_kernel(tiles, token, *refs, base, offsets_row, offsets_col):
    count = len(refs) - 2 - len(offsets_col)
    blocks, outs, ends, probes = refs[:count], refs[count:-2], refs[-2], refs[-1]
    own = blocks[0].shape[0]
    ratio = len(offsets_row) // len(offsets_col)
    share = own * ratio
    ends[...] = jnp.full(ends.shape, at_end(len(offsets_col)).astype(F32))
    row, col = lax.axis_index("row"), lax.axis_index("col")
    pieces = [(ref, at) for ref in blocks for at in range(0, ref.shape[0], own)]
    for offset, (ref, at) in zip(offsets_row, pieces):
        column = row ^ offset
        start = (lax.div(column, ratio) ^ col) * share + lax.rem(column, ratio) * own
        probes[pl.ds(pl.multiple_of(start, own), own), :] = ref[at : at + own, :]
    for step in range(ends.shape[1] // STEP):
        rows, at = slice(base + step * STEP, base + (step + 1) * STEP), slice(step * STEP, (step + 1) * STEP)
        term = lax.dot_general(probes[...], tiles[rows, :], (((1,), (1,)), ((), ())), preferred_element_type=F32)
        for k, out in enumerate(outs):
            out[:, at] = term[k * share : (k + 1) * share].astype(out.dtype)


def partial_sketch(tiles, blocks, token, offsets_row, offsets_col, chunk, chunks):
    rows, cols = tiles.shape
    rows //= chunks
    width = blocks[0].shape[0] * len(offsets_row)
    share = width // len(offsets_col)
    vmem = pl.BlockSpec(memory_space=pltpu.VMEM)
    exact = (0, offsets_col[-1])
    outs = [jax.ShapeDtypeStruct((share, rows), F32 if offset in exact else BF16) for offset in offsets_col]
    outs.append(jax.ShapeDtypeStruct((share, rows), F32))
    return pl.pallas_call(
        functools.partial(sketch_kernel, base=chunk * rows, offsets_row=offsets_row, offsets_col=offsets_col),
        in_specs=[vmem] * (2 + len(blocks)),
        out_specs=[vmem] * len(outs),
        out_shape=outs,
        scratch_shapes=[pltpu.VMEM((width, cols), BF16)],
        compiler_params=pltpu.CompilerParams(vmem_limit_bytes=VMEM_LIMIT),
        cost_estimate=pl.CostEstimate(
            flops=2 * width * cols * rows, bytes_accessed=2 * rows * cols, transcendentals=0
        ),
        name="partial_sketch",
    )(tiles, token, *blocks)


def adjoint_kernel(tiles, *refs, base, span, parts, offsets_col, devices):
    shares, earlier, outs, lowered = refs[: len(offsets_col)], refs[len(offsets_col) : -1 - parts], refs[-1 - parts : -1], refs[-1]
    share, rows = shares[0].shape
    ratio = devices // len(offsets_col)
    own = share // ratio
    row, col = lax.axis_index("row"), lax.axis_index("col")
    for offset, ref in zip(offsets_col, shares):
        for n in range(ratio):
            apart = row ^ ((col ^ offset) * ratio + n)
            start = ((apart >> 1) + (apart & 1) * (devices // 2)) * own
            lowered[pl.ds(pl.multiple_of(start, own), own), :] = ref[n * own : (n + 1) * own, :]
    for step in range(tiles.shape[1] // STEP):
        at = slice(step * STEP, (step + 1) * STEP)
        term = jnp.dot(lowered[span, :], tiles[base : base + rows, at], preferred_element_type=F32)
        if earlier:
            term += earlier[0][span, at]
        height = outs[0].shape[0]
        for k, out in enumerate(outs):
            out[:, at] = term[k * height : (k + 1) * height]


def partial_adjoint(tiles, shares, earlier, span, parts, offsets_col, devices, base):
    cols = tiles.shape[1]
    share, rows = shares[0].shape
    width = share * len(offsets_col)
    height = (span.stop - span.start) // parts
    vmem = pl.BlockSpec(memory_space=pltpu.VMEM)
    return pl.pallas_call(
        functools.partial(
            adjoint_kernel, base=base, span=span, parts=parts, offsets_col=offsets_col, devices=devices
        ),
        in_specs=[vmem] * (1 + len(shares) + len(earlier)),
        out_specs=[vmem] * parts,
        out_shape=[jax.ShapeDtypeStruct((height, cols), F32)] * parts,
        scratch_shapes=[pltpu.VMEM((width, rows), BF16)],
        compiler_params=pltpu.CompilerParams(vmem_limit_bytes=VMEM_LIMIT),
        cost_estimate=pl.CostEstimate(
            flops=0, bytes_accessed=0, transcendentals=0
        ),
        name="partial_adjoint",
    )(tiles, *shares, *earlier)


def local(green, mask, probes):
    n_row, n_col = lax.axis_size("row"), lax.axis_size("col")
    own_width = probes.shape[1]
    chunks = CHUNKS if green.shape[0] % (CHUNKS * STEP) == 0 else 1
    offsets_col = list(range(n_col))
    offsets_core = list(range(0, n_row, 2))
    gather_core = offsets_core
    offsets_row = gather_core + [offset ^ 1 for offset in gather_core]
    tiles, token = masked(green, mask)

    own = probes.T
    held = [own] + [exchange(own, "row", offset) for offset in gather_core[1:]]
    twin = exchange(own, "row", 1)
    held, twin, token = lax.optimization_barrier((held, twin, token))
    blocks = held + [twin, exchange(jnp.concatenate(held[1:]), "row", 1)]

    totals, shares = [], []
    for chunk in range(chunks):
        *parts, ends = partial_sketch(tiles, blocks, token, offsets_row, offsets_col, chunk, chunks)
        totals.append(window_sums(parts, ends))
        shares.append(window_spread(totals[-1].astype(BF16), ends, n_col))

    earlier = []
    length = green.shape[0] // chunks
    width = own_width * n_row
    for chunk in range(chunks - 1):
        earlier = partial_adjoint(
            tiles, shares[chunk], earlier, slice(0, width), 1, offsets_col, n_row, chunk * length
        )
    theirs, ours = (
        partial_adjoint(tiles, shares[-1], earlier, span, 2, offsets_col, n_row, (chunks - 1) * length)
        for span in (slice(width // 2, width), slice(0, width // 2))
    )
    pairs = []
    for mine, others in zip(ours, theirs):
        others = exchange(others, "row", 1)
        if pairs:
            mine = after(mine, pairs[-1])
        bands = [slice(at, at + own_width) for at in range(0, mine.shape[0], own_width)]
        pairs += [mine[band] + others[band] for band in bands]
    adjoint = pairs[0]
    for offset in offsets_core[1:2] + offsets_core[:1:-1]:
        adjoint = adjoint + exchange(pairs[offset // 2].astype(BF16), "row", offset).astype(F32)
    return jnp.concatenate(totals, axis=1).T, adjoint.T


def solution(mesh):
    in_specs = (P("row", "col"), P("row", "col"), P("col", "row"))
    out_specs = (P("row", "col"), P("col", "row"))
    return jax.shard_map(local, mesh=mesh, in_specs=in_specs, out_specs=out_specs, check_vma=False)
```

```python
import functools

import jax
import jax.numpy as jnp
from jax import lax
from jax.experimental import pallas as pl
from jax.experimental.pallas import tpu as pltpu
from jax.sharding import PartitionSpec as P

F32, BF16 = jnp.float32, jnp.bfloat16
VMEM_LIMIT = 28 * 2**20
STEP = 512
CHUNKS = 2


def exchange(value, axis, offset):
    size = lax.axis_size(axis)
    return lax.ppermute(value, axis, [(i, i ^ offset) for i in range(size)])


def at_end(size):
    place = lax.axis_index("col")
    return (place == 0) | (place == size - 1)


def after(value, earlier):
    return lax.optimization_barrier((value, earlier))[0]


def window_sums(terms, ends):
    size = len(terms)
    if size == 4:
        came = lax.ppermute(terms[2], "col", [(0, 1), (3, 2), (2, 0), (1, 3)])
        came = came.astype(F32)
        onward = terms[3] + jnp.where(ends > 0, 0.0, came)
        onward = onward.astype(BF16)
        far = exchange(onward, "col", 3).astype(F32)
        near = exchange(after(terms[1], onward), "col", 1).astype(F32)
        return terms[0] + near + far + jnp.where(ends > 0, came, 0.0)
    total = terms[0]
    for offset in range(1, size):
        total = total + exchange(terms[offset].astype(BF16), "col", offset).astype(F32)
    return total


def window_spread(lowered, ends, size):
    if size == 4:
        far = exchange(lowered, "col", 3)
        near = exchange(lowered, "col", 1)
        onward = jnp.where(ends > 0, lowered, far)
        return [lowered, near, lax.ppermute(onward, "col", [(0, 2), (3, 1), (1, 0), (2, 3)]), far]
    return [lowered] + [exchange(lowered, "col", offset) for offset in range(1, size)]


def mask_kernel(mask_hbm, green_ref, tiles, token, mask_ref, mask_sem, sems, *, block):
    rows, cols = tiles.shape
    token[...] = jnp.zeros(token.shape, token.dtype)
    levels = pltpu.make_async_copy(mask_hbm, mask_ref, mask_sem)
    levels.start()
    copies = []
    for step in range(rows // STEP):
        at = pl.ds(step * STEP, STEP)
        copies.append(pltpu.make_async_copy(green_ref.at[at], tiles.at[at], sems.at[step]))
        copies[-1].start()
    levels.wait()
    for step, copy in enumerate(copies):
        copy.wait()
        for i in range(step * STEP // block, (step + 1) * STEP // block):
            for j in range(cols // block):

                @pl.when(mask_ref[i, j] == 0)
                def _():
                    tiles[i * block : (i + 1) * block, j * block : (j + 1) * block] = jnp.zeros((block, block), BF16)


def masked(green, mask):
    rows, cols = green.shape
    return pl.pallas_call(
        functools.partial(mask_kernel, block=rows // mask.shape[0]),
        in_specs=[pl.BlockSpec(memory_space=pltpu.HBM)] * 2,
        out_specs=[pl.BlockSpec(memory_space=pltpu.VMEM)] * 2,
        out_shape=[pltpu.VMEM((rows, cols), BF16), jax.ShapeDtypeStruct((8, 128), F32)],
        scratch_shapes=[
            pltpu.SMEM(mask.shape, mask.dtype),
            pltpu.SemaphoreType.DMA,
            pltpu.SemaphoreType.DMA((rows // STEP,)),
        ],
        compiler_params=pltpu.CompilerParams(vmem_limit_bytes=VMEM_LIMIT),
        cost_estimate=pl.CostEstimate(flops=0, bytes_accessed=2 * rows * cols, transcendentals=0),
        name="masked_tiles",
    )(*(pltpu.with_memory_space_constraint(array, pltpu.HBM) for array in (mask, green)))


def sketch_kernel(tiles, token, *refs, base, offsets_row, offsets_col):
    count = len(refs) - 2 - len(offsets_col)
    blocks, outs, ends, probes = refs[:count], refs[count:-2], refs[-2], refs[-1]
    own = blocks[0].shape[0]
    ratio = len(offsets_row) // len(offsets_col)
    share = own * ratio
    ends[...] = jnp.full(ends.shape, at_end(len(offsets_col)).astype(F32))
    row, col = lax.axis_index("row"), lax.axis_index("col")
    pieces = [(ref, at) for ref in blocks for at in range(0, ref.shape[0], own)]
    for offset, (ref, at) in zip(offsets_row, pieces):
        column = row ^ offset
        start = (lax.div(column, ratio) ^ col) * share + lax.rem(column, ratio) * own
        probes[pl.ds(pl.multiple_of(start, own), own), :] = ref[at : at + own, :]
    for step in range(ends.shape[1] // STEP):
        rows, at = slice(base + step * STEP, base + (step + 1) * STEP), slice(step * STEP, (step + 1) * STEP)
        term = lax.dot_general(probes[...], tiles[rows, :], (((1,), (1,)), ((), ())), preferred_element_type=F32)
        for k, out in enumerate(outs):
            out[:, at] = term[k * share : (k + 1) * share].astype(out.dtype)


def partial_sketch(tiles, blocks, token, offsets_row, offsets_col, chunk, chunks):
    rows, cols = tiles.shape
    rows //= chunks
    width = blocks[0].shape[0] * len(offsets_row)
    share = width // len(offsets_col)
    vmem = pl.BlockSpec(memory_space=pltpu.VMEM)
    exact = (0, offsets_col[-1])
    outs = [jax.ShapeDtypeStruct((share, rows), F32 if offset in exact else BF16) for offset in offsets_col]
    outs.append(jax.ShapeDtypeStruct((share, rows), F32))
    return pl.pallas_call(
        functools.partial(sketch_kernel, base=chunk * rows, offsets_row=offsets_row, offsets_col=offsets_col),
        in_specs=[vmem] * (2 + len(blocks)),
        out_specs=[vmem] * len(outs),
        out_shape=outs,
        scratch_shapes=[pltpu.VMEM((width, cols), BF16)],
        compiler_params=pltpu.CompilerParams(vmem_limit_bytes=VMEM_LIMIT),
        cost_estimate=pl.CostEstimate(
            flops=2 * width * cols * rows, bytes_accessed=2 * rows * cols, transcendentals=0
        ),
        name="partial_sketch",
    )(tiles, token, *blocks)


def adjoint_kernel(tiles, *refs, base, span, parts, offsets_col, devices):
    shares, earlier, outs, lowered = refs[: len(offsets_col)], refs[len(offsets_col) : -1 - parts], refs[-1 - parts : -1], refs[-1]
    share, rows = shares[0].shape
    ratio = devices // len(offsets_col)
    own = share // ratio
    row, col = lax.axis_index("row"), lax.axis_index("col")
    for offset, ref in zip(offsets_col, shares):
        for n in range(ratio):
            apart = row ^ ((col ^ offset) * ratio + n)
            start = ((apart >> 1) + (apart & 1) * (devices // 2)) * own
            lowered[pl.ds(pl.multiple_of(start, own), own), :] = ref[n * own : (n + 1) * own, :]
    for step in range(tiles.shape[1] // STEP):
        at = slice(step * STEP, (step + 1) * STEP)
        term = jnp.dot(lowered[span, :], tiles[base : base + rows, at], preferred_element_type=F32)
        if earlier:
            term += earlier[0][span, at]
        height = outs[0].shape[0]
        for k, out in enumerate(outs):
            out[:, at] = term[k * height : (k + 1) * height]


def partial_adjoint(tiles, shares, earlier, span, parts, offsets_col, devices, base):
    cols = tiles.shape[1]
    share, rows = shares[0].shape
    width = share * len(offsets_col)
    height = (span.stop - span.start) // parts
    vmem = pl.BlockSpec(memory_space=pltpu.VMEM)
    return pl.pallas_call(
        functools.partial(
            adjoint_kernel, base=base, span=span, parts=parts, offsets_col=offsets_col, devices=devices
        ),
        in_specs=[vmem] * (1 + len(shares) + len(earlier)),
        out_specs=[vmem] * parts,
        out_shape=[jax.ShapeDtypeStruct((height, cols), F32)] * parts,
        scratch_shapes=[pltpu.VMEM((width, rows), BF16)],
        compiler_params=pltpu.CompilerParams(vmem_limit_bytes=VMEM_LIMIT),
        cost_estimate=pl.CostEstimate(
            flops=0, bytes_accessed=0, transcendentals=0
        ),
        name="partial_adjoint",
    )(tiles, *shares, *earlier)


def local(green, mask, probes):
    n_row, n_col = lax.axis_size("row"), lax.axis_size("col")
    own_width = probes.shape[1]
    chunks = CHUNKS if green.shape[0] % (CHUNKS * STEP) == 0 else 1
    offsets_col = list(range(n_col))
    offsets_core = list(range(0, n_row, 2))
    gather_core = offsets_core
    offsets_row = gather_core + [offset ^ 1 for offset in gather_core]
    tiles, token = masked(green, mask)

    own = probes.T
    held = [own] + [exchange(own, "row", offset) for offset in gather_core[1:]]
    twin = exchange(own, "row", 1)
    early, late = held[1:-1], held[-1]
    early, twin, token = lax.optimization_barrier((early, twin, token))
    blocks = [own, *early, late, twin, exchange(jnp.concatenate(early), "row", 1), exchange(late, "row", 1)]

    totals, shares = [], []
    for chunk in range(chunks):
        *parts, ends = partial_sketch(tiles, blocks, token, offsets_row, offsets_col, chunk, chunks)
        totals.append(window_sums(parts, ends))
        shares.append(window_spread(totals[-1].astype(BF16), ends, n_col))

    earlier = []
    length = green.shape[0] // chunks
    width = own_width * n_row
    for chunk in range(chunks - 1):
        earlier = partial_adjoint(
            tiles, shares[chunk], earlier, slice(0, width), 1, offsets_col, n_row, chunk * length
        )
    theirs, ours = (
        partial_adjoint(tiles, shares[-1], earlier, span, 2, offsets_col, n_row, (chunks - 1) * length)
        for span in (slice(width // 2, width), slice(0, width // 2))
    )
    pairs = []
    for mine, others in zip(ours, theirs):
        others = exchange(others, "row", 1)
        if pairs:
            mine = after(mine, pairs[-1])
        bands = [slice(at, at + own_width) for at in range(0, mine.shape[0], own_width)]
        pairs += [mine[band] + others[band] for band in bands]
    adjoint = pairs[0]
    for offset in offsets_core[1:2] + offsets_core[:1:-1]:
        adjoint = adjoint + exchange(pairs[offset // 2].astype(BF16), "row", offset).astype(F32)
    return jnp.concatenate(totals, axis=1).T, adjoint.T


def solution(mesh):
    in_specs = (P("row", "col"), P("row", "col"), P("col", "row"))
    out_specs = (P("row", "col"), P("col", "row"))
    return jax.shard_map(local, mesh=mesh, in_specs=in_specs, out_specs=out_specs, check_vma=False)
```

```python
import functools

import jax
import jax.numpy as jnp
from jax import lax
from jax.experimental import pallas as pl
from jax.experimental.pallas import tpu as pltpu
from jax.sharding import PartitionSpec as P

F32, BF16 = jnp.float32, jnp.bfloat16
VMEM_LIMIT = 28 * 2**20
STEP = 512
CHUNKS = 2


def exchange(value, axis, offset):
    size = lax.axis_size(axis)
    return lax.ppermute(value, axis, [(i, i ^ offset) for i in range(size)])


def at_end(size):
    place = lax.axis_index("col")
    return (place == 0) | (place == size - 1)


def after(value, earlier):
    return lax.optimization_barrier((value, earlier))[0]


def window_sums(terms, ends, earlier):
    size = len(terms)
    if size == 4:
        came = lax.ppermute(terms[2], "col", [(0, 1), (3, 2), (2, 0), (1, 3)])
        came = came.astype(F32)
        onward = terms[3] + jnp.where(ends > 0, 0.0, came)
        onward = onward.astype(BF16)
        far = exchange(onward, "col", 3).astype(F32)
        near = exchange(after(terms[1], onward if earlier is None else earlier), "col", 1).astype(F32)
        return terms[0] + near + far + jnp.where(ends > 0, came, 0.0)
    total = terms[0]
    for offset in range(1, size):
        total = total + exchange(terms[offset].astype(BF16), "col", offset).astype(F32)
    return total


def window_spread(lowered, ends, size):
    if size == 4:
        far = exchange(lowered, "col", 3)
        near = exchange(lowered, "col", 1)
        onward = jnp.where(ends > 0, lowered, far)
        return [lowered, near, lax.ppermute(onward, "col", [(0, 2), (3, 1), (1, 0), (2, 3)]), far]
    return [lowered] + [exchange(lowered, "col", offset) for offset in range(1, size)]


def mask_kernel(mask_hbm, green_ref, tiles, token, mask_ref, mask_sem, sems, *, block):
    rows, cols = tiles.shape
    token[...] = jnp.zeros(token.shape, token.dtype)
    levels = pltpu.make_async_copy(mask_hbm, mask_ref, mask_sem)
    levels.start()
    copies = []
    for step in range(rows // STEP):
        at = pl.ds(step * STEP, STEP)
        copies.append(pltpu.make_async_copy(green_ref.at[at], tiles.at[at], sems.at[step]))
        copies[-1].start()
    levels.wait()
    for step, copy in enumerate(copies):
        copy.wait()
        for i in range(step * STEP // block, (step + 1) * STEP // block):
            for j in range(cols // block):

                @pl.when(mask_ref[i, j] == 0)
                def _():
                    tiles[i * block : (i + 1) * block, j * block : (j + 1) * block] = jnp.zeros((block, block), BF16)


def masked(green, mask):
    rows, cols = green.shape
    return pl.pallas_call(
        functools.partial(mask_kernel, block=rows // mask.shape[0]),
        in_specs=[pl.BlockSpec(memory_space=pltpu.HBM)] * 2,
        out_specs=[pl.BlockSpec(memory_space=pltpu.VMEM)] * 2,
        out_shape=[pltpu.VMEM((rows, cols), BF16), jax.ShapeDtypeStruct((8, 128), F32)],
        scratch_shapes=[
            pltpu.SMEM(mask.shape, mask.dtype),
            pltpu.SemaphoreType.DMA,
            pltpu.SemaphoreType.DMA((rows // STEP,)),
        ],
        compiler_params=pltpu.CompilerParams(vmem_limit_bytes=VMEM_LIMIT),
        cost_estimate=pl.CostEstimate(flops=0, bytes_accessed=2 * rows * cols, transcendentals=0),
        name="masked_tiles",
    )(*(pltpu.with_memory_space_constraint(array, pltpu.HBM) for array in (mask, green)))


def sketch_kernel(tiles, token, *refs, base, offsets_row, offsets_col):
    count = len(refs) - 2 - len(offsets_col)
    blocks, outs, ends, probes = refs[:count], refs[count:-2], refs[-2], refs[-1]
    own = blocks[0].shape[0]
    ratio = len(offsets_row) // len(offsets_col)
    share = own * ratio
    ends[...] = jnp.full(ends.shape, at_end(len(offsets_col)).astype(F32))
    row, col = lax.axis_index("row"), lax.axis_index("col")
    pieces = [(ref, at) for ref in blocks for at in range(0, ref.shape[0], own)]
    for offset, (ref, at) in zip(offsets_row, pieces):
        column = row ^ offset
        start = (lax.div(column, ratio) ^ col) * share + lax.rem(column, ratio) * own
        probes[pl.ds(pl.multiple_of(start, own), own), :] = ref[at : at + own, :]
    for step in range(ends.shape[1] // STEP):
        rows, at = slice(base + step * STEP, base + (step + 1) * STEP), slice(step * STEP, (step + 1) * STEP)
        term = lax.dot_general(probes[...], tiles[rows, :], (((1,), (1,)), ((), ())), preferred_element_type=F32)
        for k, out in enumerate(outs):
            out[:, at] = term[k * share : (k + 1) * share].astype(out.dtype)


def partial_sketch(tiles, blocks, token, offsets_row, offsets_col, chunk, chunks):
    rows, cols = tiles.shape
    rows //= chunks
    width = blocks[0].shape[0] * len(offsets_row)
    share = width // len(offsets_col)
    vmem = pl.BlockSpec(memory_space=pltpu.VMEM)
    exact = (0, offsets_col[-1])
    outs = [jax.ShapeDtypeStruct((share, rows), F32 if offset in exact else BF16) for offset in offsets_col]
    outs.append(jax.ShapeDtypeStruct((share, rows), F32))
    return pl.pallas_call(
        functools.partial(sketch_kernel, base=chunk * rows, offsets_row=offsets_row, offsets_col=offsets_col),
        in_specs=[vmem] * (2 + len(blocks)),
        out_specs=[vmem] * len(outs),
        out_shape=outs,
        scratch_shapes=[pltpu.VMEM((width, cols), BF16)],
        compiler_params=pltpu.CompilerParams(vmem_limit_bytes=VMEM_LIMIT),
        cost_estimate=pl.CostEstimate(
            flops=2 * width * cols * rows, bytes_accessed=2 * rows * cols, transcendentals=0
        ),
        name="partial_sketch",
    )(tiles, token, *blocks)


def adjoint_kernel(tiles, *refs, base, span, parts, offsets_col, devices):
    shares, earlier, outs, lowered = refs[: len(offsets_col)], refs[len(offsets_col) : -1 - parts], refs[-1 - parts : -1], refs[-1]
    share, rows = shares[0].shape
    ratio = devices // len(offsets_col)
    own = share // ratio
    row, col = lax.axis_index("row"), lax.axis_index("col")
    for offset, ref in zip(offsets_col, shares):
        for n in range(ratio):
            apart = row ^ ((col ^ offset) * ratio + n)
            start = ((apart >> 1) + (apart & 1) * (devices // 2)) * own
            lowered[pl.ds(pl.multiple_of(start, own), own), :] = ref[n * own : (n + 1) * own, :]
    for step in range(tiles.shape[1] // STEP):
        at = slice(step * STEP, (step + 1) * STEP)
        term = jnp.dot(lowered[span, :], tiles[base : base + rows, at], preferred_element_type=F32)
        if earlier:
            term += earlier[0][span, at]
        height = outs[0].shape[0]
        for k, out in enumerate(outs):
            out[:, at] = term[k * height : (k + 1) * height]


def partial_adjoint(tiles, shares, earlier, span, parts, offsets_col, devices, base):
    cols = tiles.shape[1]
    share, rows = shares[0].shape
    width = share * len(offsets_col)
    height = (span.stop - span.start) // parts
    vmem = pl.BlockSpec(memory_space=pltpu.VMEM)
    return pl.pallas_call(
        functools.partial(
            adjoint_kernel, base=base, span=span, parts=parts, offsets_col=offsets_col, devices=devices
        ),
        in_specs=[vmem] * (1 + len(shares) + len(earlier)),
        out_specs=[vmem] * parts,
        out_shape=[jax.ShapeDtypeStruct((height, cols), F32)] * parts,
        scratch_shapes=[pltpu.VMEM((width, rows), BF16)],
        compiler_params=pltpu.CompilerParams(vmem_limit_bytes=VMEM_LIMIT),
        cost_estimate=pl.CostEstimate(
            flops=0, bytes_accessed=0, transcendentals=0
        ),
        name="partial_adjoint",
    )(tiles, *shares, *earlier)


def local(green, mask, probes):
    n_row, n_col = lax.axis_size("row"), lax.axis_size("col")
    own_width = probes.shape[1]
    chunks = CHUNKS if green.shape[0] % (CHUNKS * STEP) == 0 else 1
    offsets_col = list(range(n_col))
    offsets_core = list(range(0, n_row, 2))
    gather_core = offsets_core
    offsets_row = gather_core + [offset ^ 1 for offset in gather_core]
    tiles, token = masked(green, mask)

    own = probes.T
    held = [own] + [exchange(own, "row", offset) for offset in gather_core[1:]]
    twin = exchange(own, "row", 1)
    early, late = held[1:-1], held[-1]
    early, twin, token = lax.optimization_barrier((early, twin, token))
    blocks = [own, *early, late, twin, exchange(jnp.concatenate(early), "row", 1), exchange(late, "row", 1)]

    totals, shares = [], []
    parts = [
        partial_sketch(tiles, blocks, token, offsets_row, offsets_col, chunk, chunks) for chunk in range(chunks)
    ]
    for chunk, (*terms, ends) in enumerate(parts):
        earlier = parts[chunk + 1][-1] if chunk + 1 < chunks else None
        totals.append(window_sums(terms, ends, earlier))
        shares.append(window_spread(totals[-1].astype(BF16), ends, n_col))

    earlier = []
    length = green.shape[0] // chunks
    width = own_width * n_row
    for chunk in range(chunks - 1):
        earlier = partial_adjoint(
            tiles, shares[chunk], earlier, slice(0, width), 1, offsets_col, n_row, chunk * length
        )
    theirs, ours = (
        partial_adjoint(tiles, shares[-1], earlier, span, 2, offsets_col, n_row, (chunks - 1) * length)
        for span in (slice(width // 2, width), slice(0, width // 2))
    )
    pairs = []
    for mine, others in zip(ours, theirs):
        others = exchange(others, "row", 1)
        if pairs:
            mine = after(mine, pairs[-1])
        bands = [slice(at, at + own_width) for at in range(0, mine.shape[0], own_width)]
        pairs += [mine[band] + others[band] for band in bands]
    adjoint = pairs[0]
    for offset in offsets_core[1:2] + offsets_core[:1:-1]:
        adjoint = adjoint + exchange(pairs[offset // 2].astype(BF16), "row", offset).astype(F32)
    return jnp.concatenate(totals, axis=1).T, adjoint.T


def solution(mesh):
    in_specs = (P("row", "col"), P("row", "col"), P("col", "row"))
    out_specs = (P("row", "col"), P("col", "row"))
    return jax.shard_map(local, mesh=mesh, in_specs=in_specs, out_specs=out_specs, check_vma=False)
```

```python
import functools

import jax
import jax.numpy as jnp
from jax import lax
from jax.experimental import pallas as pl
from jax.experimental.pallas import tpu as pltpu
from jax.sharding import PartitionSpec as P

F32, BF16 = jnp.float32, jnp.bfloat16
VMEM_LIMIT = 28 * 2**20
STEP = 512
WIDE = 1024
CHUNKS = 2


def exchange(value, axis, offset):
    size = lax.axis_size(axis)
    return lax.ppermute(value, axis, [(i, i ^ offset) for i in range(size)])


def at_end(size):
    place = lax.axis_index("col")
    return (place == 0) | (place == size - 1)


def after(value, earlier):
    return lax.optimization_barrier((value, earlier))[0]


def window_sums(terms, ends):
    size = len(terms)
    if size == 4:
        came = lax.ppermute(terms[2], "col", [(0, 1), (3, 2), (2, 0), (1, 3)])
        came = came.astype(F32)
        onward = terms[3] + jnp.where(ends > 0, 0.0, came)
        onward = onward.astype(BF16)
        far = exchange(onward, "col", 3).astype(F32)
        near = exchange(after(terms[1], onward), "col", 1).astype(F32)
        return terms[0] + near + far + jnp.where(ends > 0, came, 0.0)
    total = terms[0]
    for offset in range(1, size):
        total = total + exchange(terms[offset].astype(BF16), "col", offset).astype(F32)
    return total


def window_spread(lowered, ends, size):
    if size == 4:
        far = exchange(lowered, "col", 3)
        near = exchange(lowered, "col", 1)
        onward = jnp.where(ends > 0, lowered, far)
        return [lowered, near, lax.ppermute(onward, "col", [(0, 2), (3, 1), (1, 0), (2, 3)]), far]
    return [lowered] + [exchange(lowered, "col", offset) for offset in range(1, size)]


def mask_kernel(mask_hbm, green_ref, tiles, token, mask_ref, mask_sem, sems, *, block):
    rows, cols = tiles.shape
    token[...] = jnp.zeros(token.shape, token.dtype)
    levels = pltpu.make_async_copy(mask_hbm, mask_ref, mask_sem)
    levels.start()
    copies = []
    for step in range(rows // STEP):
        at = pl.ds(step * STEP, STEP)
        copies.append(pltpu.make_async_copy(green_ref.at[at], tiles.at[at], sems.at[step]))
        copies[-1].start()
    levels.wait()
    for step, copy in enumerate(copies):
        copy.wait()
        for i in range(step * STEP // block, (step + 1) * STEP // block):
            for j in range(cols // block):

                @pl.when(mask_ref[i, j] == 0)
                def _():
                    tiles[i * block : (i + 1) * block, j * block : (j + 1) * block] = jnp.zeros((block, block), BF16)


def masked(green, mask):
    rows, cols = green.shape
    return pl.pallas_call(
        functools.partial(mask_kernel, block=rows // mask.shape[0]),
        in_specs=[pl.BlockSpec(memory_space=pltpu.HBM)] * 2,
        out_specs=[pl.BlockSpec(memory_space=pltpu.VMEM)] * 2,
        out_shape=[pltpu.VMEM((rows, cols), BF16), jax.ShapeDtypeStruct((8, 128), F32)],
        scratch_shapes=[
            pltpu.SMEM(mask.shape, mask.dtype),
            pltpu.SemaphoreType.DMA,
            pltpu.SemaphoreType.DMA((rows // STEP,)),
        ],
        compiler_params=pltpu.CompilerParams(vmem_limit_bytes=VMEM_LIMIT),
        cost_estimate=pl.CostEstimate(flops=0, bytes_accessed=2 * rows * cols, transcendentals=0),
        name="masked_tiles",
    )(*(pltpu.with_memory_space_constraint(array, pltpu.HBM) for array in (mask, green)))


def sketch_kernel(tiles, token, *refs, base, offsets_row, offsets_col):
    count = len(refs) - 2 - len(offsets_col)
    blocks, outs, ends, probes = refs[:count], refs[count:-2], refs[-2], refs[-1]
    own = blocks[0].shape[0]
    ratio = len(offsets_row) // len(offsets_col)
    share = own * ratio
    ends[...] = jnp.full(ends.shape, at_end(len(offsets_col)).astype(F32))
    row, col = lax.axis_index("row"), lax.axis_index("col")
    pieces = [(ref, at) for ref in blocks for at in range(0, ref.shape[0], own)]
    for offset, (ref, at) in zip(offsets_row, pieces):
        column = row ^ offset
        start = (lax.div(column, ratio) ^ col) * share + lax.rem(column, ratio) * own
        probes[pl.ds(pl.multiple_of(start, own), own), :] = ref[at : at + own, :]
    for step in range(ends.shape[1] // WIDE):
        rows, at = slice(base + step * WIDE, base + (step + 1) * WIDE), slice(step * WIDE, (step + 1) * WIDE)
        term = lax.dot_general(probes[...], tiles[rows, :], (((1,), (1,)), ((), ())), preferred_element_type=F32)
        for k, out in enumerate(outs):
            out[:, at] = term[k * share : (k + 1) * share].astype(out.dtype)


def partial_sketch(tiles, blocks, token, offsets_row, offsets_col, chunk, chunks):
    rows, cols = tiles.shape
    rows //= chunks
    width = blocks[0].shape[0] * len(offsets_row)
    share = width // len(offsets_col)
    vmem = pl.BlockSpec(memory_space=pltpu.VMEM)
    exact = (0, offsets_col[-1])
    outs = [jax.ShapeDtypeStruct((share, rows), F32 if offset in exact else BF16) for offset in offsets_col]
    outs.append(jax.ShapeDtypeStruct((share, rows), F32))
    return pl.pallas_call(
        functools.partial(sketch_kernel, base=chunk * rows, offsets_row=offsets_row, offsets_col=offsets_col),
        in_specs=[vmem] * (2 + len(blocks)),
        out_specs=[vmem] * len(outs),
        out_shape=outs,
        scratch_shapes=[pltpu.VMEM((width, cols), BF16)],
        compiler_params=pltpu.CompilerParams(vmem_limit_bytes=VMEM_LIMIT),
        cost_estimate=pl.CostEstimate(
            flops=2 * width * cols * rows, bytes_accessed=2 * rows * cols, transcendentals=0
        ),
        name="partial_sketch",
    )(tiles, token, *blocks)


def adjoint_kernel(tiles, *refs, base, span, parts, offsets_col, devices):
    shares, earlier, outs, lowered = refs[: len(offsets_col)], refs[len(offsets_col) : -1 - parts], refs[-1 - parts : -1], refs[-1]
    share, rows = shares[0].shape
    ratio = devices // len(offsets_col)
    own = share // ratio
    row, col = lax.axis_index("row"), lax.axis_index("col")
    for offset, ref in zip(offsets_col, shares):
        for n in range(ratio):
            apart = row ^ ((col ^ offset) * ratio + n)
            start = ((apart >> 1) + (apart & 1) * (devices // 2)) * own
            lowered[pl.ds(pl.multiple_of(start, own), own), :] = ref[n * own : (n + 1) * own, :]
    for step in range(tiles.shape[1] // WIDE):
        at = slice(step * WIDE, (step + 1) * WIDE)
        term = jnp.dot(lowered[span, :], tiles[base : base + rows, at], preferred_element_type=F32)
        if earlier:
            term += earlier[0][span, at]
        height = outs[0].shape[0]
        for k, out in enumerate(outs):
            out[:, at] = term[k * height : (k + 1) * height]


def partial_adjoint(tiles, shares, earlier, span, parts, offsets_col, devices, base):
    cols = tiles.shape[1]
    share, rows = shares[0].shape
    width = share * len(offsets_col)
    height = (span.stop - span.start) // parts
    vmem = pl.BlockSpec(memory_space=pltpu.VMEM)
    return pl.pallas_call(
        functools.partial(
            adjoint_kernel, base=base, span=span, parts=parts, offsets_col=offsets_col, devices=devices
        ),
        in_specs=[vmem] * (1 + len(shares) + len(earlier)),
        out_specs=[vmem] * parts,
        out_shape=[jax.ShapeDtypeStruct((height, cols), F32)] * parts,
        scratch_shapes=[pltpu.VMEM((width, rows), BF16)],
        compiler_params=pltpu.CompilerParams(vmem_limit_bytes=VMEM_LIMIT),
        cost_estimate=pl.CostEstimate(
            flops=0, bytes_accessed=0, transcendentals=0
        ),
        name="partial_adjoint",
    )(tiles, *shares, *earlier)


def local(green, mask, probes):
    n_row, n_col = lax.axis_size("row"), lax.axis_size("col")
    own_width = probes.shape[1]
    chunks = CHUNKS if green.shape[0] % (CHUNKS * WIDE) == 0 else 1
    offsets_col = list(range(n_col))
    offsets_core = list(range(0, n_row, 2))
    gather_core = offsets_core
    offsets_row = gather_core + [offset ^ 1 for offset in gather_core]
    tiles, token = masked(green, mask)

    own = probes.T
    held = [own] + [exchange(own, "row", offset) for offset in gather_core[1:]]
    twin = exchange(own, "row", 1)
    early, late = held[1:-1], held[-1]
    early, twin, token = lax.optimization_barrier((early, twin, token))
    blocks = [own, *early, late, twin, exchange(jnp.concatenate(early), "row", 1), exchange(late, "row", 1)]

    totals, shares = [], []
    for chunk in range(chunks):
        *parts, ends = partial_sketch(tiles, blocks, token, offsets_row, offsets_col, chunk, chunks)
        totals.append(window_sums(parts, ends))
        shares.append(window_spread(totals[-1].astype(BF16), ends, n_col))

    earlier = []
    length = green.shape[0] // chunks
    width = own_width * n_row
    for chunk in range(chunks - 1):
        earlier = partial_adjoint(
            tiles, shares[chunk], earlier, slice(0, width), 1, offsets_col, n_row, chunk * length
        )
    theirs, ours = (
        partial_adjoint(tiles, shares[-1], earlier, span, 2, offsets_col, n_row, (chunks - 1) * length)
        for span in (slice(width // 2, width), slice(0, width // 2))
    )
    pairs = []
    for mine, others in zip(ours, theirs):
        others = exchange(others, "row", 1)
        if pairs:
            mine = after(mine, pairs[-1])
        bands = [slice(at, at + own_width) for at in range(0, mine.shape[0], own_width)]
        pairs += [mine[band] + others[band] for band in bands]
    adjoint = pairs[0]
    for offset in offsets_core[1:2] + offsets_core[:1:-1]:
        adjoint = adjoint + exchange(pairs[offset // 2].astype(BF16), "row", offset).astype(F32)
    return jnp.concatenate(totals, axis=1).T, adjoint.T


def solution(mesh):
    in_specs = (P("row", "col"), P("row", "col"), P("col", "row"))
    out_specs = (P("row", "col"), P("col", "row"))
    return jax.shard_map(local, mesh=mesh, in_specs=in_specs, out_specs=out_specs, check_vma=False)
```

```python
import functools

import jax
import jax.numpy as jnp
from jax import lax
from jax.experimental import pallas as pl
from jax.experimental.pallas import tpu as pltpu
from jax.sharding import PartitionSpec as P

F32, BF16 = jnp.float32, jnp.bfloat16
VMEM_LIMIT = 28 * 2**20
STEP = 512
CHUNKS = 2


def exchange(value, axis, offset):
    size = lax.axis_size(axis)
    return lax.ppermute(value, axis, [(i, i ^ offset) for i in range(size)])


def at_end(size):
    place = lax.axis_index("col")
    return (place == 0) | (place == size - 1)


def after(value, earlier):
    return lax.optimization_barrier((value, earlier))[0]


def window_sums(terms, ends):
    size = len(terms)
    if size == 4:
        came = lax.ppermute(terms[2], "col", [(0, 1), (3, 2), (2, 0), (1, 3)])
        came = came.astype(F32)
        onward = terms[3] + jnp.where(ends > 0, 0.0, came)
        onward = onward.astype(BF16)
        far = exchange(onward, "col", 3).astype(F32)
        near = exchange(after(terms[1], onward), "col", 1).astype(F32)
        return terms[0] + near + far + jnp.where(ends > 0, came, 0.0)
    total = terms[0]
    for offset in range(1, size):
        total = total + exchange(terms[offset].astype(BF16), "col", offset).astype(F32)
    return total


def window_spread(lowered, ends, size):
    if size == 4:
        far = exchange(lowered, "col", 3)
        near = exchange(lowered, "col", 1)
        onward = jnp.where(ends > 0, lowered, far)
        return [lowered, near, lax.ppermute(onward, "col", [(0, 2), (3, 1), (1, 0), (2, 3)]), far]
    return [lowered] + [exchange(lowered, "col", offset) for offset in range(1, size)]


def mask_kernel(mask_hbm, green_ref, tiles, token, mask_ref, mask_sem, sems, *, block):
    rows, cols = tiles.shape
    token[...] = jnp.zeros(token.shape, token.dtype)
    levels = pltpu.make_async_copy(mask_hbm, mask_ref, mask_sem)
    levels.start()
    copies = []
    for step in range(rows // STEP):
        at = pl.ds(step * STEP, STEP)
        copies.append(pltpu.make_async_copy(green_ref.at[at], tiles.at[at], sems.at[step]))
        copies[-1].start()
    levels.wait()
    for step, copy in enumerate(copies):
        copy.wait()
        for i in range(step * STEP // block, (step + 1) * STEP // block):
            for j in range(cols // block):

                @pl.when(mask_ref[i, j] == 0)
                def _():
                    tiles[i * block : (i + 1) * block, j * block : (j + 1) * block] = jnp.zeros((block, block), BF16)


def masked(green, mask):
    rows, cols = green.shape
    return pl.pallas_call(
        functools.partial(mask_kernel, block=rows // mask.shape[0]),
        in_specs=[pl.BlockSpec(memory_space=pltpu.HBM)] * 2,
        out_specs=[pl.BlockSpec(memory_space=pltpu.VMEM)] * 2,
        out_shape=[pltpu.VMEM((rows, cols), BF16), jax.ShapeDtypeStruct((8, 128), F32)],
        scratch_shapes=[
            pltpu.SMEM(mask.shape, mask.dtype),
            pltpu.SemaphoreType.DMA,
            pltpu.SemaphoreType.DMA((rows // STEP,)),
        ],
        compiler_params=pltpu.CompilerParams(vmem_limit_bytes=VMEM_LIMIT),
        cost_estimate=pl.CostEstimate(flops=0, bytes_accessed=2 * rows * cols, transcendentals=0),
        name="masked_tiles",
    )(*(pltpu.with_memory_space_constraint(array, pltpu.HBM) for array in (mask, green)))


def sketch_kernel(tiles, token, *refs, base, offsets_row, offsets_col):
    count = len(refs) - 2 - len(offsets_col)
    blocks, outs, ends, probes = refs[:count], refs[count:-2], refs[-2], refs[-1]
    own = blocks[0].shape[0]
    ratio = len(offsets_row) // len(offsets_col)
    share = own * ratio
    ends[...] = jnp.full(ends.shape, at_end(len(offsets_col)).astype(F32))
    row, col = lax.axis_index("row"), lax.axis_index("col")
    pieces = [(ref, at) for ref in blocks for at in range(0, ref.shape[0], own)]
    for offset, (ref, at) in zip(offsets_row, pieces):
        column = row ^ offset
        start = (lax.div(column, ratio) ^ col) * share + lax.rem(column, ratio) * own
        probes[pl.ds(pl.multiple_of(start, own), own), :] = ref[at : at + own, :]
    for step in range(ends.shape[1] // STEP):
        rows, at = slice(base + step * STEP, base + (step + 1) * STEP), slice(step * STEP, (step + 1) * STEP)
        term = lax.dot_general(probes[...], tiles[rows, :], (((1,), (1,)), ((), ())), preferred_element_type=F32)
        for k, out in enumerate(outs):
            out[:, at] = term[k * share : (k + 1) * share].astype(out.dtype)


def partial_sketch(tiles, blocks, token, offsets_row, offsets_col, chunk, chunks):
    rows, cols = tiles.shape
    rows //= chunks
    width = blocks[0].shape[0] * len(offsets_row)
    share = width // len(offsets_col)
    vmem = pl.BlockSpec(memory_space=pltpu.VMEM)
    exact = (0, offsets_col[-1])
    outs = [jax.ShapeDtypeStruct((share, rows), F32 if offset in exact else BF16) for offset in offsets_col]
    outs.append(jax.ShapeDtypeStruct((share, rows), F32))
    return pl.pallas_call(
        functools.partial(sketch_kernel, base=chunk * rows, offsets_row=offsets_row, offsets_col=offsets_col),
        in_specs=[vmem] * (2 + len(blocks)),
        out_specs=[vmem] * len(outs),
        out_shape=outs,
        scratch_shapes=[pltpu.VMEM((width, cols), BF16)],
        compiler_params=pltpu.CompilerParams(vmem_limit_bytes=VMEM_LIMIT),
        cost_estimate=pl.CostEstimate(
            flops=2 * width * cols * rows, bytes_accessed=2 * rows * cols, transcendentals=0
        ),
        name="partial_sketch",
    )(tiles, token, *blocks)


def adjoint_kernel(tiles, *refs, base, span, parts, offsets_col, devices):
    shares, earlier, outs, lowered = refs[: len(offsets_col)], refs[len(offsets_col) : -1 - parts], refs[-1 - parts : -1], refs[-1]
    share, rows = shares[0].shape
    ratio = devices // len(offsets_col)
    own = share // ratio
    row, col = lax.axis_index("row"), lax.axis_index("col")
    for offset, ref in zip(offsets_col, shares):
        for n in range(ratio):
            apart = row ^ ((col ^ offset) * ratio + n)
            start = ((apart >> 1) + (apart & 1) * (devices // 2)) * own
            lowered[pl.ds(pl.multiple_of(start, own), own), :] = ref[n * own : (n + 1) * own, :]
    for step in range(tiles.shape[1] // STEP):
        at = slice(step * STEP, (step + 1) * STEP)
        term = jnp.dot(lowered[span, :], tiles[base : base + rows, at], preferred_element_type=F32)
        if earlier:
            term += earlier[0][span, at]
        height = outs[0].shape[0]
        for k, out in enumerate(outs):
            out[:, at] = term[k * height : (k + 1) * height]


def partial_adjoint(tiles, shares, earlier, span, parts, offsets_col, devices, base):
    cols = tiles.shape[1]
    share, rows = shares[0].shape
    width = share * len(offsets_col)
    height = (span.stop - span.start) // parts
    vmem = pl.BlockSpec(memory_space=pltpu.VMEM)
    return pl.pallas_call(
        functools.partial(
            adjoint_kernel, base=base, span=span, parts=parts, offsets_col=offsets_col, devices=devices
        ),
        in_specs=[vmem] * (1 + len(shares) + len(earlier)),
        out_specs=[vmem] * parts,
        out_shape=[jax.ShapeDtypeStruct((height, cols), F32)] * parts,
        scratch_shapes=[pltpu.VMEM((width, rows), BF16)],
        compiler_params=pltpu.CompilerParams(vmem_limit_bytes=VMEM_LIMIT),
        cost_estimate=pl.CostEstimate(
            flops=0, bytes_accessed=0, transcendentals=0
        ),
        name="partial_adjoint",
    )(tiles, *shares, *earlier)


def local(green, mask, probes):
    n_row, n_col = lax.axis_size("row"), lax.axis_size("col")
    own_width = probes.shape[1]
    chunks = CHUNKS if green.shape[0] % (CHUNKS * STEP) == 0 else 1
    offsets_col = list(range(n_col))
    offsets_core = list(range(0, n_row, 2))
    gather_core = [0, offsets_core[-1], *offsets_core[1:-1]]
    offsets_row = gather_core + [offset ^ 1 for offset in gather_core]
    tiles, token = masked(green, mask)

    own = probes.T
    held = [own] + [exchange(own, "row", offset) for offset in gather_core[1:]]
    twin = exchange(own, "row", 1)
    early, late = held[1:-1], held[-1]
    early, twin, token = lax.optimization_barrier((early, twin, token))
    blocks = [own, *early, late, twin, exchange(jnp.concatenate(early), "row", 1), exchange(late, "row", 1)]

    totals, shares = [], []
    for chunk in range(chunks):
        *parts, ends = partial_sketch(tiles, blocks, token, offsets_row, offsets_col, chunk, chunks)
        totals.append(window_sums(parts, ends))
        shares.append(window_spread(totals[-1].astype(BF16), ends, n_col))

    earlier = []
    length = green.shape[0] // chunks
    width = own_width * n_row
    for chunk in range(chunks - 1):
        earlier = partial_adjoint(
            tiles, shares[chunk], earlier, slice(0, width), 1, offsets_col, n_row, chunk * length
        )
    theirs, ours = (
        partial_adjoint(tiles, shares[-1], earlier, span, 2, offsets_col, n_row, (chunks - 1) * length)
        for span in (slice(width // 2, width), slice(0, width // 2))
    )
    pairs = []
    for mine, others in zip(ours, theirs):
        others = exchange(others, "row", 1)
        if pairs:
            mine = after(mine, pairs[-1])
        bands = [slice(at, at + own_width) for at in range(0, mine.shape[0], own_width)]
        pairs += [mine[band] + others[band] for band in bands]
    adjoint = pairs[0]
    for offset in offsets_core[1:2] + offsets_core[:1:-1]:
        adjoint = adjoint + exchange(pairs[offset // 2].astype(BF16), "row", offset).astype(F32)
    return jnp.concatenate(totals, axis=1).T, adjoint.T


def solution(mesh):
    in_specs = (P("row", "col"), P("row", "col"), P("col", "row"))
    out_specs = (P("row", "col"), P("col", "row"))
    return jax.shard_map(local, mesh=mesh, in_specs=in_specs, out_specs=out_specs, check_vma=False)
```

```python
import functools

import jax
import jax.numpy as jnp
from jax import lax
from jax.experimental import pallas as pl
from jax.experimental.pallas import tpu as pltpu
from jax.sharding import PartitionSpec as P

F32, BF16 = jnp.float32, jnp.bfloat16
VMEM_LIMIT = 28 * 2**20
STEP = 512
CHUNKS = 2


def exchange(value, axis, offset):
    size = lax.axis_size(axis)
    return lax.ppermute(value, axis, [(i, i ^ offset) for i in range(size)])


def at_end(size):
    place = lax.axis_index("col")
    return (place == 0) | (place == size - 1)


def after(value, earlier):
    return lax.optimization_barrier((value, earlier))[0]


def window_sums(terms, ends, first):
    size = len(terms)
    if size == 4:
        came = lax.ppermute(terms[2], "col", [(0, 1), (3, 2), (2, 0), (1, 3)])
        came = came.astype(F32)
        onward = terms[3] + jnp.where(ends > 0, 0.0, came)
        onward = onward.astype(BF16)
        far = exchange(onward, "col", 3)
        near = exchange(after(terms[1], onward if first is None else first), "col", 1).astype(F32)
        return terms[0] + near + far.astype(F32) + jnp.where(ends > 0, came, 0.0), far
    total = terms[0]
    for offset in range(1, size):
        total = total + exchange(terms[offset].astype(BF16), "col", offset).astype(F32)
    return total, None


def window_spread(lowered, ends, size):
    if size == 4:
        far = exchange(lowered, "col", 3)
        near = exchange(lowered, "col", 1)
        onward = jnp.where(ends > 0, lowered, far)
        return [lowered, near, lax.ppermute(onward, "col", [(0, 2), (3, 1), (1, 0), (2, 3)]), far]
    return [lowered] + [exchange(lowered, "col", offset) for offset in range(1, size)]


def mask_kernel(mask_hbm, green_ref, tiles, token, mask_ref, mask_sem, sems, *, block):
    rows, cols = tiles.shape
    token[...] = jnp.zeros(token.shape, token.dtype)
    levels = pltpu.make_async_copy(mask_hbm, mask_ref, mask_sem)
    levels.start()
    copies = []
    for step in range(rows // STEP):
        at = pl.ds(step * STEP, STEP)
        copies.append(pltpu.make_async_copy(green_ref.at[at], tiles.at[at], sems.at[step]))
        copies[-1].start()
    levels.wait()
    for step, copy in enumerate(copies):
        copy.wait()
        for i in range(step * STEP // block, (step + 1) * STEP // block):
            for j in range(cols // block):

                @pl.when(mask_ref[i, j] == 0)
                def _():
                    tiles[i * block : (i + 1) * block, j * block : (j + 1) * block] = jnp.zeros((block, block), BF16)


def masked(green, mask):
    rows, cols = green.shape
    return pl.pallas_call(
        functools.partial(mask_kernel, block=rows // mask.shape[0]),
        in_specs=[pl.BlockSpec(memory_space=pltpu.HBM)] * 2,
        out_specs=[pl.BlockSpec(memory_space=pltpu.VMEM)] * 2,
        out_shape=[pltpu.VMEM((rows, cols), BF16), jax.ShapeDtypeStruct((8, 128), F32)],
        scratch_shapes=[
            pltpu.SMEM(mask.shape, mask.dtype),
            pltpu.SemaphoreType.DMA,
            pltpu.SemaphoreType.DMA((rows // STEP,)),
        ],
        compiler_params=pltpu.CompilerParams(vmem_limit_bytes=VMEM_LIMIT),
        cost_estimate=pl.CostEstimate(flops=0, bytes_accessed=2 * rows * cols, transcendentals=0),
        name="masked_tiles",
    )(*(pltpu.with_memory_space_constraint(array, pltpu.HBM) for array in (mask, green)))


def sketch_kernel(tiles, token, *refs, base, offsets_row, offsets_col):
    count = len(refs) - 2 - len(offsets_col)
    blocks, outs, ends, probes = refs[:count], refs[count:-2], refs[-2], refs[-1]
    own = blocks[0].shape[0]
    ratio = len(offsets_row) // len(offsets_col)
    share = own * ratio
    ends[...] = jnp.full(ends.shape, at_end(len(offsets_col)).astype(F32))
    row, col = lax.axis_index("row"), lax.axis_index("col")
    pieces = [(ref, at) for ref in blocks for at in range(0, ref.shape[0], own)]
    for offset, (ref, at) in zip(offsets_row, pieces):
        column = row ^ offset
        start = (lax.div(column, ratio) ^ col) * share + lax.rem(column, ratio) * own
        probes[pl.ds(pl.multiple_of(start, own), own), :] = ref[at : at + own, :]
    for step in range(ends.shape[1] // STEP):
        rows, at = slice(base + step * STEP, base + (step + 1) * STEP), slice(step * STEP, (step + 1) * STEP)
        term = lax.dot_general(probes[...], tiles[rows, :], (((1,), (1,)), ((), ())), preferred_element_type=F32)
        for k, out in enumerate(outs):
            out[:, at] = term[k * share : (k + 1) * share].astype(out.dtype)


def partial_sketch(tiles, blocks, token, offsets_row, offsets_col, chunk, chunks):
    rows, cols = tiles.shape
    rows //= chunks
    width = blocks[0].shape[0] * len(offsets_row)
    share = width // len(offsets_col)
    vmem = pl.BlockSpec(memory_space=pltpu.VMEM)
    exact = (0, offsets_col[-1])
    outs = [jax.ShapeDtypeStruct((share, rows), F32 if offset in exact else BF16) for offset in offsets_col]
    outs.append(jax.ShapeDtypeStruct((share, rows), F32))
    return pl.pallas_call(
        functools.partial(sketch_kernel, base=chunk * rows, offsets_row=offsets_row, offsets_col=offsets_col),
        in_specs=[vmem] * (2 + len(blocks)),
        out_specs=[vmem] * len(outs),
        out_shape=outs,
        scratch_shapes=[pltpu.VMEM((width, cols), BF16)],
        compiler_params=pltpu.CompilerParams(vmem_limit_bytes=VMEM_LIMIT),
        cost_estimate=pl.CostEstimate(
            flops=2 * width * cols * rows, bytes_accessed=2 * rows * cols, transcendentals=0
        ),
        name="partial_sketch",
    )(tiles, token, *blocks)


def adjoint_kernel(tiles, *refs, base, span, parts, offsets_col, devices):
    shares, earlier, outs, lowered = refs[: len(offsets_col)], refs[len(offsets_col) : -1 - parts], refs[-1 - parts : -1], refs[-1]
    share, rows = shares[0].shape
    ratio = devices // len(offsets_col)
    own = share // ratio
    row, col = lax.axis_index("row"), lax.axis_index("col")
    for offset, ref in zip(offsets_col, shares):
        for n in range(ratio):
            apart = row ^ ((col ^ offset) * ratio + n)
            start = ((apart >> 1) + (apart & 1) * (devices // 2)) * own
            lowered[pl.ds(pl.multiple_of(start, own), own), :] = ref[n * own : (n + 1) * own, :]
    for step in range(tiles.shape[1] // STEP):
        at = slice(step * STEP, (step + 1) * STEP)
        term = jnp.dot(lowered[span, :], tiles[base : base + rows, at], preferred_element_type=F32)
        if earlier:
            term += earlier[0][span, at]
        height = outs[0].shape[0]
        for k, out in enumerate(outs):
            out[:, at] = term[k * height : (k + 1) * height]


def partial_adjoint(tiles, shares, earlier, span, parts, offsets_col, devices, base):
    cols = tiles.shape[1]
    share, rows = shares[0].shape
    width = share * len(offsets_col)
    height = (span.stop - span.start) // parts
    vmem = pl.BlockSpec(memory_space=pltpu.VMEM)
    return pl.pallas_call(
        functools.partial(
            adjoint_kernel, base=base, span=span, parts=parts, offsets_col=offsets_col, devices=devices
        ),
        in_specs=[vmem] * (1 + len(shares) + len(earlier)),
        out_specs=[vmem] * parts,
        out_shape=[jax.ShapeDtypeStruct((height, cols), F32)] * parts,
        scratch_shapes=[pltpu.VMEM((width, rows), BF16)],
        compiler_params=pltpu.CompilerParams(vmem_limit_bytes=VMEM_LIMIT),
        cost_estimate=pl.CostEstimate(
            flops=0, bytes_accessed=0, transcendentals=0
        ),
        name="partial_adjoint",
    )(tiles, *shares, *earlier)


def local(green, mask, probes):
    n_row, n_col = lax.axis_size("row"), lax.axis_size("col")
    own_width = probes.shape[1]
    chunks = CHUNKS if green.shape[0] % (CHUNKS * STEP) == 0 else 1
    offsets_col = list(range(n_col))
    offsets_core = list(range(0, n_row, 2))
    gather_core = offsets_core
    offsets_row = gather_core + [offset ^ 1 for offset in gather_core]
    tiles, token = masked(green, mask)

    own = probes.T
    held = [own] + [exchange(own, "row", offset) for offset in gather_core[1:]]
    twin = exchange(own, "row", 1)
    early, late = held[1:-1], held[-1]
    early, twin, token = lax.optimization_barrier((early, twin, token))
    blocks = [own, *early, late, twin, exchange(jnp.concatenate(early), "row", 1), exchange(late, "row", 1)]

    totals, shares, first = [], [], None
    for chunk in range(chunks):
        *parts, ends = partial_sketch(tiles, blocks, token, offsets_row, offsets_col, chunk, chunks)
        total, first = window_sums(parts, ends, first)
        totals.append(total)
        shares.append(window_spread(totals[-1].astype(BF16), ends, n_col))

    earlier = []
    length = green.shape[0] // chunks
    width = own_width * n_row
    for chunk in range(chunks - 1):
        earlier = partial_adjoint(
            tiles, shares[chunk], earlier, slice(0, width), 1, offsets_col, n_row, chunk * length
        )
    theirs, ours = (
        partial_adjoint(tiles, shares[-1], earlier, span, 2, offsets_col, n_row, (chunks - 1) * length)
        for span in (slice(width // 2, width), slice(0, width // 2))
    )
    pairs = []
    for mine, others in zip(ours, theirs):
        others = exchange(others, "row", 1)
        if pairs:
            mine = after(mine, pairs[-1])
        bands = [slice(at, at + own_width) for at in range(0, mine.shape[0], own_width)]
        pairs += [mine[band] + others[band] for band in bands]
    adjoint = pairs[0]
    for offset in offsets_core[1:2] + offsets_core[:1:-1]:
        adjoint = adjoint + exchange(pairs[offset // 2].astype(BF16), "row", offset).astype(F32)
    return jnp.concatenate(totals, axis=1).T, adjoint.T


def solution(mesh):
    in_specs = (P("row", "col"), P("row", "col"), P("col", "row"))
    out_specs = (P("row", "col"), P("col", "row"))
    return jax.shard_map(local, mesh=mesh, in_specs=in_specs, out_specs=out_specs, check_vma=False)
```

```python
import functools

import jax
import jax.numpy as jnp
from jax import lax
from jax.experimental import pallas as pl
from jax.experimental.pallas import tpu as pltpu
from jax.sharding import PartitionSpec as P

F32, BF16 = jnp.float32, jnp.bfloat16
VMEM_LIMIT = 28 * 2**20
STEP = 512
CHUNKS = 2


def exchange(value, axis, offset):
    size = lax.axis_size(axis)
    return lax.ppermute(value, axis, [(i, i ^ offset) for i in range(size)])


def at_end(size):
    place = lax.axis_index("col")
    return (place == 0) | (place == size - 1)


def after(value, earlier):
    return lax.optimization_barrier((value, earlier))[0]


def window_sums(terms, ends):
    size = len(terms)
    if size == 4:
        came = lax.ppermute(terms[2], "col", [(0, 1), (3, 2), (2, 0), (1, 3)])
        came = came.astype(F32)
        onward = terms[3] + jnp.where(ends > 0, 0.0, came)
        onward = onward.astype(BF16)
        far = exchange(onward, "col", 3).astype(F32)
        near = exchange(after(terms[1], onward), "col", 1).astype(F32)
        return terms[0] + near + far + jnp.where(ends > 0, came, 0.0)
    total = terms[0]
    for offset in range(1, size):
        total = total + exchange(terms[offset].astype(BF16), "col", offset).astype(F32)
    return total


def window_spread(lowered, ends, size):
    if size == 4:
        far = exchange(lowered, "col", 3)
        near = exchange(lowered, "col", 1)
        onward = jnp.where(ends > 0, lowered, far)
        return [lowered, near, lax.ppermute(onward, "col", [(0, 2), (3, 1), (1, 0), (2, 3)]), far]
    return [lowered] + [exchange(lowered, "col", offset) for offset in range(1, size)]


def mask_kernel(mask_hbm, green_ref, tiles, token, mask_ref, mask_sem, sems, *, block):
    rows, cols = tiles.shape
    token[...] = jnp.zeros(token.shape, token.dtype)
    levels = pltpu.make_async_copy(mask_hbm, mask_ref, mask_sem)
    levels.start()
    copies = []
    for step in range(rows // STEP):
        at = pl.ds(step * STEP, STEP)
        copies.append(pltpu.make_async_copy(green_ref.at[at], tiles.at[at], sems.at[step]))
        copies[-1].start()
    levels.wait()
    for step, copy in enumerate(copies):
        copy.wait()
        for i in range(step * STEP // block, (step + 1) * STEP // block):
            for j in range(cols // block):

                @pl.when(mask_ref[i, j] == 0)
                def _():
                    tiles[i * block : (i + 1) * block, j * block : (j + 1) * block] = jnp.zeros((block, block), BF16)


def masked(green, mask):
    rows, cols = green.shape
    return pl.pallas_call(
        functools.partial(mask_kernel, block=rows // mask.shape[0]),
        in_specs=[pl.BlockSpec(memory_space=pltpu.HBM)] * 2,
        out_specs=[pl.BlockSpec(memory_space=pltpu.VMEM)] * 2,
        out_shape=[pltpu.VMEM((rows, cols), BF16), jax.ShapeDtypeStruct((8, 128), F32)],
        scratch_shapes=[
            pltpu.SMEM(mask.shape, mask.dtype),
            pltpu.SemaphoreType.DMA,
            pltpu.SemaphoreType.DMA((rows // STEP,)),
        ],
        compiler_params=pltpu.CompilerParams(vmem_limit_bytes=VMEM_LIMIT),
        cost_estimate=pl.CostEstimate(flops=0, bytes_accessed=2 * rows * cols, transcendentals=0),
        name="masked_tiles",
    )(*(pltpu.with_memory_space_constraint(array, pltpu.HBM) for array in (mask, green)))


def sketch_kernel(tiles, token, *refs, base, offsets_row, offsets_col):
    count = len(refs) - 2 - len(offsets_col)
    blocks, outs, ends, probes = refs[:count], refs[count:-2], refs[-2], refs[-1]
    own = blocks[0].shape[0]
    ratio = len(offsets_row) // len(offsets_col)
    share = own * ratio
    ends[...] = jnp.full(ends.shape, at_end(len(offsets_col)).astype(F32))
    row, col = lax.axis_index("row"), lax.axis_index("col")
    pieces = [(ref, at) for ref in blocks for at in range(0, ref.shape[0], own)]
    for offset, (ref, at) in zip(offsets_row, pieces):
        column = row ^ offset
        start = (lax.div(column, ratio) ^ col) * share + lax.rem(column, ratio) * own
        probes[pl.ds(pl.multiple_of(start, own), own), :] = ref[at : at + own, :]
    for step in range(ends.shape[1] // STEP):
        rows, at = slice(base + step * STEP, base + (step + 1) * STEP), slice(step * STEP, (step + 1) * STEP)
        term = lax.dot_general(probes[...], tiles[rows, :], (((1,), (1,)), ((), ())), preferred_element_type=F32)
        for k, out in enumerate(outs):
            out[:, at] = term[k * share : (k + 1) * share].astype(out.dtype)


def partial_sketch(tiles, blocks, token, offsets_row, offsets_col, chunk, chunks):
    rows, cols = tiles.shape
    rows //= chunks
    width = blocks[0].shape[0] * len(offsets_row)
    share = width // len(offsets_col)
    vmem = pl.BlockSpec(memory_space=pltpu.VMEM)
    exact = (0, offsets_col[-1])
    outs = [jax.ShapeDtypeStruct((share, rows), F32 if offset in exact else BF16) for offset in offsets_col]
    outs.append(jax.ShapeDtypeStruct((share, rows), F32))
    return pl.pallas_call(
        functools.partial(sketch_kernel, base=chunk * rows, offsets_row=offsets_row, offsets_col=offsets_col),
        in_specs=[vmem] * (2 + len(blocks)),
        out_specs=[vmem] * len(outs),
        out_shape=outs,
        scratch_shapes=[pltpu.VMEM((width, cols), BF16)],
        compiler_params=pltpu.CompilerParams(vmem_limit_bytes=VMEM_LIMIT),
        cost_estimate=pl.CostEstimate(
            flops=2 * width * cols * rows, bytes_accessed=2 * rows * cols, transcendentals=0
        ),
        name="partial_sketch",
    )(tiles, token, *blocks)


def adjoint_kernel(tiles, *refs, base, span, parts, offsets_col, devices):
    shares, earlier, outs, lowered = refs[: len(offsets_col)], refs[len(offsets_col) : -1 - parts], refs[-1 - parts : -1], refs[-1]
    share, rows = shares[0].shape
    ratio = devices // len(offsets_col)
    own = share // ratio
    row, col = lax.axis_index("row"), lax.axis_index("col")
    for offset, ref in zip(offsets_col, shares):
        for n in range(ratio):
            apart = row ^ ((col ^ offset) * ratio + n)
            start = ((apart >> 1) + (apart & 1) * (devices // 2)) * own
            lowered[pl.ds(pl.multiple_of(start, own), own), :] = ref[n * own : (n + 1) * own, :]
    for step in range(tiles.shape[1] // STEP):
        at = slice(step * STEP, (step + 1) * STEP)
        term = jnp.dot(lowered[span, :], tiles[base : base + rows, at], preferred_element_type=F32)
        if earlier:
            term += earlier[0][span, at]
        height = outs[0].shape[0]
        for k, out in enumerate(outs):
            out[:, at] = term[k * height : (k + 1) * height]


def partial_adjoint(tiles, shares, earlier, span, parts, offsets_col, devices, base):
    cols = tiles.shape[1]
    share, rows = shares[0].shape
    width = share * len(offsets_col)
    height = (span.stop - span.start) // parts
    vmem = pl.BlockSpec(memory_space=pltpu.VMEM)
    return pl.pallas_call(
        functools.partial(
            adjoint_kernel, base=base, span=span, parts=parts, offsets_col=offsets_col, devices=devices
        ),
        in_specs=[vmem] * (1 + len(shares) + len(earlier)),
        out_specs=[vmem] * parts,
        out_shape=[jax.ShapeDtypeStruct((height, cols), F32)] * parts,
        scratch_shapes=[pltpu.VMEM((width, rows), BF16)],
        compiler_params=pltpu.CompilerParams(vmem_limit_bytes=VMEM_LIMIT),
        cost_estimate=pl.CostEstimate(
            flops=0, bytes_accessed=0, transcendentals=0
        ),
        name="partial_adjoint",
    )(tiles, *shares, *earlier)


def local(green, mask, probes):
    n_row, n_col = lax.axis_size("row"), lax.axis_size("col")
    own_width = probes.shape[1]
    chunks = CHUNKS if green.shape[0] % (CHUNKS * STEP) == 0 else 1
    offsets_col = list(range(n_col))
    offsets_core = list(range(0, n_row, 2))
    gather_core = offsets_core
    offsets_row = gather_core + [offset ^ 1 for offset in gather_core]
    tiles, token = masked(green, mask)

    own = probes.T
    held = [own] + [exchange(own, "row", offset) for offset in gather_core[1:]]
    early, late = held[:-1], held[-1]
    early, token = lax.optimization_barrier((early, token))
    blocks = [*early, late, exchange(jnp.concatenate(early), "row", 1), exchange(late, "row", 1)]

    totals, shares = [], []
    for chunk in range(chunks):
        *parts, ends = partial_sketch(tiles, blocks, token, offsets_row, offsets_col, chunk, chunks)
        totals.append(window_sums(parts, ends))
        shares.append(window_spread(totals[-1].astype(BF16), ends, n_col))

    earlier = []
    length = green.shape[0] // chunks
    width = own_width * n_row
    for chunk in range(chunks - 1):
        earlier = partial_adjoint(
            tiles, shares[chunk], earlier, slice(0, width), 1, offsets_col, n_row, chunk * length
        )
    theirs, ours = (
        partial_adjoint(tiles, shares[-1], earlier, span, 2, offsets_col, n_row, (chunks - 1) * length)
        for span in (slice(width // 2, width), slice(0, width // 2))
    )
    pairs = []
    for mine, others in zip(ours, theirs):
        others = exchange(others, "row", 1)
        if pairs:
            mine = after(mine, pairs[-1])
        bands = [slice(at, at + own_width) for at in range(0, mine.shape[0], own_width)]
        pairs += [mine[band] + others[band] for band in bands]
    adjoint = pairs[0]
    for offset in offsets_core[1:2] + offsets_core[:1:-1]:
        adjoint = adjoint + exchange(pairs[offset // 2].astype(BF16), "row", offset).astype(F32)
    return jnp.concatenate(totals, axis=1).T, adjoint.T


def solution(mesh):
    in_specs = (P("row", "col"), P("row", "col"), P("col", "row"))
    out_specs = (P("row", "col"), P("col", "row"))
    return jax.shard_map(local, mesh=mesh, in_specs=in_specs, out_specs=out_specs, check_vma=False)
```
